256 devices in a mesh: plane: 4 (over x_lo, core), col: 64 (over x_hi, y, z).
Axes of the slice: x: 4 (x_hi: 2, x_lo: 2; x = x_hi * 2 + x_lo), y: 4, z: 8, core: 2. Of those that a mesh axis runs over, the one named last changes fastest.
Arguments:
- exposures: float32 [8, 1024, 16384], P('plane', None, 'col'), may hold values from -6 to 6
Outputs:
- joined: float32 [1024, 16384], P('plane', 'col')
The draws below stay inside these ranges and needn't reach their ends.
All inputs are finite; a program needn't handle non-finite values.
Results may differ from the reference program's by a relative error of at most 0.00002.
Values sent between devices are 32-bit elements; how exact they have to be, the bound alone decides.
A program may use at most 128 MiB of HBM per device.

```python
import jax
import jax.numpy as jnp
from jax import lax

P_SIZE = 8
H = 1024
W = 16384


def levels(stream_key, shape, cuts, smallest, high):
    level = 1.0
    for axis_at, shards_of in cuts:
        heights = jax.random.uniform(jax.random.fold_in(jax.random.fold_in(stream_key, 6), axis_at), (shards_of,), jnp.float32, smallest / len(cuts), high / len(cuts))
        level = level * jnp.repeat(jnp.exp(heights), shape[axis_at] // shards_of).reshape((-1,) + (1,) * (len(shape) - 1 - axis_at))
    return level


def noise(rng, extent, deviation, reach, shards=(), held_as=jnp.bfloat16):
    entries = jax.random.normal(rng, extent, jnp.float32) * deviation
    if len(shards) > 0:
        entries = levels(rng, extent, shards, -0.22, 0.18) * entries
    return jnp.clip(entries, min=-reach, max=reach).astype(held_as)


def setup_inputs(seed: int = 0) -> dict:
    streams_of = jax.random.split(jax.random.key(seed), 2)
    return {
        "exposures": noise(streams_of[0], (P_SIZE, H, W), 1.0, 6.0, ((0, 4), (2, 64)), jnp.float32),
    }


FILTER_TAPS = (0.0625, 0.25, 0.375, 0.25, 0.0625)


def pad_axis(values, along, margin):
    widths = [(0, 0)] * values.ndim
    widths[along] = (margin, margin)
    return jnp.pad(values, widths)


def reduce_axis(padded, along, amount):
    summed = FILTER_TAPS[0] * lax.slice_in_dim(padded, 0, 2 * amount - 1, 2, along)
    for offset in range(1, 5):
        summed = summed + FILTER_TAPS[offset] * lax.slice_in_dim(padded, offset, offset + 2 * amount - 1, 2, along)
    return summed


def expand_axis(padded, along, amount):
    filler = jnp.zeros_like(padded)
    new_shape = list(padded.shape)
    new_shape[along] = 2 * new_shape[along]
    stuffed = jnp.stack([padded, filler], axis=along + 1).reshape(new_shape)
    summed = 2.0 * FILTER_TAPS[0] * lax.slice_in_dim(stuffed, 0, 2 * amount, 1, along)
    for offset in range(1, 5):
        summed = summed + 2.0 * FILTER_TAPS[offset] * lax.slice_in_dim(stuffed, offset, offset + 2 * amount, 1, along)
    return summed


def energy_logit(detail):
    squared = detail * detail
    return 4.0 * squared / (1.0 + squared)


def one_plane(carry, image):
    half_rows = reduce_axis(pad_axis(image, 0, 2), 0, H // 2)
    coarse_one = reduce_axis(pad_axis(half_rows, 1, 2), 1, W // 2)
    widened = expand_axis(pad_axis(coarse_one, 1, 1), 1, W // 2)
    detail_zero = image - expand_axis(pad_axis(widened, 0, 1), 0, H // 2)
    quarter_rows = reduce_axis(pad_axis(coarse_one, 0, 2), 0, H // 4)
    coarse_two = reduce_axis(pad_axis(quarter_rows, 1, 2), 1, W // 4)
    widened_two = expand_axis(pad_axis(coarse_two, 1, 1), 1, W // 4)
    base_two = expand_axis(pad_axis(widened_two, 0, 1), 0, H // 4)
    detail_one = coarse_one - base_two
    weight_zero = jnp.exp(energy_logit(detail_zero))
    weight_one = jnp.exp(energy_logit(detail_one))
    return (carry[0] + weight_zero * detail_zero, carry[1] + weight_zero,
            carry[2] + weight_one * detail_one, carry[3] + weight_one, carry[4] + base_two), None


def reference(exposures):
    big_zero = jnp.zeros((H, W), jnp.float32)
    small_zero = jnp.zeros((H // 2, W // 2), jnp.float32)
    start = (big_zero, big_zero, small_zero, small_zero, small_zero)
    sums, _ = lax.scan(one_plane, start, exposures)
    joined_zero = sums[0] / sums[1]
    joined_one = sums[2] / sums[3] + sums[4] / P_SIZE
    rows_up = expand_axis(pad_axis(joined_one, 0, 1), 0, H // 2)
    return joined_zero + expand_axis(pad_axis(rows_up, 1, 1), 1, W // 2)
```

```python
import functools

import jax
import jax.numpy as jnp
import ml_dtypes
import numpy as np
from jax import lax
from jax.experimental import pallas as pl
from jax.experimental.pallas import tpu as pltpu
from jax.sharding import PartitionSpec as P

TAPS = np.array([1.0, 4.0, 6.0, 4.0, 1.0]) / 16.0
MESH = pl.DeviceIdType.MESH
BF = jnp.bfloat16
F32 = jnp.float32

ROWS = 1024
BLOCK = 256
COLS = 256
WIN = 288
MID = 144
LOW = 80
KEEP = 136
KEEP2 = 72
SUB = 64
SUBS = BLOCK // SUB
EXPO = float(-4.0 * np.log2(np.e))


def reduce_matrix(n):
    m = np.zeros((n // 2, n))
    for i in range(n // 2):
        for t in range(5):
            j = 2 * i - 2 + t
            if 0 <= j < n:
                m[i, j] = TAPS[t]
    return m


def expand_matrix(n):
    m = np.zeros((2 * n, n))
    for j in range(2 * n):
        for i in range(max(0, j // 2 - 2), min(n, j // 2 + 3)):
            t = j - 2 * i + 2
            if 0 <= t <= 4:
                m[j, i] = 2.0 * TAPS[t]
    return m


def window(m, row, rows, col, cols):
    out = np.zeros((rows, cols))
    r0, r1 = max(row, 0), min(row + rows, m.shape[0])
    c0, c1 = max(col, 0), min(col + cols, m.shape[1])
    out[r0 - row : r1 - row, c0 - col : c1 - col] = m[r0:r1, c0:c1]
    return out


def exact(m):
    cast = m.astype(ml_dtypes.bfloat16)
    assert (cast.astype(np.float64) == m).all()
    return cast


@functools.lru_cache(None)
def matrices():
    r0, r1 = reduce_matrix(ROWS), reduce_matrix(ROWS // 2)
    e0 = expand_matrix(ROWS // 2)
    row_in, row_low, row_up = [], [], []
    for p in range(4):
        start = min(max(BLOCK * p - 16, 0), ROWS - WIN)
        m = window(r0, 128 * p - 4, MID, start, WIN)
        row_in.append(np.concatenate([m, m], 1))
        m = window(r1, 64 * p - 2, LOW, 128 * p - 4, MID)
        row_low.append(np.concatenate([m, m], 1))
        m = window(e0, BLOCK * p, BLOCK, 128 * p - 4, MID)
        row_up.append(np.concatenate([m, m], 1))
    m = window(e0, SUB, SUB, 28, 48)
    row_sub = np.concatenate([m, m], 1)
    m = window(expand_matrix(ROWS // 4), 124, MID, 62, LOW)
    row_base = np.concatenate([m, m], 1)
    n = 3 * COLS
    c0, c1 = reduce_matrix(n), reduce_matrix(n // 2)
    x0 = expand_matrix(n // 2)
    col_in, col_halo, col_up = [], [], []
    for b in range(3):
        full = np.concatenate(
            [
                (x0 @ c0)[COLS * b : COLS * (b + 1)],
                c0[128 * b : 128 * (b + 1)],
                window(c1 @ c0, 64 * b - 1, 66, 0, n),
                np.zeros((62, n)),
            ],
            0,
        ).T
        col_in.append(full[COLS * b : COLS * (b + 1)])
        halo = np.zeros((128, 512))
        halo[:16] = window(full, COLS * b - 16, 16, 0, 512)
        halo[16:32] = window(full, COLS * (b + 1), 16, 0, 512)
        col_halo.append(np.concatenate([halo, halo], 0))
        up = x0[COLS * b : COLS * (b + 1)].T
        both = np.zeros((256, COLS))
        both[:128] = up[128 * b : 128 * (b + 1)]
        both[128:129] = window(up, 128 * b - 1, 1, 0, COLS)
        both[129:130] = window(up, 128 * (b + 1), 1, 0, COLS)
        col_up.append(both)
    col_base = np.zeros((128, 128))
    col_base[:66] = window(expand_matrix(n // 4), 128, 128, 63, 66).T
    stacks = (row_in, row_low, row_up, [row_sub], [row_base], col_in, col_halo, col_up, [col_base])
    return tuple(exact(np.stack(s)) for s in stacks)


def split(v):
    hi = v.astype(BF)
    lo = (v - hi.astype(F32)).astype(BF)
    return hi, lo


def dot(a, b):
    return jnp.dot(a, b, preferred_element_type=F32)


def tall(v):
    return jnp.concatenate(split(v), 0)


def inverse(v):
    r = pl.reciprocal(v, approx=True)
    return r * (2.0 - v * r)


def weight(d):
    return jnp.exp2(EXPO * inverse(1.0 + d * d))


def kernel(
    count,
    x_ref, row_in_ref, row_low_ref, row_up_ref, row_sub_ref, row_base_ref,
    col_in_ref, col_halo_ref, col_up_ref, col_base_ref,
    out_ref,
    xwin, m_row_in, m_row_low, m_row_up, m_row_sub, m_row_base, m_col_in, m_col_halo, m_col_up, m_col_base,
    hr, pack, halo, wide, mid, low,
    level0, level1, far0, far1, jbuf, jhalo, upper,
    m_sem, x_sem, swap_send, swap_recv, halo_send, halo_recv, far_send, far_recv, j_send, j_recv,
):
    me = lax.axis_index("plane")
    q = lax.axis_index("col")
    chip, core = me // 2, me % 2
    far = 2 * (1 - chip) + core
    sibling = 2 * chip + 1 - core
    far_sibling = 2 * (1 - chip) + 1 - core
    right = (q + 1) % count
    left = (q + count - 1) % count
    side = (q + count - 2) // (count - 1) + q // (count - 1)
    blocks = (far, me)

    def start_of(p):
        return pl.multiple_of(BLOCK * p - 16 + 16 * ((3 - p) // 3) - 16 * (p // 3), 16)

    def offset_of(p):
        return pl.multiple_of(16 - 16 * ((3 - p) // 3) + 16 * (p // 3), 16)

    own = []
    for b in range(2):
        own.append(
            pltpu.make_async_copy(
                x_ref.at[:, pl.ds(start_of(blocks[b]), WIN)], xwin.at[b, pl.ds(0, 2)], x_sem.at[b]
            )
        )
    loads = [
        (row_in_ref.at[far], m_row_in.at[0]),
        (row_in_ref.at[me], m_row_in.at[1]),
        (col_in_ref.at[side], m_col_in),
        (col_halo_ref.at[side], m_col_halo),
        (row_sub_ref.at[0], m_row_sub),
        (row_low_ref.at[far], m_row_low.at[0]),
        (row_low_ref.at[me], m_row_low.at[1]),
        (col_base_ref.at[0], m_col_base),
        (row_base_ref.at[0], m_row_base),
        (col_up_ref.at[side], m_col_up),
        (row_up_ref.at[me], m_row_up),
    ]
    loads = [pltpu.make_async_copy(s, d, m_sem.at[i]) for i, (s, d) in enumerate(loads)]
    own[0].start()
    loads[0].start()
    own[1].start()
    for copy in loads[1:]:
        copy.start()

    barrier = pltpu.get_barrier_semaphore()
    for plane, col in ((sibling, q), (far, q), (me, left), (me, right)):
        pl.semaphore_signal(barrier, inc=1, device_id=(plane, col), device_id_type=MESH)
    jbuf[pl.ds(KEEP, MID - KEEP)] = jnp.zeros((MID - KEEP, 128), F32)
    pl.semaphore_wait(barrier, 4)

    def remote(src, dst, send, recv, plane, col):
        return pltpu.make_async_remote_copy(
            src_ref=src, dst_ref=dst, send_sem=send, recv_sem=recv, device_id=(plane, col), device_id_type=MESH
        )

    swaps = []
    for b, p in enumerate((far_sibling, sibling)):
        swaps.append(
            remote(
                x_ref.at[:, pl.ds(start_of(p), WIN)],
                xwin.at[b, pl.ds(2, 2)],
                swap_send.at[b],
                swap_recv.at[b],
                sibling,
                q,
            )
        )
    for copy in swaps:
        copy.start()

    lane = lax.broadcasted_iota(jnp.int32, (MID, 128), 1)
    halos = []
    for b in range(2):
        packs = [jnp.zeros((MID, 128), F32), jnp.zeros((MID, 128), F32)]
        for p in range(4):
            if p == 0:
                own[b].wait()
                loads[b].wait()
            if p == 2:
                swaps[b].wait_recv()
            value = dot(m_row_in[b], tall(xwin[b, p]))
            hr[b, p] = value
            here = (lane >= 16 * p) & (lane < 16 * p + 16)
            low_cols = value[:, :128]
            high_cols = value[:, 128:]
            if p > 0:
                low_cols = pltpu.roll(low_cols, 16 * p, 1)
            high_cols = pltpu.roll(high_cols, (16 + 16 * p) % 128, 1)
            packs[0] = jnp.where(here, low_cols, packs[0])
            packs[1] = jnp.where(here, high_cols, packs[1])
        pack[b, 0] = packs[0]
        pack[b, 1] = packs[1]
        for d, col in enumerate((left, right)):
            copy = remote(pack.at[b, d], halo.at[b, 1 - d], halo_send.at[b, d], halo_recv.at[b, 1 - d], me, col)
            copy.start()
            halos.append(copy)

    for copy in loads[2:]:
        copy.wait()

    fars = []

    def send_far(src, dst, i):
        copy = remote(src, dst, far_send.at[i], far_recv.at[i], far, q)
        copy.start()
        fars.append(copy)

    for b in range(2):
        halos[2 * b].wait_recv()
        halos[2 * b + 1].wait_recv()
        for p in range(4):
            hi, lo = split(hr[b, p])
            from_left, from_right = halo[b, 0], halo[b, 1]
            if p > 0:
                from_left = pltpu.roll(from_left, 128 - 16 * p, 1)
            from_right = pltpu.roll(from_right, (128 + 16 - 16 * p) % 128, 1)
            edge = jnp.where(lane < 16, from_left, jnp.where(lane < 32, from_right, 0.0))
            ehi, elo = split(edge)
            value = dot(hi, m_col_in[...]) + dot(lo, m_col_in[...])
            value = value + dot(jnp.concatenate([ehi, elo], 1), m_col_halo[...])
            whi, wlo = split(value[:, :COLS])
            wide[p, 0] = whi
            wide[p, 1] = wlo
            mid[p] = value[:, COLS : COLS + 128]
            low[p] = value[:, COLS + 128 :]

        def join_zero(s):
            num = jnp.zeros((SUB, COLS), F32)
            den = jnp.zeros((SUB, COLS), F32)
            for p in range(4):
                rows = pl.ds(32 * s, 48)
                both = jnp.concatenate([wide[p, 0, rows], wide[p, 1, rows]], 0)
                z = dot(m_row_sub[...], both)
                d = xwin[b, p, pl.ds(pl.multiple_of(offset_of(blocks[b]) + SUB * s, 16), SUB)] - z
                w = weight(d)
                num = num + w * d
                den = den + w
            level0[b, s, 0] = num
            level0[b, s, 1] = den
            if b == 0:
                send_far(level0.at[b, s], far0.at[s], s)

        def join_one():
            num = jnp.zeros((MID, 128), F32)
            den = jnp.zeros((MID, 128), F32)
            total = jnp.zeros((LOW, 128), F32)
            for p in range(4):
                c2 = dot(m_row_low[b], tall(low[p]))
                total = total + c2
                hi, lo = split(c2)
                u = dot(hi, m_col_base[...]) + dot(lo, m_col_base[...])
                base = dot(m_row_base[...], tall(u))
                d = mid[p] - base
                w = weight(d)
                num = num + w * d
                den = den + w
            level1[b, pl.ds(0, KEEP)] = num[:KEEP]
            level1[b, pl.ds(KEEP, KEEP)] = den[:KEEP]
            level1[b, pl.ds(2 * KEEP, KEEP2)] = total[:KEEP2]
            if b == 0:
                send_far(level1.at[b], far1, SUBS)

        join_zero(0)
        join_one()
        for s in range(1, SUBS):
            join_zero(s)

    fars[1].wait_recv()
    num = level1[1, pl.ds(0, KEEP)] + far1[pl.ds(0, KEEP)]
    den = level1[1, pl.ds(KEEP, KEEP)] + far1[pl.ds(KEEP, KEEP)]
    total = level1[1, pl.ds(2 * KEEP, KEEP2)] + far1[pl.ds(2 * KEEP, KEEP2)]
    total = jnp.concatenate([total, jnp.zeros((LOW - KEEP2, 128), F32)], 0)
    hi, lo = split(total)
    u = dot(hi, m_col_base[...]) + dot(lo, m_col_base[...])
    base = dot(m_row_base[...], tall(u))
    jbuf[pl.ds(0, KEEP)] = num * inverse(den) + base[:KEEP] * 0.125
    js = []
    for d, col in enumerate((left, right)):
        copy = remote(jbuf.at[pl.ds(0, KEEP)], jhalo.at[1 - d, pl.ds(0, KEEP)], j_send.at[d], j_recv.at[1 - d], me, col)
        copy.start()
        js.append(copy)
    for copy in js:
        copy.wait_recv()
    from_left = pltpu.roll(jhalo[0, pl.ds(0, KEEP)], 1, 1)
    from_right = pltpu.roll(jhalo[1, pl.ds(0, KEEP)], 1, 1)
    lane = lax.broadcasted_iota(jnp.int32, (KEEP, 128), 1)
    edge = jnp.where(lane == 0, from_left, jnp.where(lane == 1, from_right, 0.0))
    edge = jnp.concatenate([edge, jnp.zeros((MID - KEEP, 128), F32)], 0)
    hi, lo = split(jnp.concatenate([jbuf[...], edge], 1))
    u = dot(hi, m_col_up[...]) + dot(lo, m_col_up[...])
    upper[...] = dot(m_row_up[...], tall(u))

    for s in range(SUBS):
        fars[0 if s == 0 else s + 1].wait_recv()
        num = level0[1, s, 0] + far0[s, 0]
        den = level0[1, s, 1] + far0[s, 1]
        rows = pl.ds(SUB * s, SUB)
        out_ref[rows] = num * inverse(den) + upper[rows]

    for copy in swaps + halos + fars + js:
        copy.wait_send()


def solution(mesh):
    count = mesh.shape["col"]
    consts = matrices()

    def body(x):
        dma = pltpu.SemaphoreType.DMA
        vmem = pltpu.VMEM
        shapes = [c.shape[1:] for c in consts]
        per_block = {0: 2, 1: 2}
        held = [vmem((per_block[i],) + s if i in per_block else s, BF) for i, s in enumerate(shapes)]
        return pl.pallas_call(
            functools.partial(kernel, count),
            out_shape=jax.ShapeDtypeStruct((BLOCK, COLS), F32),
            in_specs=[pl.BlockSpec(memory_space=pl.ANY)] * (1 + len(consts)),
            out_specs=pl.BlockSpec(memory_space=pltpu.VMEM),
            scratch_shapes=[vmem((2, 4, WIN, COLS), F32)]
            + held
            + [
                vmem((2, 4, MID, COLS), F32),
                vmem((2, 2, MID, 128), F32),
                vmem((2, 2, MID, 128), F32),
                vmem((4, 2, MID, COLS), BF),
                vmem((4, MID, 128), F32),
                vmem((4, MID, 128), F32),
                vmem((2, SUBS, 2, SUB, COLS), F32),
                vmem((2, 2 * KEEP + KEEP2, 128), F32),
                vmem((SUBS, 2, SUB, COLS), F32),
                vmem((2 * KEEP + KEEP2, 128), F32),
                vmem((MID, 128), F32),
                vmem((2, MID, 128), F32),
                vmem((BLOCK, COLS), F32),
                dma((11,)),
                dma((2,)),
                dma((2,)),
                dma((2,)),
                dma((2, 2)),
                dma((2, 2)),
                dma((SUBS + 1,)),
                dma((SUBS + 1,)),
                dma((2,)),
                dma((2,)),
            ],
            compiler_params=pltpu.CompilerParams(
                collective_id=0, has_side_effects=True, vmem_limit_bytes=48 * 1024 * 1024
            ),
        )(x, *consts)

    return jax.shard_map(body, mesh=mesh, in_specs=(P("plane", None, "col"),), out_specs=P("plane", "col"), check_vma=False)
```

```python
import functools

import jax
import jax.numpy as jnp
import ml_dtypes
import numpy as np
from jax import lax
from jax.experimental import pallas as pl
from jax.experimental.pallas import tpu as pltpu
from jax.sharding import PartitionSpec as P

TAPS = np.array([1.0, 4.0, 6.0, 4.0, 1.0]) / 16.0
MESH = pl.DeviceIdType.MESH
BF = jnp.bfloat16
F32 = jnp.float32

ROWS = 1024
BLOCK = 256
COLS = 256
WIN = 288
MID = 144
LOW = 80
KEEP = 136
KEEP2 = 72
SUB = 64
SUBS = BLOCK // SUB
EXT = 67
MESSAGE = 2 * KEEP + KEEP2 + SUB
GATE = 3
EXPO = float(-4.0 * np.log2(np.e))


def reduce_matrix(n):
    m = np.zeros((n // 2, n))
    for i in range(n // 2):
        for t in range(5):
            j = 2 * i - 2 + t
            if 0 <= j < n:
                m[i, j] = TAPS[t]
    return m


def expand_matrix(n):
    m = np.zeros((2 * n, n))
    for j in range(2 * n):
        for i in range(max(0, j // 2 - 2), min(n, j // 2 + 3)):
            t = j - 2 * i + 2
            if 0 <= t <= 4:
                m[j, i] = 2.0 * TAPS[t]
    return m


def window(m, row, rows, col, cols):
    out = np.zeros((rows, cols))
    r0, r1 = max(row, 0), min(row + rows, m.shape[0])
    c0, c1 = max(col, 0), min(col + cols, m.shape[1])
    out[r0 - row : r1 - row, c0 - col : c1 - col] = m[r0:r1, c0:c1]
    return out


def exact(m):
    cast = m.astype(ml_dtypes.bfloat16)
    assert (cast.astype(np.float64) == m).all()
    return cast


@functools.lru_cache(None)
def matrices():
    r0, r1 = reduce_matrix(ROWS), reduce_matrix(ROWS // 2)
    e0 = expand_matrix(ROWS // 2)
    row_in, row_low, row_up = [], [], []
    for p in range(4):
        start = min(max(BLOCK * p - 16, 0), ROWS - WIN)
        m = window(r0, 128 * p - 4, MID, start, WIN)
        row_in.append(np.concatenate([m, m], 1))
        m = window(r1, 64 * p - 2, LOW, 128 * p - 4, MID)
        row_low.append(np.concatenate([m, m], 1))
        m = window(e0, BLOCK * p, BLOCK, 128 * p - 4, MID)
        row_up.append(np.concatenate([m, m], 1))
    m = window(e0, SUB, SUB, 28, 48)
    row_sub = np.concatenate([m, m], 1)
    m = window(expand_matrix(ROWS // 4), 124, MID, 62, LOW)
    row_base = np.concatenate([m, m], 1)
    n = 3 * COLS
    c0, c1 = reduce_matrix(n), reduce_matrix(n // 2)
    x0 = expand_matrix(n // 2)
    col_in, col_halo, col_up = [], [], []
    for b in range(3):
        full = np.concatenate(
            [
                (x0 @ c0)[COLS * b : COLS * (b + 1)],
                c0[128 * b : 128 * (b + 1)],
                window(c1 @ c0, 64 * b - 1, 67, 0, n),
                window(c0, 128 * b - 1, 1, 0, n),
                window(c0, 128 * (b + 1), 1, 0, n),
                np.zeros((59, n)),
            ],
            0,
        ).T
        col_in.append(full[COLS * b : COLS * (b + 1)])
        halo = np.zeros((128, 512))
        halo[:16] = window(full, COLS * b - 16, 16, 0, 512)
        halo[16:32] = window(full, COLS * (b + 1), 16, 0, 512)
        col_halo.append(np.concatenate([halo, halo], 0))
        up = x0[COLS * b : COLS * (b + 1)].T
        both = np.zeros((256, COLS))
        both[:128] = up[128 * b : 128 * (b + 1)]
        both[128 + EXT] = window(up, 128 * b - 1, 1, 0, COLS)[0]
        both[128 + EXT + 1] = window(up, 128 * (b + 1), 1, 0, COLS)[0]
        col_up.append(both)
    col_base = np.zeros((128, 256))
    base = expand_matrix(n // 4)
    col_base[:67, :128] = window(base, 128, 128, 63, 67).T
    col_base[:67, 128 + EXT] = window(base, 127, 1, 63, 67)[0]
    col_base[:67, 128 + EXT + 1] = window(base, 256, 1, 63, 67)[0]
    stacks = (row_in, row_low, row_up, [row_sub], [row_base], col_in, col_halo, col_up, [col_base])
    return tuple(exact(np.stack(s)) for s in stacks)


def split(v):
    hi = v.astype(BF)
    lo = (v - hi.astype(F32)).astype(BF)
    return hi, lo


def dot(a, b):
    return jnp.dot(a, b, preferred_element_type=F32)


def tall(v):
    return jnp.concatenate(split(v), 0)


def inverse(v):
    r = pl.reciprocal(v, approx=True)
    return r * (2.0 - v * r)


def weight(d):
    return jnp.exp2(EXPO * inverse(1.0 + d * d))


def kernel(
    count,
    x_ref, row_in_ref, row_low_ref, row_up_ref, row_sub_ref, row_base_ref,
    col_in_ref, col_halo_ref, col_up_ref, col_base_ref,
    out_ref,
    xwin, m_row_in, m_row_low, m_row_up, m_row_sub, m_row_base, m_col_in, m_col_halo, m_col_up, m_col_base,
    hr, pack, halo, wide, fine,
    level0, level1, far0, far1, jbuf, upper,
    m_sem, x_sem, swap_send, swap_recv, halo_send, halo_recv, far_send, far_recv, group_sem, beside_sem,
):
    me = lax.axis_index("plane")
    q = lax.axis_index("col")
    chip, core = me // 2, me % 2
    far = 2 * (1 - chip) + core
    sibling = 2 * chip + 1 - core
    far_sibling = 2 * (1 - chip) + 1 - core
    side = (q + count - 2) // (count - 1) + q // (count - 1)
    left, right = (q + count - 1) % count, (q + 1) % count
    has_left, has_right = q > 0, q < count - 1
    blocks = (far, me)

    def start_of(p):
        return pl.multiple_of(BLOCK * p - 16 + 16 * ((3 - p) // 3) - 16 * (p // 3), 16)

    def offset_of(p):
        return pl.multiple_of(16 - 16 * ((3 - p) // 3) + 16 * (p // 3), 16)

    own = []
    for b in range(2):
        own.append(
            pltpu.make_async_copy(
                x_ref.at[:, pl.ds(start_of(blocks[b]), WIN)], xwin.at[b, pl.ds(0, 2)], x_sem.at[b]
            )
        )
    loads = [
        (row_in_ref.at[far], m_row_in.at[0]),
        (row_in_ref.at[me], m_row_in.at[1]),
        (col_in_ref.at[side], m_col_in),
        (row_sub_ref.at[0], m_row_sub),
        (col_halo_ref.at[side], m_col_halo),
        (row_low_ref.at[far], m_row_low.at[0]),
        (row_low_ref.at[me], m_row_low.at[1]),
        (col_base_ref.at[0], m_col_base),
        (row_base_ref.at[0], m_row_base),
        (col_up_ref.at[side], m_col_up),
        (row_up_ref.at[me], m_row_up),
    ]
    loads = [pltpu.make_async_copy(s, d, m_sem.at[i]) for i, (s, d) in enumerate(loads)]
    own[0].start()
    loads[0].start()
    loads[2].start()
    loads[3].start()
    own[1].start()
    loads[1].start()
    for copy in loads[4:]:
        copy.start()

    barrier = pltpu.get_barrier_semaphore()

    def tell(sem, plane, col):
        pl.semaphore_signal(sem, inc=1, device_id=(plane, col), device_id_type=MESH)

    @pl.when(sibling != GATE)
    def _():
        tell(barrier, sibling, q)

    @pl.when(far != GATE)
    def _():
        tell(barrier, far, q)

    jbuf[pl.ds(KEEP, MID - KEEP)] = jnp.zeros((MID - KEEP, COLS), F32)

    @pl.when(q == 0)
    def _():
        halo[0] = jnp.zeros((MID, 128), F32)

    @pl.when(q == count - 1)
    def _():
        halo[1] = jnp.zeros((MID, 128), F32)

    @pl.when(me != GATE)
    def _():
        pl.semaphore_wait(barrier, 2)

    @pl.when((sibling == GATE) | (far == GATE))
    def _():
        tell(group_sem, GATE, q)

    @pl.when(me == GATE)
    def _():
        pl.semaphore_wait(group_sem, 2)

        @pl.when(has_left)
        def _():
            tell(barrier, GATE, left)

        @pl.when(has_right)
        def _():
            tell(barrier, GATE, right)

    def remote(src, dst, send, recv, plane, col):
        return pltpu.make_async_remote_copy(
            src_ref=src, dst_ref=dst, send_sem=send, recv_sem=recv, device_id=(plane, col), device_id_type=MESH
        )

    swaps = []
    for b, p in enumerate((far_sibling, sibling)):
        swaps.append(
            remote(
                x_ref.at[:, pl.ds(start_of(p), WIN)],
                xwin.at[b, pl.ds(2, 2)],
                swap_send.at[b],
                swap_recv.at[b],
                sibling,
                q,
            )
        )
    for copy in swaps:
        copy.start()

    lane = lax.broadcasted_iota(jnp.int32, (MID, 128), 1)
    sub_lane = lax.broadcasted_iota(jnp.int32, (SUB, 128), 1)
    low_lane = lax.broadcasted_iota(jnp.int32, (KEEP2, 128), 1)

    def turn(v, by):
        by = by % 128
        return pltpu.roll(v, by, 1) if by else v

    def rows_in(b):
        for p in range(4):
            if p == 0:
                own[b].wait()
                loads[b].wait()
            if p == 2:
                swaps[b].wait_recv()
            hr[b, p] = dot(m_row_in[b], tall(xwin[b, p]))

    def pack_edges(b, packs):
        for p in range(4):
            at = 64 * b + 16 * p
            here = (lane >= at) & (lane < at + 16)
            packs[0] = jnp.where(here, turn(hr[b, p, :, pl.ds(0, 128)], at), packs[0])
            packs[1] = jnp.where(here, turn(hr[b, p, :, pl.ds(128, 128)], 16 + at), packs[1])

    def put_wide(p, value):
        whi, wlo = split(value)
        wide[p, 0] = whi
        wide[p, 1] = wlo

    def sums_zero(b, s):
        num = jnp.zeros((SUB, COLS), F32)
        den = jnp.zeros((SUB, COLS), F32)
        for p in range(4):
            rows = pl.ds(32 * s, 48)
            both = jnp.concatenate([wide[p, 0, rows], wide[p, 1, rows]], 0)
            z = dot(m_row_sub[...], both)
            d = xwin[b, p, pl.ds(pl.multiple_of(offset_of(blocks[b]) + SUB * s, 16), SUB)] - z
            w = weight(d)
            num = num + w * d
            den = den + w
        return num, den

    far_zero = [remote(level0.at[0, s], far0.at[s], far_send.at[s], far_recv.at[s], far, q) for s in range(SUBS)]
    rows_in(0)
    loads[2].wait()
    loads[3].wait()
    for p in range(4):
        hi, lo = split(hr[0, p])
        m = m_col_in[:, pl.ds(0, COLS)]
        put_wide(p, dot(jnp.concatenate([hi, lo], 1), jnp.concatenate([m, m], 0)))
    for s in range(SUBS):
        num, den = sums_zero(0, s)
        level0[0, s, 0] = num
        level0[0, s, 1] = den
        if s < SUBS - 1:
            far_zero[s].start()

    rows_in(1)
    packs = [jnp.zeros((MID, 128), F32), jnp.zeros((MID, 128), F32)]
    pack_edges(0, packs)
    pack_edges(1, packs)
    pack[0] = packs[0]
    pack[1] = packs[1]

    @pl.when(me == GATE)
    def _():
        pl.semaphore_wait(barrier, (q + count - 1) // count + (2 * count - 2 - q) // count)

        for plane in range(GATE):
            tell(beside_sem, plane, q)

    @pl.when(me != GATE)
    def _():
        pl.semaphore_wait(beside_sem, 1)

    to_left = remote(pack.at[0], halo.at[1], halo_send.at[0], halo_recv.at[1], me, left)
    to_right = remote(pack.at[1], halo.at[0], halo_send.at[1], halo_recv.at[0], me, right)

    @pl.when(has_left)
    def _():
        to_left.start()

    @pl.when(has_right)
    def _():
        to_right.start()

    for copy in loads[4:]:
        copy.wait()

    @pl.when(has_left)
    def _():
        to_right.wait_recv()

    @pl.when(has_right)
    def _():
        to_left.wait_recv()

    far_one = remote(level1.at[0], far1, far_send.at[SUBS], far_recv.at[SUBS], far, q)
    for b in range(2):
        for p in range(4):
            hi, lo = split(hr[b, p])
            at = 64 * b + 16 * p
            edge = jnp.where(lane < 16, turn(halo[0], -at), jnp.where(lane < 32, turn(halo[1], 16 - at), 0.0))
            ehi, elo = split(edge)
            m = m_col_in[...]
            value = dot(jnp.concatenate([hi, lo, ehi, elo], 1), jnp.concatenate([m, m, m_col_halo[...]], 0))
            put_wide(p, value[:, :COLS])
            fine[p] = value[:, COLS:]

        num = jnp.zeros((MID, COLS), F32)
        den = jnp.zeros((MID, COLS), F32)
        total = jnp.zeros((LOW, 128), F32)
        for p in range(4):
            c2 = dot(m_row_low[b], tall(fine[p, :, pl.ds(128, 128)]))
            total = total + c2
            hi, lo = split(c2)
            m = m_col_base[...]
            u = dot(jnp.concatenate([hi, lo], 1), jnp.concatenate([m, m], 0))
            d = fine[p] - dot(m_row_base[...], tall(u))
            w = weight(d)
            num = num + w * d
            den = den + w
        level1[b, pl.ds(0, KEEP)] = num[:KEEP, :128]
        level1[b, pl.ds(KEEP, KEEP)] = den[:KEEP, :128]
        tile = turn(den[64 : 64 + KEEP2, 128:], 6)
        tile = jnp.where(low_lane < EXT + 6, turn(den[:KEEP2, 128:], 4), tile)
        tile = jnp.where(low_lane < EXT + 4, turn(num[64 : 64 + KEEP2, 128:], 2), tile)
        tile = jnp.where(low_lane < EXT + 2, num[:KEEP2, 128:], tile)
        level1[b, pl.ds(2 * KEEP, KEEP2)] = jnp.where(low_lane < EXT, total[:KEEP2], tile)

        patch = jnp.zeros((SUB, 128), F32)
        for s in range(SUBS):
            num, den = sums_zero(b, s)
            if b == 0:
                for at, v in ((8 * s, num), (32 + 8 * s, den)):
                    edges = jnp.where(sub_lane < 64, v[:, :128], v[:, 128:])
                    patch = jnp.where((sub_lane >= at) & (sub_lane < at + 8), turn(edges, 4 + at), patch)
            else:
                level0[1, s, 0] = num
                level0[1, s, 1] = den
        if b == 0:
            level1[0, pl.ds(2 * KEEP + KEEP2, SUB)] = patch
            far_one.start()
            far_zero[SUBS - 1].start()

    far_one.wait_recv()
    rows = pl.ds(2 * KEEP, KEEP2)
    tile = level1[1, rows] + far1[rows]
    total = jnp.concatenate([jnp.where(low_lane < EXT, tile, 0.0), jnp.zeros((LOW - KEEP2, 128), F32)], 0)
    hi, lo = split(total)
    m = m_col_base[...]
    u = dot(jnp.concatenate([hi, lo], 1), jnp.concatenate([m, m], 0))
    base = dot(m_row_base[...], tall(u))
    num = level1[1, pl.ds(0, KEEP)] + far1[pl.ds(0, KEEP)]
    den = level1[1, pl.ds(KEEP, KEEP)] + far1[pl.ds(KEEP, KEEP)]
    jbuf[pl.ds(0, KEEP), pl.ds(0, 128)] = num * inverse(den) + base[:KEEP, :128] * 0.125
    outer = (low_lane >= EXT) & (low_lane < EXT + 4)
    ratio = jnp.where(outer, tile, 0.0) * inverse(jnp.where(outer, turn(tile, -4), 1.0))
    ratio = jnp.concatenate([ratio[:64], turn(ratio, -2)], 0) + base[:KEEP, 128:] * 0.125
    keep_lane = lax.broadcasted_iota(jnp.int32, (KEEP, 128), 1)
    ratio = jnp.where((keep_lane >= EXT) & (keep_lane < EXT + 2), ratio, 0.0)
    jbuf[pl.ds(0, KEEP), pl.ds(128, 128)] = ratio
    hi, lo = split(jbuf[...])
    m = m_col_up[...]
    u = dot(jnp.concatenate([hi, lo], 1), jnp.concatenate([m, m], 0))
    upper[...] = dot(m_row_up[...], tall(u))

    patch = far1[pl.ds(2 * KEEP + KEEP2, SUB)]
    for s in range(SUBS):
        far_zero[s].wait_recv()
        sums = []
        for i in range(2):
            edges = turn(patch, -(4 + 32 * i + 8 * s))
            first = jnp.where(sub_lane < 4, edges, far0[s, i, :, pl.ds(0, 128)])
            second = jnp.where(sub_lane >= 124, edges, far0[s, i, :, pl.ds(128, 128)])
            sums.append(level0[1, s, i] + jnp.concatenate([first, second], 1))
        rows = pl.ds(SUB * s, SUB)
        out_ref[rows] = sums[0] * inverse(sums[1]) + upper[rows]

    @pl.when(has_left)
    def _():
        to_left.wait_send()

    @pl.when(has_right)
    def _():
        to_right.wait_send()

    for copy in swaps + far_zero + [far_one]:
        copy.wait_send()


def solution(mesh):
    count = mesh.shape["col"]
    consts = matrices()

    def body(x):
        dma = pltpu.SemaphoreType.DMA
        vmem = pltpu.VMEM
        shapes = [c.shape[1:] for c in consts]
        per_block = {0: 2, 1: 2}
        held = [vmem((per_block[i],) + s if i in per_block else s, BF) for i, s in enumerate(shapes)]
        return pl.pallas_call(
            functools.partial(kernel, count),
            out_shape=jax.ShapeDtypeStruct((BLOCK, COLS), F32),
            in_specs=[pl.BlockSpec(memory_space=pl.ANY)] * (1 + len(consts)),
            out_specs=pl.BlockSpec(memory_space=pltpu.VMEM),
            scratch_shapes=[vmem((2, 4, WIN, COLS), F32)]
            + held
            + [
                vmem((2, 4, MID, COLS), F32),
                vmem((2, MID, 128), F32),
                vmem((2, MID, 128), F32),
                vmem((4, 2, MID, COLS), BF),
                vmem((4, MID, COLS), F32),
                vmem((2, SUBS, 2, SUB, COLS), F32),
                vmem((2, MESSAGE, 128), F32),
                vmem((SUBS, 2, SUB, COLS), F32),
                vmem((MESSAGE, 128), F32),
                vmem((MID, COLS), F32),
                vmem((BLOCK, COLS), F32),
                dma((11,)),
                dma((2,)),
                dma((2,)),
                dma((2,)),
                dma((2,)),
                dma((2,)),
                dma((SUBS + 1,)),
                dma((SUBS + 1,)),
                pltpu.SemaphoreType.REGULAR,
                pltpu.SemaphoreType.REGULAR,
            ],
            compiler_params=pltpu.CompilerParams(
                collective_id=0, has_side_effects=True, vmem_limit_bytes=63 * 1024 * 1024
            ),
        )(x, *consts)

    return jax.shard_map(body, mesh=mesh, in_specs=(P("plane", None, "col"),), out_specs=P("plane", "col"), check_vma=False)
```

```python
import functools

import jax
import jax.numpy as jnp
import ml_dtypes
import numpy as np
from jax import lax
from jax.experimental import pallas as pl
from jax.experimental.pallas import tpu as pltpu
from jax.sharding import PartitionSpec as P

TAPS = np.array([1.0, 4.0, 6.0, 4.0, 1.0]) / 16.0
MESH = pl.DeviceIdType.MESH
BF = jnp.bfloat16
F32 = jnp.float32

ROWS = 1024
BLOCK = 256
COLS = 256
WIN = 288
MID = 144
LOW = 80
KEEP = 136
KEEP2 = 72
SUB = 64
SUBS = BLOCK // SUB
EXT = 67
WIDE = 640
ROW_PART = MID + LOW + BLOCK
COL_PART = 3 * 256
REST = 4 * ROW_PART + 3 * COL_PART
LATE = KEEP2 + SUB // 2
EDGE = 76
VMEM_BYTES = 52 * 1024 * 1024
GATE = 3
EXPO = float(-4.0 * np.log2(np.e))


def reduce_matrix(n):
    m = np.zeros((n // 2, n))
    for i in range(n // 2):
        for t in range(5):
            j = 2 * i - 2 + t
            if 0 <= j < n:
                m[i, j] = TAPS[t]
    return m


def expand_matrix(n):
    m = np.zeros((2 * n, n))
    for j in range(2 * n):
        for i in range(max(0, j // 2 - 2), min(n, j // 2 + 3)):
            t = j - 2 * i + 2
            if 0 <= t <= 4:
                m[j, i] = 2.0 * TAPS[t]
    return m


def window(m, row, rows, col, cols):
    out = np.zeros((rows, cols))
    r0, r1 = max(row, 0), min(row + rows, m.shape[0])
    c0, c1 = max(col, 0), min(col + cols, m.shape[1])
    out[r0 - row : r1 - row, c0 - col : c1 - col] = m[r0:r1, c0:c1]
    return out


def exact(m):
    cast = m.astype(ml_dtypes.bfloat16)
    assert (cast.astype(np.float64) == m).all()
    return cast


@functools.lru_cache(None)
def matrices():
    r0, r1 = reduce_matrix(ROWS), reduce_matrix(ROWS // 2)
    e0 = expand_matrix(ROWS // 2)
    row_in, row_low, row_up = [], [], []
    for p in range(4):
        start = min(max(BLOCK * p - 16, 0), ROWS - WIN)
        m = window(r0, 128 * p - 4, MID, start, WIN)
        row_in.append(np.concatenate([m, m], 1))
        m = window(r1, 64 * p - 2, LOW, 128 * p - 4, MID)
        row_low.append(np.concatenate([m, m], 1))
        m = window(e0, BLOCK * p, BLOCK, 128 * p - 4, MID)
        row_up.append(np.concatenate([m, m], 1))
    m = window(e0, SUB, SUB, 28, 48)
    row_sub = np.concatenate([m, m], 1)
    m = window(expand_matrix(ROWS // 4), 124, MID, 62, LOW)
    row_base = np.concatenate([m, m], 1)
    n = 3 * COLS
    c0, c1 = reduce_matrix(n), reduce_matrix(n // 2)
    x0 = expand_matrix(n // 2)
    col_in, col_halo, col_up = [], [], []
    for b in range(3):
        full = np.concatenate(
            [
                (x0 @ c0)[COLS * b : COLS * (b + 1)],
                c0[128 * b : 128 * (b + 1)],
                window(c1 @ c0, 64 * b - 1, 67, 0, n),
                window(c0, 128 * b - 1, 1, 0, n),
                window(c0, 128 * (b + 1), 1, 0, n),
                np.zeros((59, n)),
            ],
            0,
        ).T
        col_in.append(full[COLS * b : COLS * (b + 1)])
        halo = np.zeros((128, 512))
        halo[:16] = window(full, COLS * b - 16, 16, 0, 512)
        halo[16:32] = window(full, COLS * (b + 1), 16, 0, 512)
        col_halo.append(np.concatenate([halo, halo], 0))
        up = x0[COLS * b : COLS * (b + 1)].T
        both = np.zeros((256, COLS))
        both[:128] = up[128 * b : 128 * (b + 1)]
        both[128 + EXT] = window(up, 128 * b - 1, 1, 0, COLS)[0]
        both[128 + EXT + 1] = window(up, 128 * (b + 1), 1, 0, COLS)[0]
        col_up.append(both)
    col_base = np.zeros((128, 256))
    base = expand_matrix(n // 4)
    col_base[:67, :128] = window(base, 128, 128, 63, 67).T
    col_base[:67, 128 + EXT] = window(base, 127, 1, 63, 67)[0]
    col_base[:67, 128 + EXT + 1] = window(base, 256, 1, 63, 67)[0]
    parts = []
    for p in range(4):
        parts += [row_in[p], row_low[p], row_up[p]]
    for b in range(3):
        parts += [col_in[b], col_halo[b], col_up[b]]
    parts += [col_base, row_base, row_sub]
    return np.concatenate([exact(np.pad(m, ((0, 0), (0, WIDE - m.shape[1])))) for m in parts], 0)


def split(v):
    hi = v.astype(BF)
    lo = (v - hi.astype(F32)).astype(BF)
    return hi, lo


def dot(a, b):
    return jnp.dot(a, b, preferred_element_type=F32)


def tall(v):
    return jnp.concatenate(split(v), 0)


def inverse(v):
    r = pl.reciprocal(v, approx=True)
    return r * (2.0 - v * r)


def weight(d):
    return jnp.exp2(EXPO * inverse(1.0 + d * d))


def kernel(
    count,
    x_ref, const_ref,
    out_ref,
    xwin, m_row_in, m_row_low, m_row_up, m_row_sub, m_row_base, m_col_in, m_col_halo, m_col_up, m_col_base,
    hr, pack, halo, wide, c1, low,
    level0, level1, late, far0, far1, far_late, jbuf, upper,
    m_sem, x_sem, swap_send, swap_recv, halo_send, halo_recv, far_send, far_recv, group_sem, beside_sem,
):
    me = lax.axis_index("plane")
    q = lax.axis_index("col")
    chip, core = me // 2, me % 2
    far = 2 * (1 - chip) + core
    sibling = 2 * chip + 1 - core
    far_sibling = 2 * (1 - chip) + 1 - core
    side = (q + count - 2) // (count - 1) + q // (count - 1)
    left, right = (q + count - 1) % count, (q + 1) % count
    has_left, has_right = q > 0, q < count - 1
    blocks = (far, me)

    def start_of(p):
        return pl.multiple_of(BLOCK * p - 16 + 16 * ((3 - p) // 3) - 16 * (p // 3), 16)

    def offset_of(p):
        return pl.multiple_of(16 - 16 * ((3 - p) // 3) + 16 * (p // 3), 16)

    own = []
    for b in range(2):
        own.append(
            pltpu.make_async_copy(
                x_ref.at[:, pl.ds(start_of(blocks[b]), WIN)], xwin.at[b, pl.ds(0, 2)], x_sem.at[b]
            )
        )

    def const(at, rows, cols):
        return const_ref.at[pl.ds(pl.multiple_of(at, 16), rows), pl.ds(0, cols)]

    col_at = 4 * ROW_PART + COL_PART * side
    loads = [
        (const(ROW_PART * far, MID, WIDE), m_row_in.at[0]),
        (const(ROW_PART * me, MID, WIDE), m_row_in.at[1]),
        (const(col_at, 256, 512), m_col_in),
        (const(REST + 128 + MID, SUB, 128), m_row_sub),
        (const(ROW_PART * far + MID, LOW, 384), m_row_low.at[0]),
        (const(REST, 128, 256), m_col_base),
        (const(REST + 128, MID, 256), m_row_base),
        (const(col_at + 256, 256, 512), m_col_halo),
        (const(ROW_PART * me + MID, LOW, 384), m_row_low.at[1]),
        (const(col_at + 512, 256, 256), m_col_up),
        (const(ROW_PART * me + MID + LOW, BLOCK, 384), m_row_up),
    ]
    loads = [pltpu.make_async_copy(s, d, m_sem.at[i]) for i, (s, d) in enumerate(loads)]
    own[0].start()
    loads[0].start()
    loads[2].start()
    loads[3].start()

    barrier = pltpu.get_barrier_semaphore()

    def tell(sem, plane, col):
        pl.semaphore_signal(sem, inc=1, device_id=(plane, col), device_id_type=MESH)

    @pl.when(sibling != GATE)
    def _():
        tell(barrier, sibling, q)

    @pl.when(far != GATE)
    def _():
        tell(barrier, far, q)

    own[1].start()
    loads[1].start()
    for copy in loads[4:]:
        copy.start()
    jbuf[pl.ds(KEEP, MID - KEEP)] = jnp.zeros((MID - KEEP, COLS), F32)

    @pl.when(q == 0)
    def _():
        halo[0] = jnp.zeros((MID, 128), F32)

    @pl.when(q == count - 1)
    def _():
        halo[1] = jnp.zeros((MID, 128), F32)

    @pl.when(me != GATE)
    def _():
        pl.semaphore_wait(barrier, 2)

    @pl.when((sibling == GATE) | (far == GATE))
    def _():
        tell(group_sem, GATE, q)

    @pl.when(me == GATE)
    def _():
        pl.semaphore_wait(group_sem, 2)

        @pl.when(has_left)
        def _():
            tell(barrier, GATE, left)

        @pl.when(has_right)
        def _():
            tell(barrier, GATE, right)

    def remote(src, dst, send, recv, plane, col):
        return pltpu.make_async_remote_copy(
            src_ref=src, dst_ref=dst, send_sem=send, recv_sem=recv, device_id=(plane, col), device_id_type=MESH
        )

    swaps = []
    for b, p in enumerate((far_sibling, sibling)):
        swaps.append(
            remote(
                x_ref.at[:, pl.ds(start_of(p), WIN)],
                xwin.at[b, pl.ds(2, 2)],
                swap_send.at[b],
                swap_recv.at[b],
                sibling,
                q,
            )
        )
    for copy in swaps:
        copy.start()

    lane = lax.broadcasted_iota(jnp.int32, (MID, 128), 1)
    half_lane = lax.broadcasted_iota(jnp.int32, (SUB // 2, 128), 1)
    sub_lane = lax.broadcasted_iota(jnp.int32, (SUB, 128), 1)
    low_lane = lax.broadcasted_iota(jnp.int32, (KEEP2, 128), 1)
    keep_lane = lax.broadcasted_iota(jnp.int32, (KEEP, 128), 1)

    def turn(v, by):
        by = by % 128
        return pltpu.roll(v, by, 1) if by else v

    def rows_in(b, p):
        if p == 0:
            own[b].wait()
            loads[b].wait()
        if p == 2:
            swaps[b].wait_recv()
        value = dot(m_row_in[b, :, pl.ds(0, 2 * WIN)], tall(xwin[b, p]))
        hr[b, p] = value
        return value

    def put(p, value):
        whi, wlo = split(value[:, :COLS])
        wide[p, 0] = whi
        wide[p, 1] = wlo
        c1[p] = value[:, COLS : COLS + 128]
        low[:, pl.ds(128 * p, 128)] = value[:, COLS + 128 :]

    def sums_zero(b, s):
        num = jnp.zeros((SUB, COLS), F32)
        den = jnp.zeros((SUB, COLS), F32)
        for p in range(4):
            rows = pl.ds(32 * s, 48)
            both = jnp.concatenate([wide[p, 0, rows], wide[p, 1, rows]], 0)
            z = dot(m_row_sub[:, pl.ds(0, 96)], both)
            d = xwin[b, p, pl.ds(pl.multiple_of(offset_of(blocks[b]) + SUB * s, 16), SUB)] - z
            w = weight(d)
            num = num + w * d
            den = den + w
        return num, den

    def twice(ref):
        m = ref[...]
        return jnp.concatenate([m, m], 0)

    def columns_up(c2):
        return dot(jnp.concatenate(split(c2), 1), twice(m_col_base))

    def sums_one(b):
        c2 = dot(m_row_low[b, :, pl.ds(0, 2 * MID)], tall(low[...]))
        parts = [c2[:, 128 * p : 128 * p + 128] for p in range(4)]
        u = columns_up(jnp.concatenate(parts, 0))
        u = jnp.concatenate([u[LOW * p : LOW * p + LOW] for p in range(4)], 1)
        base = dot(m_row_base[:, pl.ds(0, 2 * LOW)], tall(u))
        num = jnp.zeros((MID, COLS), F32)
        den = jnp.zeros((MID, COLS), F32)
        for p in range(4):
            d = jnp.concatenate([c1[p], low[:, pl.ds(128 * p, 128)]], 1) - base[:, COLS * p : COLS * p + COLS]
            w = weight(d)
            num = num + w * d
            den = den + w
        return num, den, parts[0] + parts[1] + parts[2] + parts[3]

    def put_one(b, num, den):
        level1[b, 0] = num[:KEEP, :128]
        level1[b, 1] = den[:KEEP, :128]

    def late_tile(num, den, total):
        tile = turn(den[64 : 64 + KEEP2, 128:], 6)
        tile = jnp.where(low_lane < EXT + 6, turn(den[:KEEP2, 128:], 4), tile)
        tile = jnp.where(low_lane < EXT + 4, turn(num[64 : 64 + KEEP2, 128:], 2), tile)
        tile = jnp.where(low_lane < EXT + 2, num[:KEEP2, 128:], tile)
        tile = jnp.where(low_lane < EXT, total[:KEEP2], tile)
        for i, v in enumerate((num, den)):
            for h in range(2):
                at = EDGE + 20 * i + 10 * h
                tile = jnp.where(low_lane >= at, turn(v[64 * h : 64 * h + KEEP2, :128], 4 + at), tile)
        return tile

    far_zero = [remote(level0.at[0, s], far0.at[s], far_send.at[s], far_recv.at[s], far, q) for s in range(SUBS)]
    far_one = remote(level1.at[0], far1, far_send.at[SUBS], far_recv.at[SUBS], far, q)
    far_last = remote(late.at[0], far_late, far_send.at[SUBS + 1], far_recv.at[SUBS + 1], far, q)
    for p in range(4):
        value = rows_in(0, p)
        if p == 0:
            loads[2].wait()
            loads[3].wait()
        put(p, dot(jnp.concatenate(split(value), 1), twice(m_col_in)))

    def far_chunk(s):
        num, den = sums_zero(0, s)
        level0[0, s, 0] = num
        level0[0, s, 1] = den
        if s < SUBS - 1:
            far_zero[s].start()

    far_chunk(0)
    for p in range(4):
        rows_in(1, p)
    packs = [jnp.zeros((MID, 128), F32), jnp.zeros((MID, 128), F32)]
    for b in range(2):
        for p in range(4):
            at = 64 * b + 16 * p
            here = (lane >= at) & (lane < at + 16)
            packs[0] = jnp.where(here, turn(hr[b, p, :, pl.ds(0, 128)], at), packs[0])
            packs[1] = jnp.where(here, turn(hr[b, p, :, pl.ds(128, 128)], 16 + at), packs[1])
    pack[0] = packs[0]
    pack[1] = packs[1]

    to_left = remote(pack.at[0], halo.at[1], halo_send.at[0], halo_recv.at[1], me, left)
    to_right = remote(pack.at[1], halo.at[0], halo_send.at[1], halo_recv.at[0], me, right)

    def send_halo():
        @pl.when(me == GATE)
        def _():
            pl.semaphore_wait(barrier, (q + count - 1) // count + (2 * count - 2 - q) // count)
            for plane in range(GATE):
                tell(beside_sem, plane, q)

        @pl.when(me != GATE)
        def _():
            pl.semaphore_wait(beside_sem, 1)

        @pl.when(has_left)
        def _():
            to_left.start()

        @pl.when(has_right)
        def _():
            to_right.start()

    ahead = q % 8 == 0
    pl.when(jnp.logical_not(ahead))(send_halo)

    for s in range(1, SUBS):
        far_chunk(s)
    for copy in loads[4:7]:
        copy.wait()
    num, den, _ = sums_one(0)
    put_one(0, num, den)
    far_one.start()

    pl.when(ahead)(send_halo)

    for copy in loads[7:]:
        copy.wait()

    @pl.when(has_left)
    def _():
        to_right.wait_recv()

    @pl.when(has_right)
    def _():
        to_left.wait_recv()

    for b in range(2):
        for p in range(4):
            at = 64 * b + 16 * p
            edge = jnp.where(lane < 16, turn(halo[0], -at), jnp.where(lane < 32, turn(halo[1], 16 - at), 0.0))
            lhs = jnp.concatenate(split(hr[b, p]) + split(edge), 1)
            put(p, dot(lhs, jnp.concatenate([twice(m_col_in), m_col_halo[...]], 0)))

        num, den, total = sums_one(b)
        late[b, pl.ds(0, KEEP2)] = late_tile(num, den, total)
        if b == 1:
            put_one(b, num, den)

        patch = jnp.zeros((SUB // 2, 128), F32)
        for s in range(SUBS):
            num, den = sums_zero(b, s)
            if b == 1:
                level0[1, s, 0] = num
                level0[1, s, 1] = den
                continue
            for i, v in enumerate((num, den)):
                edges = jnp.where(sub_lane < 64, v[:, :128], v[:, 128:])
                for h in range(2):
                    at = 32 * s + 16 * h + 8 * i
                    moved = turn(edges[32 * h : 32 * h + 32], 4 + at)
                    patch = jnp.where((half_lane >= at) & (half_lane < at + 8), moved, patch)
        if b == 0:
            late[0, pl.ds(KEEP2, SUB // 2)] = patch
            far_last.start()
            far_zero[SUBS - 1].start()

    far_one.wait_recv()
    far_last.wait_recv()
    own_tile, far_tile = late[1, pl.ds(0, KEEP2)], far_late[pl.ds(0, KEEP2)]
    tile = own_tile + far_tile
    total = jnp.concatenate([jnp.where(low_lane < EXT, tile, 0.0), jnp.zeros((LOW - KEEP2, 128), F32)], 0)
    base = dot(m_row_base[:, pl.ds(0, 2 * LOW)], tall(columns_up(total)))
    at_edge = (keep_lane < 6) | (keep_lane >= 124)
    sums = []
    for i in range(2):
        at = EDGE + 20 * i
        edges = jnp.concatenate([turn(far_tile, -(4 + at))[:64], turn(far_tile, -(14 + at))], 0)
        sums.append(level1[1, i] + jnp.where(at_edge, edges, far1[i]))
    jbuf[pl.ds(0, KEEP), pl.ds(0, 128)] = sums[0] * inverse(sums[1]) + base[:KEEP, :128] * 0.125
    outer = (low_lane >= EXT) & (low_lane < EXT + 4)
    ratio = jnp.where(outer, tile, 0.0) * inverse(jnp.where(outer, turn(tile, -4), 1.0))
    ratio = jnp.concatenate([ratio[:64], turn(ratio, -2)], 0) + base[:KEEP, 128:] * 0.125
    ratio = jnp.where((keep_lane >= EXT) & (keep_lane < EXT + 2), ratio, 0.0)
    jbuf[pl.ds(0, KEEP), pl.ds(128, 128)] = ratio
    u = dot(jnp.concatenate(split(jbuf[...]), 1), twice(m_col_up))
    upper[...] = dot(m_row_up[:, pl.ds(0, 2 * MID)], tall(u))

    patch = far_late[pl.ds(KEEP2, SUB // 2)]
    for s in range(SUBS):
        far_zero[s].wait_recv()
        sums = []
        for i in range(2):
            at = 32 * s + 8 * i
            edges = jnp.concatenate([turn(patch, -(4 + at)), turn(patch, -(20 + at))], 0)
            first = jnp.where(sub_lane < 4, edges, far0[s, i, :, pl.ds(0, 128)])
            second = jnp.where(sub_lane >= 124, edges, far0[s, i, :, pl.ds(128, 128)])
            sums.append(level0[1, s, i] + jnp.concatenate([first, second], 1))
        rows = pl.ds(SUB * s, SUB)
        out_ref[rows] = sums[0] * inverse(sums[1]) + upper[rows]

    @pl.when(has_left)
    def _():
        to_left.wait_send()

    @pl.when(has_right)
    def _():
        to_right.wait_send()

    for copy in swaps + far_zero + [far_one, far_last]:
        copy.wait_send()


def solution(mesh):
    count = mesh.shape["col"]
    consts = matrices()

    def body(x):
        dma = pltpu.SemaphoreType.DMA
        vmem = pltpu.VMEM
        return pl.pallas_call(
            functools.partial(kernel, count),
            out_shape=jax.ShapeDtypeStruct((BLOCK, COLS), F32),
            in_specs=[pl.BlockSpec(memory_space=pl.ANY)] * 2,
            out_specs=pl.BlockSpec(memory_space=pltpu.VMEM),
            scratch_shapes=[
                vmem((2, 4, WIN, COLS), F32),
                vmem((2, MID, WIDE), BF),
                vmem((2, LOW, 384), BF),
                vmem((BLOCK, 384), BF),
                vmem((SUB, 128), BF),
                vmem((MID, 256), BF),
                vmem((256, 512), BF),
                vmem((256, 512), BF),
                vmem((256, 256), BF),
                vmem((128, 256), BF),
                vmem((2, 4, MID, COLS), F32),
                vmem((2, MID, 128), F32),
                vmem((2, MID, 128), F32),
                vmem((4, 2, MID, COLS), BF),
                vmem((4, MID, 128), F32),
                vmem((MID, 512), F32),
                vmem((2, SUBS, 2, SUB, COLS), F32),
                vmem((2, 2, KEEP, 128), F32),
                vmem((2, LATE, 128), F32),
                vmem((SUBS, 2, SUB, COLS), F32),
                vmem((2, KEEP, 128), F32),
                vmem((LATE, 128), F32),
                vmem((MID, COLS), F32),
                vmem((BLOCK, COLS), F32),
                dma((11,)),
                dma((2,)),
                dma((2,)),
                dma((2,)),
                dma((2,)),
                dma((2,)),
                dma((SUBS + 2,)),
                dma((SUBS + 2,)),
                pltpu.SemaphoreType.REGULAR,
                pltpu.SemaphoreType.REGULAR,
            ],
            compiler_params=pltpu.CompilerParams(
                collective_id=0, has_side_effects=True, vmem_limit_bytes=VMEM_BYTES
            ),
        )(x, consts)

    return jax.shard_map(body, mesh=mesh, in_specs=(P("plane", None, "col"),), out_specs=P("plane", "col"), check_vma=False)
```

```python
import functools

import jax
import jax.numpy as jnp
import ml_dtypes
import numpy as np
from jax import lax
from jax.experimental import pallas as pl
from jax.experimental.pallas import tpu as pltpu
from jax.sharding import PartitionSpec as P

TAPS = np.array([1.0, 4.0, 6.0, 4.0, 1.0]) / 16.0
MESH = pl.DeviceIdType.MESH
BF = jnp.bfloat16
F32 = jnp.float32

ROWS = 1024
BLOCK = 256
COLS = 256
WIN = 288
MID = 144
LOW = 80
KEEP = 136
KEEP2 = 72
SUB = 64
SUBS = BLOCK // SUB
EXT = 67
WIDE = 640
ROW_PART = MID + LOW + BLOCK
COL_PART = 2 * 256
REST = 4 * ROW_PART + 3 * COL_PART
LATE = KEEP2 + SUB // 2
EDGE = 76
VMEM_BYTES = 52 * 1024 * 1024
TO_RIGHT = 72
TO_LEFT = 80
PART = 48
GATE = 1
EXPO = float(-4.0 * np.log2(np.e))


def reduce_matrix(n):
    m = np.zeros((n // 2, n))
    for i in range(n // 2):
        for t in range(5):
            j = 2 * i - 2 + t
            if 0 <= j < n:
                m[i, j] = TAPS[t]
    return m


def expand_matrix(n):
    m = np.zeros((2 * n, n))
    for j in range(2 * n):
        for i in range(max(0, j // 2 - 2), min(n, j // 2 + 3)):
            t = j - 2 * i + 2
            if 0 <= t <= 4:
                m[j, i] = 2.0 * TAPS[t]
    return m


def window(m, row, rows, col, cols):
    out = np.zeros((rows, cols))
    r0, r1 = max(row, 0), min(row + rows, m.shape[0])
    c0, c1 = max(col, 0), min(col + cols, m.shape[1])
    out[r0 - row : r1 - row, c0 - col : c1 - col] = m[r0:r1, c0:c1]
    return out


def exact(m):
    cast = m.astype(ml_dtypes.bfloat16)
    assert (cast.astype(np.float64) == m).all()
    return cast


@functools.lru_cache(None)
def matrices():
    r0, r1 = reduce_matrix(ROWS), reduce_matrix(ROWS // 2)
    e0 = expand_matrix(ROWS // 2)
    row_in, row_low, row_up = [], [], []
    for p in range(4):
        start = min(max(BLOCK * p - 16, 0), ROWS - WIN)
        m = window(r0, 128 * p - 4, MID, start, WIN)
        row_in.append(np.concatenate([m, m], 1))
        m = window(r1, 64 * p - 2, LOW, 128 * p - 4, MID)
        row_low.append(np.concatenate([m, m], 1))
        m = window(e0, BLOCK * p, BLOCK, 128 * p - 4, MID)
        row_up.append(np.concatenate([m, m], 1))
    m = window(e0, SUB, SUB, 28, 48)
    row_sub = np.concatenate([m, m], 1)
    m = window(expand_matrix(ROWS // 4), 124, MID, 62, LOW)
    row_base = np.concatenate([m, m], 1)
    n = 3 * COLS
    c0, c1 = reduce_matrix(n), reduce_matrix(n // 2)
    x0 = expand_matrix(n // 2)
    col_in, col_up = [], []
    for b in range(3):
        full = np.concatenate(
            [
                (x0 @ c0)[COLS * b : COLS * (b + 1)],
                c0[128 * b : 128 * (b + 1)],
                window(c1 @ c0, 64 * b - 1, 67, 0, n),
                window(c0, 128 * b - 1, 1, 0, n),
                window(c0, 128 * (b + 1), 1, 0, n),
                np.zeros((3, n)),
                window(c0, 128 * (b + 1) - 1, 2, 0, n),
                window(c1 @ c0, 64 * (b + 1) - 1, 2, 0, n),
                np.zeros((4, n)),
                window(c0, 128 * b - 1, 2, 0, n),
                window(c1 @ c0, 64 * b - 1, 3, 0, n),
                np.zeros((43, n)),
            ],
            0,
        ).T
        col_in.append(full[COLS * b : COLS * (b + 1)])
        up = x0[COLS * b : COLS * (b + 1)].T
        both = np.zeros((256, COLS))
        both[:128] = up[128 * b : 128 * (b + 1)]
        both[128 + EXT] = window(up, 128 * b - 1, 1, 0, COLS)[0]
        both[128 + EXT + 1] = window(up, 128 * (b + 1), 1, 0, COLS)[0]
        col_up.append(both)
    col_halo = np.zeros((128, 512))
    for lane, i in ((0, -1), (1, 0), (8, 127), (9, 128)):
        col_halo[lane, :COLS] = x0[COLS : 2 * COLS, 128 + i]
        if 0 <= i < 128:
            col_halo[lane, COLS + i] = 1.0
        else:
            col_halo[lane, COLS + 128 + EXT + (i > 0)] = 1.0
    col_halo[1, COLS + 128 + 2] = TAPS[0]
    for lane, i in ((2, -1), (3, 0), (10, 63), (11, 64), (12, 65)):
        col_halo[lane, COLS + 128 + 1 + i] = 1.0
    col_base = np.zeros((128, 256))
    base = expand_matrix(n // 4)
    col_base[:67, :128] = window(base, 128, 128, 63, 67).T
    col_base[:67, 128 + EXT] = window(base, 127, 1, 63, 67)[0]
    col_base[:67, 128 + EXT + 1] = window(base, 256, 1, 63, 67)[0]
    parts = []
    for p in range(4):
        parts += [row_in[p], row_low[p], row_up[p]]
    for b in range(3):
        parts += [col_in[b], col_up[b]]
    parts += [col_base, row_base, row_sub, col_halo]
    return np.concatenate([exact(np.pad(m, ((0, 0), (0, WIDE - m.shape[1])))) for m in parts], 0)


def split(v):
    hi = v.astype(BF)
    lo = (v - hi.astype(F32)).astype(BF)
    return hi, lo


def dot(a, b):
    return jnp.dot(a, b, preferred_element_type=F32)


def tall(v):
    return jnp.concatenate(split(v), 0)


def inverse(v):
    r = pl.reciprocal(v, approx=True)
    return r * (2.0 - v * r)


def weight(d):
    return jnp.exp2(EXPO * inverse(1.0 + d * d))


def kernel(
    count,
    x_ref, const_ref,
    out_ref,
    xwin, xpart, m_row_part, m_row_in, m_row_low, m_row_up, m_row_sub, m_row_base, m_col_in, m_col_halo, m_col_up, m_col_base,
    keep, pack, halo, wide, c1, low, part, part_in,
    level0, level1, late, far0, far1, far_late, jbuf, upper,
    m_sem, x_sem, part_send, part_recv, swap_send, swap_recv, halo_send, halo_recv, far_send, far_recv, group_sem, beside_sem,
):
    me = lax.axis_index("plane")
    q = lax.axis_index("col")
    chip, core = me // 2, me % 2
    far = 2 * (1 - chip) + core
    sibling = 2 * chip + 1 - core
    far_sibling = 2 * (1 - chip) + 1 - core
    side = (q + count - 2) // (count - 1) + q // (count - 1)
    left, right = (q + count - 1) % count, (q + 1) % count
    has_left, has_right = q > 0, q < count - 1
    blocks = (far, me)
    first = 2 * (1 - chip) + 1

    def start_of(p):
        return pl.multiple_of(BLOCK * p - 16 + 16 * ((3 - p) // 3) - 16 * (p // 3), 16)

    def offset_of(p):
        return pl.multiple_of(16 - 16 * ((3 - p) // 3) + 16 * (p // 3), 16)

    own = []
    for b in range(2):
        own.append(
            pltpu.make_async_copy(
                x_ref.at[:, pl.ds(start_of(blocks[b]), WIN)], xwin.at[b, pl.ds(0, 2)], x_sem.at[b]
            )
        )

    def const(at, rows, cols):
        return const_ref.at[pl.ds(pl.multiple_of(at, 16), rows), pl.ds(0, cols)]

    col_at = 4 * ROW_PART + COL_PART * side
    loads = [
        (const(ROW_PART * far, MID, WIDE), m_row_in.at[0]),
        (const(ROW_PART * me, MID, WIDE), m_row_in.at[1]),
        (const(col_at, 256, 512), m_col_in),
        (const(REST + 128 + MID, SUB, 128), m_row_sub),
        (const(ROW_PART * far + MID, LOW, 384), m_row_low.at[0]),
        (const(REST, 128, 256), m_col_base),
        (const(REST + 128, MID, 256), m_row_base),
        (const(REST + 128 + MID + SUB, 128, 512), m_col_halo),
        (const(ROW_PART * me + MID, LOW, 384), m_row_low.at[1]),
        (const(col_at + 256, 256, 256), m_col_up),
        (const(ROW_PART * me + MID + LOW, BLOCK, 384), m_row_up),
        (const(ROW_PART * first, PART, 128), m_row_part),
    ]
    loads = [pltpu.make_async_copy(s, d, m_sem.at[i]) for i, (s, d) in enumerate(loads)]
    early = pltpu.make_async_copy(x_ref.at[:, pl.ds(start_of(first), 128)], xpart, x_sem.at[2])
    early.start()
    loads[11].start()
    loads[2].start()
    loads[3].start()
    own[0].start()
    loads[0].start()

    barrier = pltpu.get_barrier_semaphore()

    def tell(sem, plane, col):
        pl.semaphore_signal(sem, inc=1, device_id=(plane, col), device_id_type=MESH)

    def enter(plane):
        @pl.when(plane != GATE)
        def _():
            tell(barrier, plane, q)

    for plane in (sibling, far, far_sibling):
        enter(plane)

    own[1].start()
    loads[1].start()
    for copy in loads[4:11]:
        copy.start()
    jbuf[pl.ds(KEEP, MID - KEEP)] = jnp.zeros((MID - KEEP, COLS), F32)

    @pl.when(q == 0)
    def _():
        halo[0] = jnp.zeros((MID // 2, 128), F32)

    @pl.when(q == count - 1)
    def _():
        halo[1] = jnp.zeros((MID // 2, 128), F32)

    def twice(ref):
        m = ref[...]
        return jnp.concatenate([m, m], 0)

    early.wait()
    for i in (11, 2, 3):
        loads[i].wait()
    num = jnp.zeros((SUB, COLS), F32)
    den = jnp.zeros((SUB, COLS), F32)
    for p in range(2):
        m = m_row_part[...]
        value = dot(jnp.concatenate([m, m], 1), tall(xpart[p]))
        m = m_col_in[:, pl.ds(0, COLS)]
        value = dot(jnp.concatenate(split(value), 1), jnp.concatenate([m, m], 0))
        z = dot(m_row_sub[:, pl.ds(0, 2 * PART)], tall(value))
        d = xpart[p, pl.ds(offset_of(first), SUB)] - z
        w = weight(d)
        num = num + w * d
        den = den + w
    part[0] = num
    part[1] = den

    @pl.when(me != GATE)
    def _():
        pl.semaphore_wait(barrier, 3)
        tell(group_sem, GATE, q)

    @pl.when(me == GATE)
    def _():
        pl.semaphore_wait(group_sem, 3)

        @pl.when(has_left)
        def _():
            tell(barrier, GATE, left)

        @pl.when(has_right)
        def _():
            tell(barrier, GATE, right)

    def remote(src, dst, send, recv, plane, col):
        return pltpu.make_async_remote_copy(
            src_ref=src, dst_ref=dst, send_sem=send, recv_sem=recv, device_id=(plane, col), device_id_type=MESH
        )

    swaps = []
    for b, p in enumerate((far_sibling, sibling)):
        swaps.append(
            remote(
                x_ref.at[:, pl.ds(start_of(p), WIN)],
                xwin.at[b, pl.ds(2, 2)],
                swap_send.at[b],
                swap_recv.at[b],
                sibling,
                q,
            )
        )
    far_part = remote(part, part_in.at[core], part_send.at[0], part_recv.at[core], first, q)
    swaps[0].start()
    far_part.start()
    swaps[1].start()

    lane = lax.broadcasted_iota(jnp.int32, (MID, 128), 1)
    fold_lane = lax.broadcasted_iota(jnp.int32, (MID // 2, 128), 1)
    half_lane = lax.broadcasted_iota(jnp.int32, (SUB // 2, 128), 1)
    sub_lane = lax.broadcasted_iota(jnp.int32, (SUB, 128), 1)
    low_lane = lax.broadcasted_iota(jnp.int32, (KEEP2, 128), 1)
    keep_lane = lax.broadcasted_iota(jnp.int32, (KEEP, 128), 1)

    def turn(v, by):
        by = by % 128
        return pltpu.roll(v, by, 1) if by else v

    def rows_in(b, p):
        if p == 0:
            own[b].wait()
            loads[b].wait()
        if p == 2:
            swaps[b].wait_recv()
        value = dot(m_row_in[b, :, pl.ds(0, 2 * WIN)], tall(xwin[b, p]))
        value = dot(jnp.concatenate(split(value), 1), twice(m_col_in))
        keep[b, p] = value
        return value

    def put(p, value):
        whi, wlo = split(value[:, :COLS])
        wide[p, 0] = whi
        wide[p, 1] = wlo
        c1[p] = value[:, COLS : COLS + 128]
        low[:, pl.ds(128 * p, 128)] = value[:, COLS + 128 :]

    def sums_zero(b, s):
        num = jnp.zeros((SUB, COLS), F32)
        den = jnp.zeros((SUB, COLS), F32)
        for p in range(4):
            rows = pl.ds(32 * s, 48)
            both = jnp.concatenate([wide[p, 0, rows], wide[p, 1, rows]], 0)
            z = dot(m_row_sub[:, pl.ds(0, 96)], both)
            d = xwin[b, p, pl.ds(pl.multiple_of(offset_of(blocks[b]) + SUB * s, 16), SUB)] - z
            w = weight(d)
            num = num + w * d
            den = den + w
        return num, den

    def columns_up(c2):
        return dot(jnp.concatenate(split(c2), 1), twice(m_col_base))

    def sums_one(b):
        c2 = dot(m_row_low[b, :, pl.ds(0, 2 * MID)], tall(low[...]))
        parts = [c2[:, 128 * p : 128 * p + 128] for p in range(4)]
        u = columns_up(jnp.concatenate(parts, 0))
        u = jnp.concatenate([u[LOW * p : LOW * p + LOW] for p in range(4)], 1)
        base = dot(m_row_base[:, pl.ds(0, 2 * LOW)], tall(u))
        num = jnp.zeros((MID, COLS), F32)
        den = jnp.zeros((MID, COLS), F32)
        for p in range(4):
            d = jnp.concatenate([c1[p], low[:, pl.ds(128 * p, 128)]], 1) - base[:, COLS * p : COLS * p + COLS]
            w = weight(d)
            num = num + w * d
            den = den + w
        return num, den, parts[0] + parts[1] + parts[2] + parts[3]

    def put_one(b, num, den):
        level1[b, 0] = num[:KEEP, :128]
        level1[b, 1] = den[:KEEP, :128]

    def late_tile(num, den, total):
        tile = turn(den[64 : 64 + KEEP2, 128:], 6)
        tile = jnp.where(low_lane < EXT + 6, turn(den[:KEEP2, 128:], 4), tile)
        tile = jnp.where(low_lane < EXT + 4, turn(num[64 : 64 + KEEP2, 128:], 2), tile)
        tile = jnp.where(low_lane < EXT + 2, num[:KEEP2, 128:], tile)
        tile = jnp.where(low_lane < EXT, total[:KEEP2], tile)
        for i, v in enumerate((num, den)):
            for h in range(2):
                at = EDGE + 20 * i + 10 * h
                tile = jnp.where(low_lane >= at, turn(v[64 * h : 64 * h + KEEP2, :128], 4 + at), tile)
        return tile

    far_zero = [remote(level0.at[0, s], far0.at[s], far_send.at[s], far_recv.at[s], far, q) for s in range(SUBS)]
    far_one = remote(level1.at[0], far1, far_send.at[SUBS], far_recv.at[SUBS], far, q)
    far_last = remote(late.at[0], far_late, far_send.at[SUBS + 1], far_recv.at[SUBS + 1], far, q)
    for p in range(4):
        put(p, rows_in(0, p))

    def far_chunk(s):
        num, den = sums_zero(0, s)
        level0[0, s, 0] = num
        level0[0, s, 1] = den

    for s in range(1, SUBS - 1):
        far_chunk(s)
        pl.when(core == 1)(far_zero[s].start)
    for p in range(4):
        rows_in(1, p)
    packs = [jnp.zeros((MID // 2, 128), F32), jnp.zeros((MID // 2, 128), F32)]
    for b in range(2):
        for p in range(4):
            tile = keep[b, p, :, pl.ds(COLS + 128, 128)]
            for h in range(2):
                at = 64 * h + 32 * b + 8 * p
                here = (fold_lane >= at) & (fold_lane < at + 8)
                rows = tile[MID // 2 * h : MID // 2 * (h + 1)]
                packs[0] = jnp.where(here, turn(rows, at - TO_LEFT), packs[0])
                packs[1] = jnp.where(here, turn(rows, at - TO_RIGHT), packs[1])
    pack[0] = packs[0]
    pack[1] = packs[1]

    to_left = remote(pack.at[0], halo.at[1], halo_send.at[0], halo_recv.at[1], me, left)
    to_right = remote(pack.at[1], halo.at[0], halo_send.at[1], halo_recv.at[0], me, right)

    def send_halo():
        @pl.when(me == GATE)
        def _():
            pl.semaphore_wait(barrier, (q + count - 1) // count + (2 * count - 2 - q) // count)
            for plane in (0, 2, 3):
                tell(beside_sem, plane, q)

        @pl.when(me != GATE)
        def _():
            pl.semaphore_wait(beside_sem, 1)

        @pl.when(has_left)
        def _():
            to_left.start()

        @pl.when(has_right)
        def _():
            to_right.start()

    ahead = q % 8 == 0
    pl.when(jnp.logical_not(ahead))(send_halo)

    far_chunk(0)
    for s in range(SUBS - 1):
        pl.when(core == 0)(far_zero[s].start)
    far_chunk(SUBS - 1)
    for copy in loads[4:7]:
        copy.wait()
    num, den, _ = sums_one(0)
    put_one(0, num, den)
    far_one.start()

    pl.when(ahead)(send_halo)
    pl.when(ahead)(far_zero[SUBS - 1].start)

    for copy in loads[7:11]:
        copy.wait()

    @pl.when(has_left)
    def _():
        to_right.wait_recv()

    @pl.when(has_right)
    def _():
        to_left.wait_recv()

    for b in range(2):
        for p in range(4):
            at = 32 * b + 8 * p
            from_left = jnp.concatenate([turn(halo[0], -at), turn(halo[0], -at - 64)], 0)
            from_right = jnp.concatenate([turn(halo[1], 8 - at), turn(halo[1], 8 - at - 64)], 0)
            edge = jnp.where(lane < 8, from_left, jnp.where(lane < 16, from_right, 0.0))
            put(p, keep[b, p] + dot(jnp.concatenate(split(edge), 1), twice(m_col_halo)))

        num, den, total = sums_one(b)
        late[b, pl.ds(0, KEEP2)] = late_tile(num, den, total)
        if b == 1:
            put_one(b, num, den)

        patch = jnp.zeros((SUB // 2, 128), F32)
        for s in range(SUBS):
            num, den = sums_zero(b, s)
            if b == 1:
                level0[1, s, 0] = num
                level0[1, s, 1] = den
                continue
            for i, v in enumerate((num, den)):
                edges = jnp.where(sub_lane < 64, v[:, :128], v[:, 128:])
                for h in range(2):
                    at = 32 * s + 16 * h + 8 * i
                    moved = turn(edges[32 * h : 32 * h + 32], 4 + at)
                    patch = jnp.where((half_lane >= at) & (half_lane < at + 8), moved, patch)
        if b == 0:
            late[0, pl.ds(KEEP2, SUB // 2)] = patch
            far_last.start()
            pl.when(jnp.logical_not(ahead))(far_zero[SUBS - 1].start)

    far_one.wait_recv()
    far_last.wait_recv()
    own_tile, far_tile = late[1, pl.ds(0, KEEP2)], far_late[pl.ds(0, KEEP2)]
    tile = own_tile + far_tile
    total = jnp.concatenate([jnp.where(low_lane < EXT, tile, 0.0), jnp.zeros((LOW - KEEP2, 128), F32)], 0)
    base = dot(m_row_base[:, pl.ds(0, 2 * LOW)], tall(columns_up(total)))
    at_edge = (keep_lane < 6) | (keep_lane >= 124)
    sums = []
    for i in range(2):
        at = EDGE + 20 * i
        edges = jnp.concatenate([turn(far_tile, -(4 + at))[:64], turn(far_tile, -(14 + at))], 0)
        sums.append(level1[1, i] + jnp.where(at_edge, edges, far1[i]))
    jbuf[pl.ds(0, KEEP), pl.ds(0, 128)] = sums[0] * inverse(sums[1]) + base[:KEEP, :128] * 0.125
    outer = (low_lane >= EXT) & (low_lane < EXT + 4)
    ratio = jnp.where(outer, tile, 0.0) * inverse(jnp.where(outer, turn(tile, -4), 1.0))
    ratio = jnp.concatenate([ratio[:64], turn(ratio, -2)], 0) + base[:KEEP, 128:] * 0.125
    ratio = jnp.where((keep_lane >= EXT) & (keep_lane < EXT + 2), ratio, 0.0)
    jbuf[pl.ds(0, KEEP), pl.ds(128, 128)] = ratio
    u = dot(jnp.concatenate(split(jbuf[...]), 1), twice(m_col_up))
    upper[...] = dot(m_row_up[:, pl.ds(0, 2 * MID)], tall(u))

    @pl.when(core == 1)
    def _():
        for i in range(2):
            remote(part, part_in.at[i], part_send.at[0], part_recv.at[i], first, q).wait_recv()
        far0[0] = part_in[0] + part_in[1]

    pl.when(core == 0)(far_zero[0].wait_recv)
    patch = far_late[pl.ds(KEEP2, SUB // 2)]
    for s in range(SUBS):
        if s:
            far_zero[s].wait_recv()
        sums = []
        for i in range(2):
            at = 32 * s + 8 * i
            edges = jnp.concatenate([turn(patch, -(4 + at)), turn(patch, -(20 + at))], 0)
            first = jnp.where(sub_lane < 4, edges, far0[s, i, :, pl.ds(0, 128)])
            second = jnp.where(sub_lane >= 124, edges, far0[s, i, :, pl.ds(128, 128)])
            sums.append(level0[1, s, i] + jnp.concatenate([first, second], 1))
        rows = pl.ds(SUB * s, SUB)
        out_ref[rows] = sums[0] * inverse(sums[1]) + upper[rows]

    @pl.when(has_left)
    def _():
        to_left.wait_send()

    @pl.when(has_right)
    def _():
        to_right.wait_send()

    pl.when(core == 0)(far_zero[0].wait_send)
    for copy in swaps + far_zero[1:] + [far_one, far_last, far_part]:
        copy.wait_send()


def solution(mesh):
    count = mesh.shape["col"]
    consts = matrices()

    def body(x):
        dma = pltpu.SemaphoreType.DMA
        vmem = pltpu.VMEM
        return pl.pallas_call(
            functools.partial(kernel, count),
            out_shape=jax.ShapeDtypeStruct((BLOCK, COLS), F32),
            in_specs=[pl.BlockSpec(memory_space=pl.ANY)] * 2,
            out_specs=pl.BlockSpec(memory_space=pltpu.VMEM),
            scratch_shapes=[
                vmem((2, 4, WIN, COLS), F32),
                vmem((2, 128, COLS), F32),
                vmem((PART, 128), BF),
                vmem((2, MID, WIDE), BF),
                vmem((2, LOW, 384), BF),
                vmem((BLOCK, 384), BF),
                vmem((SUB, 128), BF),
                vmem((MID, 256), BF),
                vmem((256, 512), BF),
                vmem((128, 512), BF),
                vmem((256, 256), BF),
                vmem((128, 256), BF),
                vmem((2, 4, MID, 512), F32),
                vmem((2, MID // 2, 128), F32),
                vmem((2, MID // 2, 128), F32),
                vmem((4, 2, MID, COLS), BF),
                vmem((4, MID, 128), F32),
                vmem((MID, 512), F32),
                vmem((2, SUB, COLS), F32),
                vmem((2, 2, SUB, COLS), F32),
                vmem((2, SUBS, 2, SUB, COLS), F32),
                vmem((2, 2, KEEP, 128), F32),
                vmem((2, LATE, 128), F32),
                vmem((SUBS, 2, SUB, COLS), F32),
                vmem((2, KEEP, 128), F32),
                vmem((LATE, 128), F32),
                vmem((MID, COLS), F32),
                vmem((BLOCK, COLS), F32),
                dma((12,)),
                dma((3,)),
                dma((1,)),
                dma((2,)),
                dma((2,)),
                dma((2,)),
                dma((2,)),
                dma((2,)),
                dma((SUBS + 2,)),
                dma((SUBS + 2,)),
                pltpu.SemaphoreType.REGULAR,
                pltpu.SemaphoreType.REGULAR,
            ],
            compiler_params=pltpu.CompilerParams(
                collective_id=0, has_side_effects=True, vmem_limit_bytes=VMEM_BYTES
            ),
        )(x, consts)

    return jax.shard_map(body, mesh=mesh, in_specs=(P("plane", None, "col"),), out_specs=P("plane", "col"), check_vma=False)
```

```python
import functools

import jax
import jax.numpy as jnp
import ml_dtypes
import numpy as np
from jax import lax
from jax.experimental import pallas as pl
from jax.experimental.pallas import tpu as pltpu
from jax.sharding import PartitionSpec as P

TAPS = np.array([1.0, 4.0, 6.0, 4.0, 1.0]) / 16.0
MESH = pl.DeviceIdType.MESH
BF = jnp.bfloat16
F32 = jnp.float32

ROWS = 1024
BLOCK = 256
COLS = 256
WIN = 288
MID = 144
LOW = 80
KEEP = 136
KEEP2 = 72
SUB = 64
SUBS = BLOCK // SUB
EXT = 67
WIDE = 640
ROW_PART = MID + LOW + BLOCK
COL_PART = 2 * 256
REST = 4 * ROW_PART + 3 * COL_PART
LATE = KEEP2 + SUB // 2
EDGE = 76
VMEM_BYTES = 52 * 1024 * 1024
TO_RIGHT = 72
TO_LEFT = 80
PART = 48
GATE = 1
EXPO = float(-4.0 * np.log2(np.e))


def reduce_matrix(n):
    m = np.zeros((n // 2, n))
    for i in range(n // 2):
        for t in range(5):
            j = 2 * i - 2 + t
            if 0 <= j < n:
                m[i, j] = TAPS[t]
    return m


def expand_matrix(n):
    m = np.zeros((2 * n, n))
    for j in range(2 * n):
        for i in range(max(0, j // 2 - 2), min(n, j // 2 + 3)):
            t = j - 2 * i + 2
            if 0 <= t <= 4:
                m[j, i] = 2.0 * TAPS[t]
    return m


def window(m, row, rows, col, cols):
    out = np.zeros((rows, cols))
    r0, r1 = max(row, 0), min(row + rows, m.shape[0])
    c0, c1 = max(col, 0), min(col + cols, m.shape[1])
    out[r0 - row : r1 - row, c0 - col : c1 - col] = m[r0:r1, c0:c1]
    return out


def exact(m):
    cast = m.astype(ml_dtypes.bfloat16)
    assert (cast.astype(np.float64) == m).all()
    return cast


@functools.lru_cache(None)
def matrices():
    r0, r1 = reduce_matrix(ROWS), reduce_matrix(ROWS // 2)
    e0 = expand_matrix(ROWS // 2)
    row_in, row_low, row_up = [], [], []
    for p in range(4):
        start = min(max(BLOCK * p - 16, 0), ROWS - WIN)
        m = window(r0, 128 * p - 4, MID, start, WIN)
        row_in.append(np.concatenate([m, m], 1))
        m = window(r1, 64 * p - 2, LOW, 128 * p - 4, MID)
        row_low.append(np.concatenate([m, m], 1))
        m = window(e0, BLOCK * p, BLOCK, 128 * p - 4, MID)
        row_up.append(np.concatenate([m, m], 1))
    m = window(e0, SUB, SUB, 28, 48)
    row_sub = np.concatenate([m, m], 1)
    m = window(expand_matrix(ROWS // 4), 124, MID, 62, LOW)
    row_base = np.concatenate([m, m], 1)
    n = 3 * COLS
    c0, c1 = reduce_matrix(n), reduce_matrix(n // 2)
    x0 = expand_matrix(n // 2)
    col_in, col_up = [], []
    for b in range(3):
        full = np.concatenate(
            [
                (x0 @ c0)[COLS * b : COLS * (b + 1)],
                c0[128 * b : 128 * (b + 1)],
                window(c1 @ c0, 64 * b - 1, 67, 0, n),
                window(c0, 128 * b - 1, 1, 0, n),
                window(c0, 128 * (b + 1), 1, 0, n),
                np.zeros((3, n)),
                window(c0, 128 * (b + 1) - 1, 2, 0, n),
                window(c1 @ c0, 64 * (b + 1) - 1, 2, 0, n),
                np.zeros((4, n)),
                window(c0, 128 * b - 1, 2, 0, n),
                window(c1 @ c0, 64 * b - 1, 3, 0, n),
                np.zeros((43, n)),
            ],
            0,
        ).T
        col_in.append(full[COLS * b : COLS * (b + 1)])
        up = x0[COLS * b : COLS * (b + 1)].T
        both = np.zeros((256, COLS))
        both[:128] = up[128 * b : 128 * (b + 1)]
        both[128 + EXT] = window(up, 128 * b - 1, 1, 0, COLS)[0]
        both[128 + EXT + 1] = window(up, 128 * (b + 1), 1, 0, COLS)[0]
        col_up.append(both)
    col_halo = np.zeros((128, 512))
    for lane, i in ((0, -1), (1, 0), (8, 127), (9, 128)):
        col_halo[lane, :COLS] = x0[COLS : 2 * COLS, 128 + i]
        if 0 <= i < 128:
            col_halo[lane, COLS + i] = 1.0
        else:
            col_halo[lane, COLS + 128 + EXT + (i > 0)] = 1.0
    col_halo[1, COLS + 128 + 2] = TAPS[0]
    for lane, i in ((2, -1), (3, 0), (10, 63), (11, 64), (12, 65)):
        col_halo[lane, COLS + 128 + 1 + i] = 1.0
    col_base = np.zeros((128, 256))
    base = expand_matrix(n // 4)
    col_base[:67, :128] = window(base, 128, 128, 63, 67).T
    col_base[:67, 128 + EXT] = window(base, 127, 1, 63, 67)[0]
    col_base[:67, 128 + EXT + 1] = window(base, 256, 1, 63, 67)[0]
    parts = []
    for p in range(4):
        parts += [row_in[p], row_low[p], row_up[p]]
    for b in range(3):
        parts += [col_in[b], col_up[b]]
    parts += [col_base, row_base, row_sub, col_halo]
    return np.concatenate([exact(np.pad(m, ((0, 0), (0, WIDE - m.shape[1])))) for m in parts], 0)


def split(v):
    hi = v.astype(BF)
    lo = (v - hi.astype(F32)).astype(BF)
    return hi, lo


def dot(a, b):
    return jnp.dot(a, b, preferred_element_type=F32)


def tall(v):
    return jnp.concatenate(split(v), 0)


def inverse(v):
    r = pl.reciprocal(v, approx=True)
    return r * (2.0 - v * r)


def weight(d):
    return jnp.exp2(EXPO * inverse(1.0 + d * d))


def kernel(
    count,
    x_ref, const_ref,
    out_ref,
    xwin, xpart, m_row_part, m_row_in, m_row_low, m_row_up, m_row_sub, m_row_base, m_col_in, m_col_halo, m_col_up, m_col_base,
    keep, pack, halo, wide, c1, low, part, part_in,
    level0, level1, late, far0, far1, far_late, jbuf, upper,
    m_sem, x_sem, part_send, part_recv, swap_send, swap_recv, halo_send, halo_recv, far_send, far_recv, group_sem, beside_sem,
):
    me = lax.axis_index("plane")
    q = lax.axis_index("col")
    chip, core = me // 2, me % 2
    far = 2 * (1 - chip) + core
    sibling = 2 * chip + 1 - core
    far_sibling = 2 * (1 - chip) + 1 - core
    side = (q + count - 2) // (count - 1) + q // (count - 1)
    left, right = (q + count - 1) % count, (q + 1) % count
    has_left, has_right = q > 0, q < count - 1
    blocks = (far, me)
    first = 2 * (1 - chip) + 1

    def start_of(p):
        return pl.multiple_of(BLOCK * p - 16 + 16 * ((3 - p) // 3) - 16 * (p // 3), 16)

    def offset_of(p):
        return pl.multiple_of(16 - 16 * ((3 - p) // 3) + 16 * (p // 3), 16)

    own = []
    for b in range(2):
        own.append(
            pltpu.make_async_copy(
                x_ref.at[:, pl.ds(start_of(blocks[b]), WIN)], xwin.at[b, pl.ds(0, 2)], x_sem.at[b]
            )
        )

    def const(at, rows, cols):
        return const_ref.at[pl.ds(pl.multiple_of(at, 16), rows), pl.ds(0, cols)]

    col_at = 4 * ROW_PART + COL_PART * side
    loads = [
        (const(ROW_PART * far, MID, WIDE), m_row_in.at[0]),
        (const(ROW_PART * me, MID, WIDE), m_row_in.at[1]),
        (const(col_at, 256, 512), m_col_in),
        (const(REST + 128 + MID, SUB, 128), m_row_sub),
        (const(ROW_PART * far + MID, LOW, 384), m_row_low.at[0]),
        (const(REST, 128, 256), m_col_base),
        (const(REST + 128, MID, 256), m_row_base),
        (const(REST + 128 + MID + SUB, 128, 512), m_col_halo),
        (const(ROW_PART * me + MID, LOW, 384), m_row_low.at[1]),
        (const(col_at + 256, 256, 256), m_col_up),
        (const(ROW_PART * me + MID + LOW, BLOCK, 384), m_row_up),
        (const(ROW_PART * first, PART, 128), m_row_part),
    ]
    loads = [pltpu.make_async_copy(s, d, m_sem.at[i]) for i, (s, d) in enumerate(loads)]
    early = pltpu.make_async_copy(x_ref.at[:, pl.ds(start_of(first), 128)], xpart, x_sem.at[2])
    early.start()
    loads[11].start()
    loads[2].start()
    loads[3].start()
    own[0].start()
    loads[0].start()

    barrier = pltpu.get_barrier_semaphore()

    def tell(sem, plane, col):
        pl.semaphore_signal(sem, inc=1, device_id=(plane, col), device_id_type=MESH)

    def enter(plane):
        @pl.when(plane != GATE)
        def _():
            tell(barrier, plane, q)

    for plane in (sibling, far, far_sibling):
        enter(plane)

    own[1].start()
    loads[1].start()
    for copy in loads[4:11]:
        copy.start()
    jbuf[pl.ds(KEEP, MID - KEEP)] = jnp.zeros((MID - KEEP, COLS), F32)

    @pl.when(q == 0)
    def _():
        halo[0] = jnp.zeros((MID // 2, 128), F32)

    @pl.when(q == count - 1)
    def _():
        halo[1] = jnp.zeros((MID // 2, 128), F32)

    def twice(ref):
        m = ref[...]
        return jnp.concatenate([m, m], 0)

    @pl.when(me != GATE)
    def _():
        pl.semaphore_wait(barrier, 3)
        tell(group_sem, GATE, q)

    @pl.when(me == GATE)
    def _():
        pl.semaphore_wait(group_sem, 3)

        @pl.when(has_left)
        def _():
            tell(barrier, GATE, left)

        @pl.when(has_right)
        def _():
            tell(barrier, GATE, right)

    def remote(src, dst, send, recv, plane, col):
        return pltpu.make_async_remote_copy(
            src_ref=src, dst_ref=dst, send_sem=send, recv_sem=recv, device_id=(plane, col), device_id_type=MESH
        )

    swaps = []
    for b, p in enumerate((far_sibling, sibling)):
        swaps.append(
            remote(
                x_ref.at[:, pl.ds(start_of(p), WIN)],
                xwin.at[b, pl.ds(2, 2)],
                swap_send.at[b],
                swap_recv.at[b],
                sibling,
                q,
            )
        )
    for copy in swaps:
        copy.start()

    early.wait()
    for i in (11, 2, 3):
        loads[i].wait()
    num = jnp.zeros((SUB, COLS), F32)
    den = jnp.zeros((SUB, COLS), F32)
    for p in range(2):
        m = m_row_part[...]
        value = dot(jnp.concatenate([m, m], 1), tall(xpart[p]))
        m = m_col_in[:, pl.ds(0, COLS)]
        value = dot(jnp.concatenate(split(value), 1), jnp.concatenate([m, m], 0))
        z = dot(m_row_sub[:, pl.ds(0, 2 * PART)], tall(value))
        d = xpart[p, pl.ds(offset_of(first), SUB)] - z
        w = weight(d)
        num = num + w * d
        den = den + w
    part[0] = num
    part[1] = den

    far_part = remote(part, part_in.at[core], part_send.at[0], part_recv.at[core], first, q)
    far_part.start()

    lane = lax.broadcasted_iota(jnp.int32, (MID, 128), 1)
    fold_lane = lax.broadcasted_iota(jnp.int32, (MID // 2, 128), 1)
    half_lane = lax.broadcasted_iota(jnp.int32, (SUB // 2, 128), 1)
    sub_lane = lax.broadcasted_iota(jnp.int32, (SUB, 128), 1)
    low_lane = lax.broadcasted_iota(jnp.int32, (KEEP2, 128), 1)
    keep_lane = lax.broadcasted_iota(jnp.int32, (KEEP, 128), 1)

    def turn(v, by):
        by = by % 128
        return pltpu.roll(v, by, 1) if by else v

    ahead = q % 8 == 0

    def meet():
        @pl.when(me == GATE)
        def _():
            pl.semaphore_wait(barrier, (q + count - 1) // count + (2 * count - 2 - q) // count)
            for plane in (0, 2, 3):
                tell(beside_sem, plane, q)

    def rows_in(b, p):
        if p == 0:
            own[b].wait()
            loads[b].wait()
        if p == 2:
            swaps[b].wait_recv()
        value = dot(m_row_in[b, :, pl.ds(0, 2 * WIN)], tall(xwin[b, p]))
        value = dot(jnp.concatenate(split(value), 1), twice(m_col_in))
        keep[b, p] = value
        return value

    def put(p, value):
        whi, wlo = split(value[:, :COLS])
        wide[p, 0] = whi
        wide[p, 1] = wlo
        c1[p] = value[:, COLS : COLS + 128]
        low[:, pl.ds(128 * p, 128)] = value[:, COLS + 128 :]

    def sums_zero(b, s):
        num = jnp.zeros((SUB, COLS), F32)
        den = jnp.zeros((SUB, COLS), F32)
        for p in range(4):
            rows = pl.ds(32 * s, 48)
            both = jnp.concatenate([wide[p, 0, rows], wide[p, 1, rows]], 0)
            z = dot(m_row_sub[:, pl.ds(0, 96)], both)
            d = xwin[b, p, pl.ds(pl.multiple_of(offset_of(blocks[b]) + SUB * s, 16), SUB)] - z
            w = weight(d)
            num = num + w * d
            den = den + w
        return num, den

    def columns_up(c2):
        return dot(jnp.concatenate(split(c2), 1), twice(m_col_base))

    def sums_one(b):
        c2 = dot(m_row_low[b, :, pl.ds(0, 2 * MID)], tall(low[...]))
        parts = [c2[:, 128 * p : 128 * p + 128] for p in range(4)]
        u = columns_up(jnp.concatenate(parts, 0))
        u = jnp.concatenate([u[LOW * p : LOW * p + LOW] for p in range(4)], 1)
        base = dot(m_row_base[:, pl.ds(0, 2 * LOW)], tall(u))
        num = jnp.zeros((MID, COLS), F32)
        den = jnp.zeros((MID, COLS), F32)
        for p in range(4):
            d = jnp.concatenate([c1[p], low[:, pl.ds(128 * p, 128)]], 1) - base[:, COLS * p : COLS * p + COLS]
            w = weight(d)
            num = num + w * d
            den = den + w
        return num, den, parts[0] + parts[1] + parts[2] + parts[3]

    def put_one(b, num, den):
        level1[b, 0] = num[:KEEP, :128]
        level1[b, 1] = den[:KEEP, :128]

    def late_tile(num, den, total):
        tile = turn(den[64 : 64 + KEEP2, 128:], 6)
        tile = jnp.where(low_lane < EXT + 6, turn(den[:KEEP2, 128:], 4), tile)
        tile = jnp.where(low_lane < EXT + 4, turn(num[64 : 64 + KEEP2, 128:], 2), tile)
        tile = jnp.where(low_lane < EXT + 2, num[:KEEP2, 128:], tile)
        tile = jnp.where(low_lane < EXT, total[:KEEP2], tile)
        for i, v in enumerate((num, den)):
            for h in range(2):
                at = EDGE + 20 * i + 10 * h
                tile = jnp.where(low_lane >= at, turn(v[64 * h : 64 * h + KEEP2, :128], 4 + at), tile)
        return tile

    far_zero = [remote(level0.at[0, s], far0.at[s], far_send.at[s], far_recv.at[s], far, q) for s in range(SUBS)]
    far_one = remote(level1.at[0], far1, far_send.at[SUBS], far_recv.at[SUBS], far, q)
    far_last = remote(late.at[0], far_late, far_send.at[SUBS + 1], far_recv.at[SUBS + 1], far, q)
    for p in range(4):
        if p == 2:
            pl.when(jnp.logical_not(ahead))(meet)
        put(p, rows_in(0, p))

    def far_chunk(s):
        num, den = sums_zero(0, s)
        level0[0, s, 0] = num
        level0[0, s, 1] = den

    for s in range(1, SUBS - 1):
        far_chunk(s)
        pl.when(core == 1)(far_zero[s].start)
    for p in range(4):
        rows_in(1, p)
    packs = [jnp.zeros((MID // 2, 128), F32), jnp.zeros((MID // 2, 128), F32)]
    for b in range(2):
        for p in range(4):
            tile = keep[b, p, :, pl.ds(COLS + 128, 128)]
            for h in range(2):
                at = 64 * h + 32 * b + 8 * p
                here = (fold_lane >= at) & (fold_lane < at + 8)
                rows = tile[MID // 2 * h : MID // 2 * (h + 1)]
                packs[0] = jnp.where(here, turn(rows, at - TO_LEFT), packs[0])
                packs[1] = jnp.where(here, turn(rows, at - TO_RIGHT), packs[1])
    pack[0] = packs[0]
    pack[1] = packs[1]

    to_left = remote(pack.at[0], halo.at[1], halo_send.at[0], halo_recv.at[1], me, left)
    to_right = remote(pack.at[1], halo.at[0], halo_send.at[1], halo_recv.at[0], me, right)

    def send_halo():
        @pl.when(me != GATE)
        def _():
            pl.semaphore_wait(beside_sem, 1)

        @pl.when(has_left)
        def _():
            to_left.start()

        @pl.when(has_right)
        def _():
            to_right.start()

    pl.when(jnp.logical_not(ahead))(send_halo)

    far_chunk(0)
    for s in range(SUBS - 1):
        pl.when(core == 0)(far_zero[s].start)
    far_chunk(SUBS - 1)
    for copy in loads[4:7]:
        copy.wait()
    num, den, _ = sums_one(0)
    put_one(0, num, den)
    far_one.start()

    pl.when(ahead)(meet)
    pl.when(ahead)(send_halo)
    pl.when(ahead)(far_zero[SUBS - 1].start)

    for copy in loads[7:11]:
        copy.wait()

    @pl.when(has_left)
    def _():
        to_right.wait_recv()

    @pl.when(has_right)
    def _():
        to_left.wait_recv()

    for b in range(2):
        for p in range(4):
            at = 32 * b + 8 * p
            from_left = jnp.concatenate([turn(halo[0], -at), turn(halo[0], -at - 64)], 0)
            from_right = jnp.concatenate([turn(halo[1], 8 - at), turn(halo[1], 8 - at - 64)], 0)
            edge = jnp.where(lane < 8, from_left, jnp.where(lane < 16, from_right, 0.0))
            put(p, keep[b, p] + dot(jnp.concatenate(split(edge), 1), twice(m_col_halo)))

        num, den, total = sums_one(b)
        late[b, pl.ds(0, KEEP2)] = late_tile(num, den, total)
        if b == 1:
            put_one(b, num, den)

        patch = jnp.zeros((SUB // 2, 128), F32)
        for s in range(SUBS):
            num, den = sums_zero(b, s)
            if b == 1:
                level0[1, s, 0] = num
                level0[1, s, 1] = den
                continue
            for i, v in enumerate((num, den)):
                edges = jnp.where(sub_lane < 64, v[:, :128], v[:, 128:])
                for h in range(2):
                    at = 32 * s + 16 * h + 8 * i
                    moved = turn(edges[32 * h : 32 * h + 32], 4 + at)
                    patch = jnp.where((half_lane >= at) & (half_lane < at + 8), moved, patch)
        if b == 0:
            late[0, pl.ds(KEEP2, SUB // 2)] = patch
            far_last.start()
            pl.when(jnp.logical_not(ahead))(far_zero[SUBS - 1].start)

    far_one.wait_recv()
    far_last.wait_recv()
    own_tile, far_tile = late[1, pl.ds(0, KEEP2)], far_late[pl.ds(0, KEEP2)]
    tile = own_tile + far_tile
    total = jnp.concatenate([jnp.where(low_lane < EXT, tile, 0.0), jnp.zeros((LOW - KEEP2, 128), F32)], 0)
    base = dot(m_row_base[:, pl.ds(0, 2 * LOW)], tall(columns_up(total)))
    at_edge = (keep_lane < 6) | (keep_lane >= 124)
    sums = []
    for i in range(2):
        at = EDGE + 20 * i
        edges = jnp.concatenate([turn(far_tile, -(4 + at))[:64], turn(far_tile, -(14 + at))], 0)
        sums.append(level1[1, i] + jnp.where(at_edge, edges, far1[i]))
    jbuf[pl.ds(0, KEEP), pl.ds(0, 128)] = sums[0] * inverse(sums[1]) + base[:KEEP, :128] * 0.125
    outer = (low_lane >= EXT) & (low_lane < EXT + 4)
    ratio = jnp.where(outer, tile, 0.0) * inverse(jnp.where(outer, turn(tile, -4), 1.0))
    ratio = jnp.concatenate([ratio[:64], turn(ratio, -2)], 0) + base[:KEEP, 128:] * 0.125
    ratio = jnp.where((keep_lane >= EXT) & (keep_lane < EXT + 2), ratio, 0.0)
    jbuf[pl.ds(0, KEEP), pl.ds(128, 128)] = ratio
    u = dot(jnp.concatenate(split(jbuf[...]), 1), twice(m_col_up))
    upper[...] = dot(m_row_up[:, pl.ds(0, 2 * MID)], tall(u))

    @pl.when(core == 1)
    def _():
        for i in range(2):
            remote(part, part_in.at[i], part_send.at[0], part_recv.at[i], first, q).wait_recv()
        far0[0] = part_in[0] + part_in[1]

    pl.when(core == 0)(far_zero[0].wait_recv)
    patch = far_late[pl.ds(KEEP2, SUB // 2)]
    for s in range(SUBS):
        if s:
            far_zero[s].wait_recv()
        sums = []
        for i in range(2):
            at = 32 * s + 8 * i
            edges = jnp.concatenate([turn(patch, -(4 + at)), turn(patch, -(20 + at))], 0)
            first = jnp.where(sub_lane < 4, edges, far0[s, i, :, pl.ds(0, 128)])
            second = jnp.where(sub_lane >= 124, edges, far0[s, i, :, pl.ds(128, 128)])
            sums.append(level0[1, s, i] + jnp.concatenate([first, second], 1))
        rows = pl.ds(SUB * s, SUB)
        out_ref[rows] = sums[0] * inverse(sums[1]) + upper[rows]

    @pl.when(has_left)
    def _():
        to_left.wait_send()

    @pl.when(has_right)
    def _():
        to_right.wait_send()

    pl.when(core == 0)(far_zero[0].wait_send)
    for copy in swaps + far_zero[1:] + [far_one, far_last, far_part]:
        copy.wait_send()


def solution(mesh):
    count = mesh.shape["col"]
    consts = matrices()

    def body(x):
        dma = pltpu.SemaphoreType.DMA
        vmem = pltpu.VMEM
        return pl.pallas_call(
            functools.partial(kernel, count),
            out_shape=jax.ShapeDtypeStruct((BLOCK, COLS), F32),
            in_specs=[pl.BlockSpec(memory_space=pl.ANY)] * 2,
            out_specs=pl.BlockSpec(memory_space=pltpu.VMEM),
            scratch_shapes=[
                vmem((2, 4, WIN, COLS), F32),
                vmem((2, 128, COLS), F32),
                vmem((PART, 128), BF),
                vmem((2, MID, WIDE), BF),
                vmem((2, LOW, 384), BF),
                vmem((BLOCK, 384), BF),
                vmem((SUB, 128), BF),
                vmem((MID, 256), BF),
                vmem((256, 512), BF),
                vmem((128, 512), BF),
                vmem((256, 256), BF),
                vmem((128, 256), BF),
                vmem((2, 4, MID, 512), F32),
                vmem((2, MID // 2, 128), F32),
                vmem((2, MID // 2, 128), F32),
                vmem((4, 2, MID, COLS), BF),
                vmem((4, MID, 128), F32),
                vmem((MID, 512), F32),
                vmem((2, SUB, COLS), F32),
                vmem((2, 2, SUB, COLS), F32),
                vmem((2, SUBS, 2, SUB, COLS), F32),
                vmem((2, 2, KEEP, 128), F32),
                vmem((2, LATE, 128), F32),
                vmem((SUBS, 2, SUB, COLS), F32),
                vmem((2, KEEP, 128), F32),
                vmem((LATE, 128), F32),
                vmem((MID, COLS), F32),
                vmem((BLOCK, COLS), F32),
                dma((12,)),
                dma((3,)),
                dma((1,)),
                dma((2,)),
                dma((2,)),
                dma((2,)),
                dma((2,)),
                dma((2,)),
                dma((SUBS + 2,)),
                dma((SUBS + 2,)),
                pltpu.SemaphoreType.REGULAR,
                pltpu.SemaphoreType.REGULAR,
            ],
            compiler_params=pltpu.CompilerParams(
                collective_id=0, has_side_effects=True, vmem_limit_bytes=VMEM_BYTES
            ),
        )(x, consts)

    return jax.shard_map(body, mesh=mesh, in_specs=(P("plane", None, "col"),), out_specs=P("plane", "col"), check_vma=False)
```

```python
import functools

import jax
import jax.numpy as jnp
import ml_dtypes
import numpy as np
from jax import lax
from jax.experimental import pallas as pl
from jax.experimental.pallas import tpu as pltpu
from jax.sharding import PartitionSpec as P

TAPS = np.array([1.0, 4.0, 6.0, 4.0, 1.0]) / 16.0
MESH = pl.DeviceIdType.MESH
BF = jnp.bfloat16
F32 = jnp.float32

ROWS = 1024
BLOCK = 256
COLS = 256
WIN = 288
MID = 144
LOW = 80
KEEP = 136
KEEP2 = 72
SUB = 64
SUBS = BLOCK // SUB
EXT = 67
WIDE = 640
ROW_PART = MID + LOW + BLOCK
COL_PART = 2 * 256
REST = 4 * ROW_PART + 3 * COL_PART
LATE = KEEP2 + SUB // 2
EDGE = 76
VMEM_BYTES = 52 * 1024 * 1024
TO_RIGHT = 72
TO_LEFT = 80
PART = 48
OWN = 48
GATE = 1
EXPO = float(-4.0 * np.log2(np.e))


def reduce_matrix(n):
    m = np.zeros((n // 2, n))
    for i in range(n // 2):
        for t in range(5):
            j = 2 * i - 2 + t
            if 0 <= j < n:
                m[i, j] = TAPS[t]
    return m


def expand_matrix(n):
    m = np.zeros((2 * n, n))
    for j in range(2 * n):
        for i in range(max(0, j // 2 - 2), min(n, j // 2 + 3)):
            t = j - 2 * i + 2
            if 0 <= t <= 4:
                m[j, i] = 2.0 * TAPS[t]
    return m


def window(m, row, rows, col, cols):
    out = np.zeros((rows, cols))
    r0, r1 = max(row, 0), min(row + rows, m.shape[0])
    c0, c1 = max(col, 0), min(col + cols, m.shape[1])
    out[r0 - row : r1 - row, c0 - col : c1 - col] = m[r0:r1, c0:c1]
    return out


def exact(m):
    cast = m.astype(ml_dtypes.bfloat16)
    assert (cast.astype(np.float64) == m).all()
    return cast


@functools.lru_cache(None)
def matrices():
    r0, r1 = reduce_matrix(ROWS), reduce_matrix(ROWS // 2)
    e0 = expand_matrix(ROWS // 2)
    row_in, row_low, row_up = [], [], []
    for p in range(4):
        start = min(max(BLOCK * p - 16, 0), ROWS - WIN)
        m = window(r0, 128 * p - 4, MID, start, WIN)
        row_in.append(np.concatenate([m, m], 1))
        m = window(r1, 64 * p - 2, LOW, 128 * p - 4, MID)
        row_low.append(np.concatenate([m, m], 1))
        m = window(e0, BLOCK * p, BLOCK, 128 * p - 4, MID)
        row_up.append(np.concatenate([m, m], 1))
    m = window(e0, SUB, SUB, 28, 48)
    row_sub = np.concatenate([m, m], 1)
    m = window(expand_matrix(ROWS // 4), 124, MID, 62, LOW)
    row_base = np.concatenate([m, m], 1)
    n = 3 * COLS
    c0, c1 = reduce_matrix(n), reduce_matrix(n // 2)
    x0 = expand_matrix(n // 2)
    col_in, col_up = [], []
    for b in range(3):
        full = np.concatenate(
            [
                (x0 @ c0)[COLS * b : COLS * (b + 1)],
                c0[128 * b : 128 * (b + 1)],
                window(c1 @ c0, 64 * b - 1, 67, 0, n),
                window(c0, 128 * b - 1, 1, 0, n),
                window(c0, 128 * (b + 1), 1, 0, n),
                np.zeros((3, n)),
                window(c0, 128 * (b + 1) - 1, 2, 0, n),
                window(c1 @ c0, 64 * (b + 1) - 1, 2, 0, n),
                np.zeros((4, n)),
                window(c0, 128 * b - 1, 2, 0, n),
                window(c1 @ c0, 64 * b - 1, 3, 0, n),
                np.zeros((43, n)),
            ],
            0,
        ).T
        col_in.append(full[COLS * b : COLS * (b + 1)])
        up = x0[COLS * b : COLS * (b + 1)].T
        both = np.zeros((256, COLS))
        both[:128] = up[128 * b : 128 * (b + 1)]
        both[128 + EXT] = window(up, 128 * b - 1, 1, 0, COLS)[0]
        both[128 + EXT + 1] = window(up, 128 * (b + 1), 1, 0, COLS)[0]
        col_up.append(both)
    col_halo = np.zeros((128, 512))
    for lane, i in ((0, -1), (1, 0), (8, 127), (9, 128)):
        col_halo[lane, :COLS] = x0[COLS : 2 * COLS, 128 + i]
        if 0 <= i < 128:
            col_halo[lane, COLS + i] = 1.0
        else:
            col_halo[lane, COLS + 128 + EXT + (i > 0)] = 1.0
    col_halo[1, COLS + 128 + 2] = TAPS[0]
    for lane, i in ((2, -1), (3, 0), (10, 63), (11, 64), (12, 65)):
        col_halo[lane, COLS + 128 + 1 + i] = 1.0
    col_base = np.zeros((128, 256))
    base = expand_matrix(n // 4)
    col_base[:67, :128] = window(base, 128, 128, 63, 67).T
    col_base[:67, 128 + EXT] = window(base, 127, 1, 63, 67)[0]
    col_base[:67, 128 + EXT + 1] = window(base, 256, 1, 63, 67)[0]
    parts = []
    for p in range(4):
        parts += [row_in[p], row_low[p], row_up[p]]
    for b in range(3):
        parts += [col_in[b], col_up[b]]
    parts += [col_base, row_base, row_sub, col_halo]
    return np.concatenate([exact(np.pad(m, ((0, 0), (0, WIDE - m.shape[1])))) for m in parts], 0)


def split(v):
    hi = v.astype(BF)
    lo = (v - hi.astype(F32)).astype(BF)
    return hi, lo


def dot(a, b):
    return jnp.dot(a, b, preferred_element_type=F32)


def tall(v):
    return jnp.concatenate(split(v), 0)


def inverse(v):
    r = pl.reciprocal(v, approx=True)
    return r * (2.0 - v * r)


def weight(d):
    return jnp.exp2(EXPO * inverse(1.0 + d * d))


def kernel(
    count,
    x_ref, const_ref,
    out_ref,
    xwin, xpart, m_row_part, m_row_in, m_row_low, m_row_up, m_row_sub, m_row_base, m_col_in, m_col_halo, m_col_up, m_col_base,
    keep, pack, halo, wide, c1, low, part, part_in,
    level0, level1, late, far0, far1, far_late, jbuf, upper,
    m_sem, x_sem, part_send, part_recv, swap_send, swap_recv, halo_send, halo_recv, far_send, far_recv, group_sem, beside_sem,
):
    me = lax.axis_index("plane")
    q = lax.axis_index("col")
    chip, core = me // 2, me % 2
    far = 2 * (1 - chip) + core
    sibling = 2 * chip + 1 - core
    far_sibling = 2 * (1 - chip) + 1 - core
    side = (q + count - 2) // (count - 1) + q // (count - 1)
    left, right = (q + count - 1) % count, (q + 1) % count
    has_left, has_right = q > 0, q < count - 1
    blocks = (far, me)
    first = 2 * (1 - chip) + 1

    def start_of(p):
        return pl.multiple_of(BLOCK * p - 16 + 16 * ((3 - p) // 3) - 16 * (p // 3), 16)

    def offset_of(p):
        return pl.multiple_of(16 - 16 * ((3 - p) // 3) + 16 * (p // 3), 16)

    own = []
    for b in range(2):
        own.append(
            pltpu.make_async_copy(
                x_ref.at[:, pl.ds(start_of(blocks[b]), WIN)], xwin.at[b, pl.ds(0, 2)], x_sem.at[b]
            )
        )

    def const(at, rows, cols):
        return const_ref.at[pl.ds(pl.multiple_of(at, 16), rows), pl.ds(0, cols)]

    col_at = 4 * ROW_PART + COL_PART * side
    loads = [
        (const(ROW_PART * far, MID, WIDE), m_row_in.at[0]),
        (const(ROW_PART * me, MID, WIDE), m_row_in.at[1]),
        (const(col_at, 256, 512), m_col_in),
        (const(REST + 128 + MID, SUB, 128), m_row_sub),
        (const(ROW_PART * far + MID, LOW, 384), m_row_low.at[0]),
        (const(REST, 128, 256), m_col_base),
        (const(REST + 128, MID, 256), m_row_base),
        (const(REST + 128 + MID + SUB, 128, 512), m_col_halo),
        (const(ROW_PART * me + MID, LOW, 384), m_row_low.at[1]),
        (const(col_at + 256, 256, 256), m_col_up),
        (const(ROW_PART * me + MID + LOW, BLOCK, 384), m_row_up),
        (const(ROW_PART * first, PART, 128), m_row_part),
    ]
    loads = [pltpu.make_async_copy(s, d, m_sem.at[i]) for i, (s, d) in enumerate(loads)]
    early = pltpu.make_async_copy(x_ref.at[:, pl.ds(start_of(first), 128)], xpart, x_sem.at[2])
    early.start()
    loads[11].start()
    loads[2].start()
    loads[3].start()
    own[0].start()
    loads[0].start()

    barrier = pltpu.get_barrier_semaphore()

    def tell(sem, plane, col):
        pl.semaphore_signal(sem, inc=1, device_id=(plane, col), device_id_type=MESH)

    def enter(plane):
        @pl.when(plane != GATE)
        def _():
            tell(barrier, plane, q)

    for plane in (sibling, far, far_sibling):
        enter(plane)

    own[1].start()
    loads[1].start()
    for copy in loads[4:11]:
        copy.start()
    jbuf[pl.ds(KEEP, MID - KEEP)] = jnp.zeros((MID - KEEP, COLS), F32)

    @pl.when(q == 0)
    def _():
        halo[0] = jnp.zeros((MID // 2, 128), F32)

    @pl.when(q == count - 1)
    def _():
        halo[1] = jnp.zeros((MID // 2, 128), F32)

    def twice(ref):
        m = ref[...]
        return jnp.concatenate([m, m], 0)

    @pl.when(me != GATE)
    def _():
        pl.semaphore_wait(barrier, 3)
        tell(group_sem, GATE, q)

    @pl.when(me == GATE)
    def _():
        pl.semaphore_wait(group_sem, 3)

        @pl.when(has_left)
        def _():
            tell(barrier, GATE, left)

        @pl.when(has_right)
        def _():
            tell(barrier, GATE, right)

    def remote(src, dst, send, recv, plane, col):
        return pltpu.make_async_remote_copy(
            src_ref=src, dst_ref=dst, send_sem=send, recv_sem=recv, device_id=(plane, col), device_id_type=MESH
        )

    swaps = []
    for b, p in enumerate((far_sibling, sibling)):
        swaps.append(
            remote(
                x_ref.at[:, pl.ds(start_of(p), WIN)],
                xwin.at[b, pl.ds(2, 2)],
                swap_send.at[b],
                swap_recv.at[b],
                sibling,
                q,
            )
        )
    swaps[0].start()

    early.wait()
    for i in (11, 2, 3):
        loads[i].wait()
    num = jnp.zeros((OWN, COLS), F32)
    den = jnp.zeros((OWN, COLS), F32)
    for p in range(2):
        m = m_row_part[...]
        value = dot(jnp.concatenate([m, m], 1), tall(xpart[p]))
        m = m_col_in[:, pl.ds(0, COLS)]
        value = dot(jnp.concatenate(split(value), 1), jnp.concatenate([m, m], 0))
        z = dot(m_row_sub[pl.ds(0, OWN), pl.ds(0, 2 * PART)], tall(value))
        d = xpart[p, pl.ds(offset_of(first), OWN)] - z
        w = weight(d)
        num = num + w * d
        den = den + w
    part[0] = num
    part[1] = den

    far_part = remote(part, part_in.at[core], part_send.at[0], part_recv.at[core], first, q)
    far_part.start()
    swaps[1].start()

    lane = lax.broadcasted_iota(jnp.int32, (MID, 128), 1)
    fold_lane = lax.broadcasted_iota(jnp.int32, (MID // 2, 128), 1)
    half_lane = lax.broadcasted_iota(jnp.int32, (SUB // 2, 128), 1)
    sub_lane = lax.broadcasted_iota(jnp.int32, (SUB, 128), 1)
    low_lane = lax.broadcasted_iota(jnp.int32, (KEEP2, 128), 1)
    keep_lane = lax.broadcasted_iota(jnp.int32, (KEEP, 128), 1)

    def turn(v, by):
        by = by % 128
        return pltpu.roll(v, by, 1) if by else v

    ahead = (q % 8 == 0) & has_left

    def meet():
        @pl.when(me == GATE)
        def _():
            pl.semaphore_wait(barrier, (q + count - 1) // count + (2 * count - 2 - q) // count)
            for plane in (0, 2, 3):
                tell(beside_sem, plane, q)

    def rows_in(b, p):
        if p == 0:
            own[b].wait()
            loads[b].wait()
        if p == 2:
            swaps[b].wait_recv()
        value = dot(m_row_in[b, :, pl.ds(0, 2 * WIN)], tall(xwin[b, p]))
        value = dot(jnp.concatenate(split(value), 1), twice(m_col_in))
        keep[b, p] = value
        return value

    def put(p, value):
        whi, wlo = split(value[:, :COLS])
        wide[p, 0] = whi
        wide[p, 1] = wlo
        c1[p] = value[:, COLS : COLS + 128]
        low[:, pl.ds(128 * p, 128)] = value[:, COLS + 128 :]

    def sums_zero(b, s):
        num = jnp.zeros((SUB, COLS), F32)
        den = jnp.zeros((SUB, COLS), F32)
        for p in range(4):
            rows = pl.ds(32 * s, 48)
            both = jnp.concatenate([wide[p, 0, rows], wide[p, 1, rows]], 0)
            z = dot(m_row_sub[:, pl.ds(0, 96)], both)
            d = xwin[b, p, pl.ds(pl.multiple_of(offset_of(blocks[b]) + SUB * s, 16), SUB)] - z
            w = weight(d)
            num = num + w * d
            den = den + w
        return num, den

    def columns_up(c2):
        return dot(jnp.concatenate(split(c2), 1), twice(m_col_base))

    def sums_one(b):
        c2 = dot(m_row_low[b, :, pl.ds(0, 2 * MID)], tall(low[...]))
        parts = [c2[:, 128 * p : 128 * p + 128] for p in range(4)]
        u = columns_up(jnp.concatenate(parts, 0))
        u = jnp.concatenate([u[LOW * p : LOW * p + LOW] for p in range(4)], 1)
        base = dot(m_row_base[:, pl.ds(0, 2 * LOW)], tall(u))
        num = jnp.zeros((MID, COLS), F32)
        den = jnp.zeros((MID, COLS), F32)
        for p in range(4):
            d = jnp.concatenate([c1[p], low[:, pl.ds(128 * p, 128)]], 1) - base[:, COLS * p : COLS * p + COLS]
            w = weight(d)
            num = num + w * d
            den = den + w
        return num, den, parts[0] + parts[1] + parts[2] + parts[3]

    def put_one(b, num, den):
        level1[b, 0] = num[:KEEP, :128]
        level1[b, 1] = den[:KEEP, :128]

    def late_tile(num, den, total):
        tile = turn(den[64 : 64 + KEEP2, 128:], 6)
        tile = jnp.where(low_lane < EXT + 6, turn(den[:KEEP2, 128:], 4), tile)
        tile = jnp.where(low_lane < EXT + 4, turn(num[64 : 64 + KEEP2, 128:], 2), tile)
        tile = jnp.where(low_lane < EXT + 2, num[:KEEP2, 128:], tile)
        tile = jnp.where(low_lane < EXT, total[:KEEP2], tile)
        for i, v in enumerate((num, den)):
            for h in range(2):
                at = EDGE + 20 * i + 10 * h
                tile = jnp.where(low_lane >= at, turn(v[64 * h : 64 * h + KEEP2, :128], 4 + at), tile)
        return tile

    far_zero = [remote(level0.at[0, s], far0.at[s], far_send.at[s], far_recv.at[s], far, q) for s in range(SUBS)]
    rest = pl.ds(OWN, SUB - OWN)
    far_rest = remote(level0.at[0, 0, :, rest], far0.at[0, :, rest], far_send.at[0], far_recv.at[0], far, q)
    far_one = remote(level1.at[0], far1, far_send.at[SUBS], far_recv.at[SUBS], far, q)
    far_last = remote(late.at[0], far_late, far_send.at[SUBS + 1], far_recv.at[SUBS + 1], far, q)
    for p in range(4):
        if p == 2:
            pl.when(jnp.logical_not(ahead))(meet)
        put(p, rows_in(0, p))

    def far_chunk(s):
        num, den = sums_zero(0, s)
        level0[0, s, 0] = num
        level0[0, s, 1] = den

    for s in range(1, SUBS - 1):
        far_chunk(s)
        pl.when(core == 1)(far_zero[s].start)
    far_chunk(0)
    pl.when(core == 1)(far_rest.start)
    for p in range(4):
        rows_in(1, p)
    packs = [jnp.zeros((MID // 2, 128), F32), jnp.zeros((MID // 2, 128), F32)]
    for b in range(2):
        for p in range(4):
            tile = keep[b, p, :, pl.ds(COLS + 128, 128)]
            for h in range(2):
                at = 64 * h + 32 * b + 8 * p
                here = (fold_lane >= at) & (fold_lane < at + 8)
                rows = tile[MID // 2 * h : MID // 2 * (h + 1)]
                packs[0] = jnp.where(here, turn(rows, at - TO_LEFT), packs[0])
                packs[1] = jnp.where(here, turn(rows, at - TO_RIGHT), packs[1])
    pack[0] = packs[0]
    pack[1] = packs[1]

    to_left = remote(pack.at[0], halo.at[1], halo_send.at[0], halo_recv.at[1], me, left)
    to_right = remote(pack.at[1], halo.at[0], halo_send.at[1], halo_recv.at[0], me, right)

    def send_halo():
        @pl.when(me != GATE)
        def _():
            pl.semaphore_wait(beside_sem, 1)

        @pl.when(has_left)
        def _():
            to_left.start()

        @pl.when(has_right)
        def _():
            to_right.start()

    pl.when(jnp.logical_not(ahead))(send_halo)

    for s in range(SUBS - 1):
        pl.when(core == 0)(far_zero[s].start)
    far_chunk(SUBS - 1)
    for copy in loads[4:7]:
        copy.wait()
    num, den, _ = sums_one(0)
    put_one(0, num, den)
    far_one.start()

    pl.when(ahead)(meet)
    pl.when(ahead)(send_halo)

    for copy in loads[7:11]:
        copy.wait()

    @pl.when(has_left)
    def _():
        to_right.wait_recv()

    @pl.when(has_right)
    def _():
        to_left.wait_recv()

    for b in range(2):
        for p in range(4):
            at = 32 * b + 8 * p
            from_left = jnp.concatenate([turn(halo[0], -at), turn(halo[0], -at - 64)], 0)
            from_right = jnp.concatenate([turn(halo[1], 8 - at), turn(halo[1], 8 - at - 64)], 0)
            edge = jnp.where(lane < 8, from_left, jnp.where(lane < 16, from_right, 0.0))
            put(p, keep[b, p] + dot(jnp.concatenate(split(edge), 1), twice(m_col_halo)))

        num, den, total = sums_one(b)
        late[b, pl.ds(0, KEEP2)] = late_tile(num, den, total)
        if b == 1:
            put_one(b, num, den)

        patch = jnp.zeros((SUB // 2, 128), F32)
        for s in range(SUBS):
            num, den = sums_zero(b, s)
            if b == 1:
                level0[1, s, 0] = num
                level0[1, s, 1] = den
                continue
            for i, v in enumerate((num, den)):
                edges = jnp.where(sub_lane < 64, v[:, :128], v[:, 128:])
                for h in range(2):
                    at = 32 * s + 16 * h + 8 * i
                    moved = turn(edges[32 * h : 32 * h + 32], 4 + at)
                    patch = jnp.where((half_lane >= at) & (half_lane < at + 8), moved, patch)
        if b == 0:
            late[0, pl.ds(KEEP2, SUB // 2)] = patch
            far_last.start()
            far_zero[SUBS - 1].start()

    far_one.wait_recv()
    far_last.wait_recv()
    own_tile, far_tile = late[1, pl.ds(0, KEEP2)], far_late[pl.ds(0, KEEP2)]
    tile = own_tile + far_tile
    total = jnp.concatenate([jnp.where(low_lane < EXT, tile, 0.0), jnp.zeros((LOW - KEEP2, 128), F32)], 0)
    base = dot(m_row_base[:, pl.ds(0, 2 * LOW)], tall(columns_up(total)))
    at_edge = (keep_lane < 6) | (keep_lane >= 124)
    sums = []
    for i in range(2):
        at = EDGE + 20 * i
        edges = jnp.concatenate([turn(far_tile, -(4 + at))[:64], turn(far_tile, -(14 + at))], 0)
        sums.append(level1[1, i] + jnp.where(at_edge, edges, far1[i]))
    jbuf[pl.ds(0, KEEP), pl.ds(0, 128)] = sums[0] * inverse(sums[1]) + base[:KEEP, :128] * 0.125
    outer = (low_lane >= EXT) & (low_lane < EXT + 4)
    ratio = jnp.where(outer, tile, 0.0) * inverse(jnp.where(outer, turn(tile, -4), 1.0))
    ratio = jnp.concatenate([ratio[:64], turn(ratio, -2)], 0) + base[:KEEP, 128:] * 0.125
    ratio = jnp.where((keep_lane >= EXT) & (keep_lane < EXT + 2), ratio, 0.0)
    jbuf[pl.ds(0, KEEP), pl.ds(128, 128)] = ratio
    u = dot(jnp.concatenate(split(jbuf[...]), 1), twice(m_col_up))
    upper[...] = dot(m_row_up[:, pl.ds(0, 2 * MID)], tall(u))

    @pl.when(core == 1)
    def _():
        for i in range(2):
            remote(part, part_in.at[i], part_send.at[0], part_recv.at[i], first, q).wait_recv()
        far_rest.wait_recv()
        far0[0, :, pl.ds(0, OWN)] = part_in[0] + part_in[1]

    pl.when(core == 0)(far_zero[0].wait_recv)
    patch = far_late[pl.ds(KEEP2, SUB // 2)]
    for s in range(SUBS):
        if s:
            far_zero[s].wait_recv()
        sums = []
        for i in range(2):
            at = 32 * s + 8 * i
            edges = jnp.concatenate([turn(patch, -(4 + at)), turn(patch, -(20 + at))], 0)
            first = jnp.where(sub_lane < 4, edges, far0[s, i, :, pl.ds(0, 128)])
            second = jnp.where(sub_lane >= 124, edges, far0[s, i, :, pl.ds(128, 128)])
            sums.append(level0[1, s, i] + jnp.concatenate([first, second], 1))
        rows = pl.ds(SUB * s, SUB)
        out_ref[rows] = sums[0] * inverse(sums[1]) + upper[rows]

    @pl.when(has_left)
    def _():
        to_left.wait_send()

    @pl.when(has_right)
    def _():
        to_right.wait_send()

    pl.when(core == 0)(far_zero[0].wait_send)
    pl.when(core == 1)(far_rest.wait_send)
    for copy in swaps + far_zero[1:] + [far_one, far_last, far_part]:
        copy.wait_send()


def solution(mesh):
    count = mesh.shape["col"]
    consts = matrices()

    def body(x):
        dma = pltpu.SemaphoreType.DMA
        vmem = pltpu.VMEM
        return pl.pallas_call(
            functools.partial(kernel, count),
            out_shape=jax.ShapeDtypeStruct((BLOCK, COLS), F32),
            in_specs=[pl.BlockSpec(memory_space=pl.ANY)] * 2,
            out_specs=pl.BlockSpec(memory_space=pltpu.VMEM),
            scratch_shapes=[
                vmem((2, 4, WIN, COLS), F32),
                vmem((2, 128, COLS), F32),
                vmem((PART, 128), BF),
                vmem((2, MID, WIDE), BF),
                vmem((2, LOW, 384), BF),
                vmem((BLOCK, 384), BF),
                vmem((SUB, 128), BF),
                vmem((MID, 256), BF),
                vmem((256, 512), BF),
                vmem((128, 512), BF),
                vmem((256, 256), BF),
                vmem((128, 256), BF),
                vmem((2, 4, MID, 512), F32),
                vmem((2, MID // 2, 128), F32),
                vmem((2, MID // 2, 128), F32),
                vmem((4, 2, MID, COLS), BF),
                vmem((4, MID, 128), F32),
                vmem((MID, 512), F32),
                vmem((2, OWN, COLS), F32),
                vmem((2, 2, OWN, COLS), F32),
                vmem((2, SUBS, 2, SUB, COLS), F32),
                vmem((2, 2, KEEP, 128), F32),
                vmem((2, LATE, 128), F32),
                vmem((SUBS, 2, SUB, COLS), F32),
                vmem((2, KEEP, 128), F32),
                vmem((LATE, 128), F32),
                vmem((MID, COLS), F32),
                vmem((BLOCK, COLS), F32),
                dma((12,)),
                dma((3,)),
                dma((1,)),
                dma((2,)),
                dma((2,)),
                dma((2,)),
                dma((2,)),
                dma((2,)),
                dma((SUBS + 2,)),
                dma((SUBS + 2,)),
                pltpu.SemaphoreType.REGULAR,
                pltpu.SemaphoreType.REGULAR,
            ],
            compiler_params=pltpu.CompilerParams(
                collective_id=0, has_side_effects=True, vmem_limit_bytes=VMEM_BYTES
            ),
        )(x, consts)

    return jax.shard_map(body, mesh=mesh, in_specs=(P("plane", None, "col"),), out_specs=P("plane", "col"), check_vma=False)
```

```python
import functools

import jax
import jax.numpy as jnp
import ml_dtypes
import numpy as np
from jax import lax
from jax.experimental import pallas as pl
from jax.experimental.pallas import tpu as pltpu
from jax.sharding import PartitionSpec as P

TAPS = np.array([1.0, 4.0, 6.0, 4.0, 1.0]) / 16.0
MESH = pl.DeviceIdType.MESH
BF = jnp.bfloat16
F32 = jnp.float32

ROWS = 1024
BLOCK = 256
COLS = 256
WIN = 288
MID = 144
LOW = 80
KEEP = 136
KEEP2 = 72
SUB = 64
SUBS = BLOCK // SUB
EXT = 67
WIDE = 640
ROW_PART = MID + LOW + BLOCK
COL_PART = 2 * 256
REST = 4 * ROW_PART + 3 * COL_PART
LATE = KEEP2 + SUB // 2
EDGE = 76
VMEM_BYTES = 52 * 1024 * 1024
TO_RIGHT = 72
TO_LEFT = 80
PART = 48
OWN = 48
GATE = 1
EXPO = float(-4.0 * np.log2(np.e))


def reduce_matrix(n):
    m = np.zeros((n // 2, n))
    for i in range(n // 2):
        for t in range(5):
            j = 2 * i - 2 + t
            if 0 <= j < n:
                m[i, j] = TAPS[t]
    return m


def expand_matrix(n):
    m = np.zeros((2 * n, n))
    for j in range(2 * n):
        for i in range(max(0, j // 2 - 2), min(n, j // 2 + 3)):
            t = j - 2 * i + 2
            if 0 <= t <= 4:
                m[j, i] = 2.0 * TAPS[t]
    return m


def window(m, row, rows, col, cols):
    out = np.zeros((rows, cols))
    r0, r1 = max(row, 0), min(row + rows, m.shape[0])
    c0, c1 = max(col, 0), min(col + cols, m.shape[1])
    out[r0 - row : r1 - row, c0 - col : c1 - col] = m[r0:r1, c0:c1]
    return out


def exact(m):
    cast = m.astype(ml_dtypes.bfloat16)
    assert (cast.astype(np.float64) == m).all()
    return cast


@functools.lru_cache(None)
def matrices():
    r0, r1 = reduce_matrix(ROWS), reduce_matrix(ROWS // 2)
    e0 = expand_matrix(ROWS // 2)
    row_in, row_low, row_up = [], [], []
    for p in range(4):
        start = min(max(BLOCK * p - 16, 0), ROWS - WIN)
        m = window(r0, 128 * p - 4, MID, start, WIN)
        row_in.append(np.concatenate([m, m], 1))
        m = window(r1, 64 * p - 2, LOW, 128 * p - 4, MID)
        row_low.append(np.concatenate([m, m], 1))
        m = window(e0, BLOCK * p, BLOCK, 128 * p - 4, MID)
        row_up.append(np.concatenate([m, m], 1))
    m = window(e0, SUB, SUB, 28, 48)
    row_sub = np.concatenate([m, m], 1)
    m = window(expand_matrix(ROWS // 4), 124, MID, 62, LOW)
    row_base = np.concatenate([m, m], 1)
    n = 3 * COLS
    c0, c1 = reduce_matrix(n), reduce_matrix(n // 2)
    x0 = expand_matrix(n // 2)
    col_in, col_up = [], []
    for b in range(3):
        full = np.concatenate(
            [
                (x0 @ c0)[COLS * b : COLS * (b + 1)],
                c0[128 * b : 128 * (b + 1)],
                window(c1 @ c0, 64 * b - 1, 67, 0, n),
                window(c0, 128 * b - 1, 1, 0, n),
                window(c0, 128 * (b + 1), 1, 0, n),
                np.zeros((3, n)),
                window(c0, 128 * (b + 1) - 1, 2, 0, n),
                window(c1 @ c0, 64 * (b + 1) - 1, 2, 0, n),
                np.zeros((4, n)),
                window(c0, 128 * b - 1, 2, 0, n),
                window(c1 @ c0, 64 * b - 1, 3, 0, n),
                np.zeros((43, n)),
            ],
            0,
        ).T
        col_in.append(full[COLS * b : COLS * (b + 1)])
        up = x0[COLS * b : COLS * (b + 1)].T
        both = np.zeros((256, COLS))
        both[:128] = up[128 * b : 128 * (b + 1)]
        both[128 + EXT] = window(up, 128 * b - 1, 1, 0, COLS)[0]
        both[128 + EXT + 1] = window(up, 128 * (b + 1), 1, 0, COLS)[0]
        col_up.append(both)
    col_halo = np.zeros((128, 512))
    for lane, i in ((0, -1), (1, 0), (8, 127), (9, 128)):
        col_halo[lane, :COLS] = x0[COLS : 2 * COLS, 128 + i]
        if 0 <= i < 128:
            col_halo[lane, COLS + i] = 1.0
        else:
            col_halo[lane, COLS + 128 + EXT + (i > 0)] = 1.0
    col_halo[1, COLS + 128 + 2] = TAPS[0]
    for lane, i in ((2, -1), (3, 0), (10, 63), (11, 64), (12, 65)):
        col_halo[lane, COLS + 128 + 1 + i] = 1.0
    col_base = np.zeros((128, 256))
    base = expand_matrix(n // 4)
    col_base[:67, :128] = window(base, 128, 128, 63, 67).T
    col_base[:67, 128 + EXT] = window(base, 127, 1, 63, 67)[0]
    col_base[:67, 128 + EXT + 1] = window(base, 256, 1, 63, 67)[0]
    parts = []
    for p in range(4):
        parts += [row_in[p], row_low[p], row_up[p]]
    for b in range(3):
        parts += [col_in[b], col_up[b]]
    parts += [col_base, row_base, row_sub, col_halo]
    return np.concatenate([exact(np.pad(m, ((0, 0), (0, WIDE - m.shape[1])))) for m in parts], 0)


def split(v):
    hi = v.astype(BF)
    lo = (v - hi.astype(F32)).astype(BF)
    return hi, lo


def dot(a, b):
    return jnp.dot(a, b, preferred_element_type=F32)


def tall(v):
    return jnp.concatenate(split(v), 0)


def inverse(v):
    r = pl.reciprocal(v, approx=True)
    return r * (2.0 - v * r)


def weight(d):
    return jnp.exp2(EXPO * inverse(1.0 + d * d))


def kernel(
    count,
    x_ref, const_ref,
    out_ref,
    xwin, xpart, m_row_part, m_row_in, m_row_low, m_row_up, m_row_sub, m_row_base, m_col_in, m_col_halo, m_col_up, m_col_base,
    keep, pack, halo, wide, c1, low, part, part_in,
    level0, level1, late, far0, far1, far_late, jbuf, upper,
    m_sem, x_sem, part_send, part_recv, swap_send, swap_recv, halo_send, halo_recv, far_send, far_recv, group_sem, sibling_sem, far_sem, beside_sem,
):
    me = lax.axis_index("plane")
    q = lax.axis_index("col")
    chip, core = me // 2, me % 2
    far = 2 * (1 - chip) + core
    sibling = 2 * chip + 1 - core
    far_sibling = 2 * (1 - chip) + 1 - core
    side = (q + count - 2) // (count - 1) + q // (count - 1)
    left, right = (q + count - 1) % count, (q + 1) % count
    has_left, has_right = q > 0, q < count - 1
    blocks = (far, me)
    first = 2 * (1 - chip) + 1

    barrier = pltpu.get_barrier_semaphore()

    def tell(sem, plane, col):
        pl.semaphore_signal(sem, inc=1, device_id=(plane, col), device_id_type=MESH)

    @pl.when(me == GATE)
    def _():
        for plane in (0, 2, 3):
            tell(barrier, plane, q)

    @pl.when((me == 0) | (me == 3))
    def _():
        tell(barrier, 2, q)

    def start_of(p):
        return pl.multiple_of(BLOCK * p - 16 + 16 * ((3 - p) // 3) - 16 * (p // 3), 16)

    def offset_of(p):
        return pl.multiple_of(16 - 16 * ((3 - p) // 3) + 16 * (p // 3), 16)

    own = []
    for b in range(2):
        own.append(
            pltpu.make_async_copy(
                x_ref.at[:, pl.ds(start_of(blocks[b]), WIN)], xwin.at[b, pl.ds(0, 2)], x_sem.at[b]
            )
        )

    def const(at, rows, cols):
        return const_ref.at[pl.ds(pl.multiple_of(at, 16), rows), pl.ds(0, cols)]

    col_at = 4 * ROW_PART + COL_PART * side
    loads = [
        (const(ROW_PART * far, MID, WIDE), m_row_in.at[0]),
        (const(ROW_PART * me, MID, WIDE), m_row_in.at[1]),
        (const(col_at, 256, 512), m_col_in),
        (const(REST + 128 + MID, SUB, 128), m_row_sub),
        (const(ROW_PART * far + MID, LOW, 384), m_row_low.at[0]),
        (const(REST, 128, 256), m_col_base),
        (const(REST + 128, MID, 256), m_row_base),
        (const(REST + 128 + MID + SUB, 128, 512), m_col_halo),
        (const(ROW_PART * me + MID, LOW, 384), m_row_low.at[1]),
        (const(col_at + 256, 256, 256), m_col_up),
        (const(ROW_PART * me + MID + LOW, BLOCK, 384), m_row_up),
        (const(ROW_PART * first, PART, 128), m_row_part),
    ]
    loads = [pltpu.make_async_copy(s, d, m_sem.at[i]) for i, (s, d) in enumerate(loads)]
    early = pltpu.make_async_copy(x_ref.at[:, pl.ds(start_of(first), 128)], xpart, x_sem.at[2])
    early.start()
    loads[11].start()
    loads[2].start()
    loads[3].start()
    own[0].start()
    loads[0].start()

    def twice(ref):
        m = ref[...]
        return jnp.concatenate([m, m], 0)

    @pl.when((me == 0) | (me == 3))
    def _():
        pl.semaphore_wait(barrier, 1)

    @pl.when(me == 2)
    def _():
        pl.semaphore_wait(barrier, 3)
        tell(sibling_sem, 3, q)
        tell(far_sem, 0, q)
        tell(group_sem, GATE, q)

    @pl.when(me == 0)
    def _():
        tell(sibling_sem, GATE, q)

    @pl.when(me == 3)
    def _():
        tell(far_sem, GATE, q)

    def remote(src, dst, send, recv, plane, col):
        return pltpu.make_async_remote_copy(
            src_ref=src, dst_ref=dst, send_sem=send, recv_sem=recv, device_id=(plane, col), device_id_type=MESH
        )

    swaps = []
    for b, p in enumerate((far_sibling, sibling)):
        swaps.append(
            remote(
                x_ref.at[:, pl.ds(start_of(p), WIN)],
                xwin.at[b, pl.ds(2, 2)],
                swap_send.at[b],
                swap_recv.at[b],
                sibling,
                q,
            )
        )
    @pl.when(core == 1)
    def _():
        pl.semaphore_wait(sibling_sem, 1)

    swaps[0].start()

    own[1].start()
    loads[1].start()
    for copy in loads[4:11]:
        copy.start()
    jbuf[pl.ds(KEEP, MID - KEEP)] = jnp.zeros((MID - KEEP, COLS), F32)

    @pl.when(q == 0)
    def _():
        halo[0] = jnp.zeros((MID // 3, 128), F32)

    @pl.when(q == count - 1)
    def _():
        halo[1] = jnp.zeros((MID // 3, 128), F32)

    early.wait()
    for i in (11, 2, 3):
        loads[i].wait()
    num = jnp.zeros((OWN, COLS), F32)
    den = jnp.zeros((OWN, COLS), F32)
    for p in range(2):
        m = m_row_part[...]
        value = dot(jnp.concatenate([m, m], 1), tall(xpart[p]))
        m = m_col_in[:, pl.ds(0, COLS)]
        value = dot(jnp.concatenate(split(value), 0), m)
        value = value[:PART] + value[PART:]
        z = dot(m_row_sub[pl.ds(0, OWN), pl.ds(0, 2 * PART)], tall(value))
        d = xpart[p, pl.ds(offset_of(first), OWN)] - z
        w = weight(d)
        num = num + w * d
        den = den + w
    part[0] = num
    part[1] = den

    far_part = remote(part, part_in.at[core], part_send.at[0], part_recv.at[core], first, q)

    @pl.when(chip == 0)
    def _():
        pl.semaphore_wait(far_sem, 1)

    far_part.start()
    swaps[1].start()

    @pl.when(me == GATE)
    def _():
        pl.semaphore_wait(group_sem, 1)

        @pl.when(has_left)
        def _():
            tell(barrier, GATE, left)

        @pl.when(has_right)
        def _():
            tell(barrier, GATE, right)

    lane = lax.broadcasted_iota(jnp.int32, (MID, 128), 1)
    fold_lane = lax.broadcasted_iota(jnp.int32, (MID // 3, 128), 1)
    half_lane = lax.broadcasted_iota(jnp.int32, (SUB // 2, 128), 1)
    sub_lane = lax.broadcasted_iota(jnp.int32, (SUB, 128), 1)
    low_lane = lax.broadcasted_iota(jnp.int32, (KEEP2, 128), 1)
    keep_lane = lax.broadcasted_iota(jnp.int32, (KEEP, 128), 1)

    def turn(v, by):
        by = by % 128
        return pltpu.roll(v, by, 1) if by else v

    ahead = (q % 8 == 0) & has_left
    behind = (q % (count // 2) == 0) & has_left

    def meet():
        @pl.when(me == GATE)
        def _():
            pl.semaphore_wait(barrier, (q + count - 1) // count + (2 * count - 2 - q) // count)
            for plane in (0, 2, 3):
                tell(beside_sem, plane, q)

    def rows_in(b, p):
        if p == 0:
            own[b].wait()
            loads[b].wait()
        if p == 2:
            swaps[b].wait_recv()
        return dot(m_row_in[b, :, pl.ds(0, 2 * WIN)], tall(xwin[b, p]))

    def columns_in(b, planes):
        halves = []
        for p in planes:
            halves += split(rows_in(b, p))
        value = dot(jnp.concatenate(halves, 0), m_col_in[...])
        for i, p in enumerate(planes):
            keep[b, p] = value[2 * MID * i : 2 * MID * i + MID] + value[2 * MID * i + MID : 2 * MID * (i + 1)]

    def put(p, value):
        whi, wlo = split(value[:, :COLS])
        wide[p, 0] = whi
        wide[p, 1] = wlo
        c1[p] = value[:, COLS : COLS + 128]
        low[:, pl.ds(128 * p, 128)] = value[:, COLS + 128 :]

    def sums_zero(b, s):
        num = jnp.zeros((SUB, COLS), F32)
        den = jnp.zeros((SUB, COLS), F32)
        for p in range(4):
            rows = pl.ds(32 * s, 48)
            both = jnp.concatenate([wide[p, 0, rows], wide[p, 1, rows]], 0)
            z = dot(m_row_sub[:, pl.ds(0, 96)], both)
            d = xwin[b, p, pl.ds(pl.multiple_of(offset_of(blocks[b]) + SUB * s, 16), SUB)] - z
            w = weight(d)
            num = num + w * d
            den = den + w
        return num, den

    def columns_up(c2):
        return dot(jnp.concatenate(split(c2), 1), twice(m_col_base))

    def sums_one(b):
        c2 = dot(m_row_low[b, :, pl.ds(0, 2 * MID)], tall(low[...]))
        parts = [c2[:, 128 * p : 128 * p + 128] for p in range(4)]
        u = columns_up(jnp.concatenate(parts, 0))
        u = jnp.concatenate([u[LOW * p : LOW * p + LOW] for p in range(4)], 1)
        base = dot(m_row_base[:, pl.ds(0, 2 * LOW)], tall(u))
        num = jnp.zeros((MID, COLS), F32)
        den = jnp.zeros((MID, COLS), F32)
        for p in range(4):
            d = jnp.concatenate([c1[p], low[:, pl.ds(128 * p, 128)]], 1) - base[:, COLS * p : COLS * p + COLS]
            w = weight(d)
            num = num + w * d
            den = den + w
        return num, den, parts[0] + parts[1] + parts[2] + parts[3]

    def put_one(b, num, den):
        level1[b, 0] = num[:KEEP, :128]
        level1[b, 1] = den[:KEEP, :128]

    def late_tile(num, den, total):
        tile = turn(den[64 : 64 + KEEP2, 128:], 6)
        tile = jnp.where(low_lane < EXT + 6, turn(den[:KEEP2, 128:], 4), tile)
        tile = jnp.where(low_lane < EXT + 4, turn(num[64 : 64 + KEEP2, 128:], 2), tile)
        tile = jnp.where(low_lane < EXT + 2, num[:KEEP2, 128:], tile)
        tile = jnp.where(low_lane < EXT, total[:KEEP2], tile)
        for i, v in enumerate((num, den)):
            for h in range(2):
                at = EDGE + 20 * i + 10 * h
                tile = jnp.where(low_lane >= at, turn(v[64 * h : 64 * h + KEEP2, :128], 4 + at), tile)
        return tile

    far_zero = [remote(level0.at[0, s], far0.at[s], far_send.at[s], far_recv.at[s], far, q) for s in range(SUBS)]
    rest = pl.ds(OWN, SUB - OWN)
    far_rest = remote(level0.at[0, 0, :, rest], far0.at[0, :, rest], far_send.at[0], far_recv.at[0], far, q)
    far_one = remote(level1.at[0], far1, far_send.at[SUBS], far_recv.at[SUBS], far, q)
    far_last = remote(late.at[0], far_late, far_send.at[SUBS + 1], far_recv.at[SUBS + 1], far, q)
    columns_in(0, (0, 1))
    put(0, keep[0, 0])
    put(1, keep[0, 1])
    columns_in(1, (0, 1))
    columns_in(0, (2, 3))
    put(2, keep[0, 2])
    put(3, keep[0, 3])

    def far_chunk(s):
        num, den = sums_zero(0, s)
        level0[0, s, 0] = num
        level0[0, s, 1] = den

    for s in range(1, SUBS - 1):
        far_chunk(s)
        pl.when(core == 1)(far_zero[s].start)
    far_chunk(0)
    pl.when(core == 1)(far_rest.start)
    pl.when(jnp.logical_not(ahead))(meet)
    columns_in(1, (2, 3))
    packs = [jnp.zeros((MID // 3, 128), F32), jnp.zeros((MID // 3, 128), F32)]
    for b in range(2):
        for p in range(4):
            tile = keep[b, p, :, pl.ds(COLS + 128, 128)]
            for h in range(3):
                at = 40 * h + 20 * b + 5 * p
                here = (fold_lane >= at) & (fold_lane < at + 5)
                rows = tile[MID // 3 * h : MID // 3 * (h + 1)]
                packs[0] = jnp.where(here, turn(rows, at - TO_LEFT), packs[0])
                packs[1] = jnp.where(here, turn(rows, at - TO_RIGHT), packs[1])
    pack[0] = packs[0]
    pack[1] = packs[1]

    to_left = remote(pack.at[0], halo.at[1], halo_send.at[0], halo_recv.at[1], me, left)
    to_right = remote(pack.at[1], halo.at[0], halo_send.at[1], halo_recv.at[0], me, right)

    def send_halo():
        @pl.when(me != GATE)
        def _():
            pl.semaphore_wait(beside_sem, 1)

        @pl.when(has_left)
        def _():
            to_left.start()

        @pl.when(has_right)
        def _():
            to_right.start()

    pl.when(jnp.logical_not(ahead))(send_halo)

    for s in range(SUBS - 1):
        pl.when(core == 0)(far_zero[s].start)
    far_chunk(SUBS - 1)
    for copy in loads[4:7]:
        copy.wait()
    num, den, _ = sums_one(0)
    put_one(0, num, den)
    far_one.start()

    pl.when(ahead)(meet)
    pl.when(ahead)(send_halo)

    pl.when(behind)(far_zero[SUBS - 1].start)
    for copy in loads[7:11]:
        copy.wait()

    @pl.when(has_left)
    def _():
        to_right.wait_recv()

    @pl.when(has_right)
    def _():
        to_left.wait_recv()

    for b in range(2):
        edges = []
        for p in range(4):
            at = 20 * b + 5 * p
            from_left = jnp.concatenate([turn(halo[0], -at - 40 * h) for h in range(3)], 0)
            from_right = jnp.concatenate([turn(halo[1], 8 - at - 40 * h) for h in range(3)], 0)
            edge = jnp.where((lane >= 8) & (lane < 13), from_right, jnp.where(lane < 5, from_left, 0.0))
            edges.append(jnp.concatenate(split(edge), 1))
        added = dot(jnp.concatenate(edges, 0), twice(m_col_halo))
        for p in range(4):
            put(p, keep[b, p] + added[MID * p : MID * (p + 1)])

        num, den, total = sums_one(b)
        late[b, pl.ds(0, KEEP2)] = late_tile(num, den, total)
        if b == 1:
            put_one(b, num, den)

        patch = jnp.zeros((SUB // 2, 128), F32)
        for s in range(SUBS):
            num, den = sums_zero(b, s)
            if b == 1:
                level0[1, s, 0] = num
                level0[1, s, 1] = den
                continue
            for i, v in enumerate((num, den)):
                edges = jnp.where(sub_lane < 64, v[:, :128], v[:, 128:])
                for h in range(2):
                    at = 32 * s + 16 * h + 8 * i
                    moved = turn(edges[32 * h : 32 * h + 32], 4 + at)
                    patch = jnp.where((half_lane >= at) & (half_lane < at + 8), moved, patch)
        if b == 0:
            late[0, pl.ds(KEEP2, SUB // 2)] = patch
            far_last.start()
            pl.when(jnp.logical_not(behind))(far_zero[SUBS - 1].start)

    far_one.wait_recv()
    far_last.wait_recv()
    own_tile, far_tile = late[1, pl.ds(0, KEEP2)], far_late[pl.ds(0, KEEP2)]
    tile = own_tile + far_tile
    total = jnp.concatenate([jnp.where(low_lane < EXT, tile, 0.0), jnp.zeros((LOW - KEEP2, 128), F32)], 0)
    base = dot(m_row_base[:, pl.ds(0, 2 * LOW)], tall(columns_up(total)))
    at_edge = (keep_lane < 6) | (keep_lane >= 124)
    sums = []
    for i in range(2):
        at = EDGE + 20 * i
        edges = jnp.concatenate([turn(far_tile, -(4 + at))[:64], turn(far_tile, -(14 + at))], 0)
        sums.append(level1[1, i] + jnp.where(at_edge, edges, far1[i]))
    jbuf[pl.ds(0, KEEP), pl.ds(0, 128)] = sums[0] * inverse(sums[1]) + base[:KEEP, :128] * 0.125
    outer = (low_lane >= EXT) & (low_lane < EXT + 4)
    ratio = jnp.where(outer, tile, 0.0) * inverse(jnp.where(outer, turn(tile, -4), 1.0))
    ratio = jnp.concatenate([ratio[:64], turn(ratio, -2)], 0) + base[:KEEP, 128:] * 0.125
    ratio = jnp.where((keep_lane >= EXT) & (keep_lane < EXT + 2), ratio, 0.0)
    jbuf[pl.ds(0, KEEP), pl.ds(128, 128)] = ratio
    u = dot(jnp.concatenate(split(jbuf[...]), 1), twice(m_col_up))
    upper[...] = dot(m_row_up[:, pl.ds(0, 2 * MID)], tall(u))

    @pl.when(core == 1)
    def _():
        for i in range(2):
            remote(part, part_in.at[i], part_send.at[0], part_recv.at[i], first, q).wait_recv()
        far_rest.wait_recv()
        far0[0, :, pl.ds(0, OWN)] = part_in[0] + part_in[1]

    pl.when(core == 0)(far_zero[0].wait_recv)
    patch = far_late[pl.ds(KEEP2, SUB // 2)]
    for s in range(SUBS):
        if s:
            far_zero[s].wait_recv()
        sums = []
        for i in range(2):
            at = 32 * s + 8 * i
            edges = jnp.concatenate([turn(patch, -(4 + at)), turn(patch, -(20 + at))], 0)
            first = jnp.where(sub_lane < 4, edges, far0[s, i, :, pl.ds(0, 128)])
            second = jnp.where(sub_lane >= 124, edges, far0[s, i, :, pl.ds(128, 128)])
            sums.append(level0[1, s, i] + jnp.concatenate([first, second], 1))
        rows = pl.ds(SUB * s, SUB)
        out_ref[rows] = sums[0] * inverse(sums[1]) + upper[rows]

    @pl.when(has_left)
    def _():
        to_left.wait_send()

    @pl.when(has_right)
    def _():
        to_right.wait_send()

    pl.when(core == 0)(far_zero[0].wait_send)
    pl.when(core == 1)(far_rest.wait_send)
    for copy in swaps + far_zero[1:] + [far_one, far_last, far_part]:
        copy.wait_send()


def solution(mesh):
    count = mesh.shape["col"]
    consts = matrices()

    def body(x):
        dma = pltpu.SemaphoreType.DMA
        vmem = pltpu.VMEM
        return pl.pallas_call(
            functools.partial(kernel, count),
            out_shape=jax.ShapeDtypeStruct((BLOCK, COLS), F32),
            in_specs=[pl.BlockSpec(memory_space=pl.ANY)] * 2,
            out_specs=pl.BlockSpec(memory_space=pltpu.VMEM),
            scratch_shapes=[
                vmem((2, 4, WIN, COLS), F32),
                vmem((2, 128, COLS), F32),
                vmem((PART, 128), BF),
                vmem((2, MID, WIDE), BF),
                vmem((2, LOW, 384), BF),
                vmem((BLOCK, 384), BF),
                vmem((SUB, 128), BF),
                vmem((MID, 256), BF),
                vmem((256, 512), BF),
                vmem((128, 512), BF),
                vmem((256, 256), BF),
                vmem((128, 256), BF),
                vmem((2, 4, MID, 512), F32),
                vmem((2, MID // 3, 128), F32),
                vmem((2, MID // 3, 128), F32),
                vmem((4, 2, MID, COLS), BF),
                vmem((4, MID, 128), F32),
                vmem((MID, 512), F32),
                vmem((2, OWN, COLS), F32),
                vmem((2, 2, OWN, COLS), F32),
                vmem((2, SUBS, 2, SUB, COLS), F32),
                vmem((2, 2, KEEP, 128), F32),
                vmem((2, LATE, 128), F32),
                vmem((SUBS, 2, SUB, COLS), F32),
                vmem((2, KEEP, 128), F32),
                vmem((LATE, 128), F32),
                vmem((MID, COLS), F32),
                vmem((BLOCK, COLS), F32),
                dma((12,)),
                dma((3,)),
                dma((1,)),
                dma((2,)),
                dma((2,)),
                dma((2,)),
                dma((2,)),
                dma((2,)),
                dma((SUBS + 2,)),
                dma((SUBS + 2,)),
                pltpu.SemaphoreType.REGULAR,
                pltpu.SemaphoreType.REGULAR,
                pltpu.SemaphoreType.REGULAR,
                pltpu.SemaphoreType.REGULAR,
            ],
            compiler_params=pltpu.CompilerParams(
                collective_id=0, has_side_effects=True, vmem_limit_bytes=VMEM_BYTES
            ),
        )(x, consts)

    return jax.shard_map(body, mesh=mesh, in_specs=(P("plane", None, "col"),), out_specs=P("plane", "col"), check_vma=False)
```

```python
import functools

import jax
import jax.numpy as jnp
import ml_dtypes
import numpy as np
from jax import lax
from jax.experimental import pallas as pl
from jax.experimental.pallas import tpu as pltpu
from jax.sharding import PartitionSpec as P

TAPS = np.array([1.0, 4.0, 6.0, 4.0, 1.0]) / 16.0
MESH = pl.DeviceIdType.MESH
BF = jnp.bfloat16
F32 = jnp.float32

ROWS = 1024
BLOCK = 256
COLS = 256
WIN = 288
MID = 144
LOW = 80
KEEP = 136
KEEP2 = 72
SUB = 64
SUBS = BLOCK // SUB
EXT = 67
WIDE = 512
ROW_PART = LOW + BLOCK
COL_PART = 2 * 256 + 128
REST = 4 * ROW_PART + 3 * COL_PART
LATE = KEEP2 + SUB // 2
EDGE = 76
VMEM_BYTES = 52 * 1024 * 1024
TO_RIGHT = 72
TO_LEFT = 80
PART = 48
OWN = 32
TOP = 16
BOTTOM = 32
P_SIZE = 8
GATE = 1
EXPO = float(-4.0 * np.log2(np.e))


def reduce_matrix(n):
    m = np.zeros((n // 2, n))
    for i in range(n // 2):
        for t in range(5):
            j = 2 * i - 2 + t
            if 0 <= j < n:
                m[i, j] = TAPS[t]
    return m


def expand_matrix(n):
    m = np.zeros((2 * n, n))
    for j in range(2 * n):
        for i in range(max(0, j // 2 - 2), min(n, j // 2 + 3)):
            t = j - 2 * i + 2
            if 0 <= t <= 4:
                m[j, i] = 2.0 * TAPS[t]
    return m


def window(m, row, rows, col, cols):
    out = np.zeros((rows, cols))
    r0, r1 = max(row, 0), min(row + rows, m.shape[0])
    c0, c1 = max(col, 0), min(col + cols, m.shape[1])
    out[r0 - row : r1 - row, c0 - col : c1 - col] = m[r0:r1, c0:c1]
    return out


def exact(m):
    cast = m.astype(ml_dtypes.bfloat16)
    assert (cast.astype(np.float64) == m).all()
    return cast


@functools.lru_cache(None)
def matrices():
    r1 = reduce_matrix(ROWS // 2)
    e0 = expand_matrix(ROWS // 2)
    row_low, row_up = [], []
    for p in range(4):
        m = window(r1, 64 * p - 2, LOW, 128 * p - 4, MID)
        row_low.append(np.concatenate([m, m], 1))
        m = window(e0, BLOCK * p, BLOCK, 128 * p - 4, MID)
        row_up.append(np.concatenate([m, m], 1))
    m = window(e0, SUB, SUB, 28, 48)
    row_sub = np.concatenate([m, m], 1)
    m = window(expand_matrix(ROWS // 4), 124, MID, 62, LOW)
    row_base = np.concatenate([m, m], 1)
    row_both = [up[:, :MID] @ m for up in row_up]
    row_up = [np.concatenate([up, np.concatenate([v, v], 1)], 1) for up, v in zip(row_up, row_both)]
    n = 3 * COLS
    c0, c1 = reduce_matrix(n), reduce_matrix(n // 2)
    x0 = expand_matrix(n // 2)
    col_in, col_up = [], []
    for b in range(3):
        full = np.concatenate(
            [
                (x0 @ c0)[COLS * b : COLS * (b + 1)],
                c0[128 * b : 128 * (b + 1)],
                window(c1 @ c0, 64 * b - 1, 67, 0, n),
                window(c0, 128 * b - 1, 1, 0, n),
                window(c0, 128 * (b + 1), 1, 0, n),
                np.zeros((3, n)),
                window(c0, 128 * (b + 1) - 1, 2, 0, n),
                window(c1 @ c0, 64 * (b + 1) - 1, 2, 0, n),
                np.zeros((4, n)),
                window(c0, 128 * b - 1, 2, 0, n),
                window(c1 @ c0, 64 * b - 1, 3, 0, n),
                np.zeros((43, n)),
            ],
            0,
        ).T
        col_in.append(full[COLS * b : COLS * (b + 1)])
        up = x0[COLS * b : COLS * (b + 1)].T
        both = np.zeros((256, COLS))
        both[:128] = up[128 * b : 128 * (b + 1)]
        both[128 + EXT] = window(up, 128 * b - 1, 1, 0, COLS)[0]
        both[128 + EXT + 1] = window(up, 128 * (b + 1), 1, 0, COLS)[0]
        col_up.append(both)
    col_halo = np.zeros((128, 512))
    for lane, i in ((0, -1), (1, 0), (8, 127), (9, 128)):
        col_halo[lane, :COLS] = x0[COLS : 2 * COLS, 128 + i]
        if 0 <= i < 128:
            col_halo[lane, COLS + i] = 1.0
        else:
            col_halo[lane, COLS + 128 + EXT + (i > 0)] = 1.0
    col_halo[1, COLS + 128 + 2] = TAPS[0]
    for lane, i in ((2, -1), (3, 0), (10, 63), (11, 64), (12, 65)):
        col_halo[lane, COLS + 128 + 1 + i] = 1.0
    col_base = np.zeros((128, 256))
    base = expand_matrix(n // 4)
    col_base[:67, :128] = window(base, 128, 128, 63, 67).T
    col_base[:67, 128 + EXT] = window(base, 127, 1, 63, 67)[0]
    col_base[:67, 128 + EXT + 1] = window(base, 256, 1, 63, 67)[0]
    col_up = [np.concatenate([up, col_base @ up / P_SIZE], 0) for up in col_up]
    parts = []
    for p in range(4):
        parts += [row_low[p], row_up[p]]
    for b in range(3):
        parts += [col_in[b], col_up[b]]
    parts += [col_base, row_base, row_sub, col_halo]
    return np.concatenate([exact(np.pad(m, ((0, 0), (0, WIDE - m.shape[1])))) for m in parts], 0)


def split(v):
    hi = v.astype(BF)
    lo = (v - hi.astype(F32)).astype(BF)
    return hi, lo


def dot(a, b):
    return jnp.dot(a, b, preferred_element_type=F32)


def tall(v):
    return jnp.concatenate(split(v), 0)


def inverse(v):
    r = pl.reciprocal(v, approx=True)
    return r * (2.0 - v * r)


def weight(d):
    return jnp.exp2(EXPO * inverse(1.0 + d * d))


def kernel(
    count,
    x_ref, const_ref,
    out_ref,
    xwin, xpart, m_row_low, m_row_up, m_row_sub, m_row_base, m_col_in, m_col_halo, m_col_up, m_col_base,
    keep, pack, halo, wide, c1, low, part, part_in,
    level0, level1, late, far0, far1, far_late, jbuf, upper,
    m_sem, x_sem, part_send, part_recv, swap_send, swap_recv, halo_send, halo_recv, far_send, far_recv, group_sem, sibling_sem, far_sem, beside_sem,
):
    me = lax.axis_index("plane")
    q = lax.axis_index("col")
    chip, core = me // 2, me % 2
    far = 2 * (1 - chip) + core
    sibling = 2 * chip + 1 - core
    far_sibling = 2 * (1 - chip) + 1 - core
    side = (q + count - 2) // (count - 1) + q // (count - 1)
    left, right = (q + count - 1) % count, (q + 1) % count
    has_left, has_right = q > 0, q < count - 1
    blocks = (far, me)
    first = 2 * (1 - chip) + 1

    barrier = pltpu.get_barrier_semaphore()

    def tell(sem, plane, col):
        pl.semaphore_signal(sem, inc=1, device_id=(plane, col), device_id_type=MESH)

    @pl.when(me == GATE)
    def _():
        for plane in (0, 2, 3):
            tell(barrier, plane, q)

    @pl.when((me == 0) | (me == 3))
    def _():
        tell(barrier, 2, q)

    def start_of(p):
        return pl.multiple_of(BLOCK * p - 16 + 16 * ((3 - p) // 3) - 16 * (p // 3), 16)

    def offset_of(p):
        return pl.multiple_of(16 - 16 * ((3 - p) // 3) + 16 * (p // 3), 16)

    def half(ref, h):
        return ref.at[:, :, pl.ds(128 * h, 128)]

    own = []
    for b in range(2):
        for h in range(2):
            own.append(
                pltpu.make_async_copy(
                    half(x_ref.at[:, pl.ds(start_of(blocks[b]), WIN)], h),
                    xwin.at[b, pl.ds(0, 2), h, pl.ds(TOP, WIN)],
                    x_sem.at[b, h],
                )
            )

    def const(at, rows, cols):
        return const_ref.at[pl.ds(pl.multiple_of(at, 16), rows), pl.ds(0, cols)]

    col_at = 4 * ROW_PART + COL_PART * side
    loads = [
        (const(col_at, 256, 512), m_col_in),
        (const(REST + 128 + MID, SUB, 128), m_row_sub),
        (const(ROW_PART * far, LOW, 384), m_row_low.at[0]),
        (const(REST, 128, 256), m_col_base),
        (const(REST + 128, MID, 256), m_row_base),
        (const(REST + 128 + MID + SUB, 128, 512), m_col_halo),
        (const(ROW_PART * me, LOW, 384), m_row_low.at[1]),
        (const(col_at + 256, 256 + 128, 256), m_col_up),
        (const(ROW_PART * me + LOW, BLOCK, 512), m_row_up),
    ]
    loads = [pltpu.make_async_copy(s, d, m_sem.at[i]) for i, (s, d) in enumerate(loads)]
    early = [
        pltpu.make_async_copy(
            half(x_ref.at[:, pl.ds(start_of(first), 128)], h), xpart.at[:, h, pl.ds(TOP, 128)], x_sem.at[2, h]
        )
        for h in range(2)
    ]
    early[0].start()
    early[1].start()
    loads[0].start()
    loads[1].start()
    own[0].start()
    own[1].start()

    def twice(ref):
        m = ref[...]
        return jnp.concatenate([m, m], 0)

    @pl.when((me == 0) | (me == 3))
    def _():
        pl.semaphore_wait(barrier, 1)

    @pl.when(me == 2)
    def _():
        pl.semaphore_wait(barrier, 3)
        tell(sibling_sem, 3, q)
        tell(far_sem, 0, q)
        tell(group_sem, GATE, q)

    @pl.when(me == 0)
    def _():
        tell(sibling_sem, GATE, q)

    @pl.when(me == 3)
    def _():
        tell(far_sem, GATE, q)

    def remote(src, dst, send, recv, plane, col):
        return pltpu.make_async_remote_copy(
            src_ref=src, dst_ref=dst, send_sem=send, recv_sem=recv, device_id=(plane, col), device_id_type=MESH
        )

    swaps = []
    for b, p in enumerate((far_sibling, sibling)):
        for h in range(2):
            swaps.append(
                remote(
                    half(x_ref.at[:, pl.ds(start_of(p), WIN)], h),
                    xwin.at[b, pl.ds(2, 2), h, pl.ds(TOP, WIN)],
                    swap_send.at[b, h],
                    swap_recv.at[b, h],
                    sibling,
                    q,
                )
            )

    @pl.when(core == 1)
    def _():
        pl.semaphore_wait(sibling_sem, 1)

    swaps[0].start()
    swaps[1].start()

    for b in range(2):
        for p in range(4):
            xwin[b, p, :, pl.ds(0, TOP)] = jnp.zeros((2, TOP, 128), F32)
            xwin[b, p, :, pl.ds(TOP + WIN, BOTTOM)] = jnp.zeros((2, BOTTOM, 128), F32)
    own[2].start()
    own[3].start()
    for copy in loads[2:]:
        copy.start()
    jbuf[pl.ds(KEEP, MID - KEEP)] = jnp.zeros((MID - KEEP, COLS), F32)

    @pl.when(q == 0)
    def _():
        halo[0] = jnp.zeros((MID // 3, 128), F32)

    @pl.when(q == count - 1)
    def _():
        halo[1] = jnp.zeros((MID // 3, 128), F32)

    def joined(ref, at, rows):
        return jnp.concatenate([ref[at + (0, rows)], ref[at + (1, rows)]], 1)

    def rows_down(ref, at, block, rows):
        base = offset_of(block) + TOP - 10
        taps = [joined(ref, at, pl.ds(base + t, rows, stride=2)) for t in range(5)]
        value = (taps[0] + taps[4]) * TAPS[0] + (taps[1] + taps[3]) * TAPS[1] + taps[2] * TAPS[2]
        row = lax.broadcasted_iota(jnp.int32, (rows, COLS), 0)
        inside = (row >= 4 * ((3 - block) // 3)) & (row < MID - 12 * (block // 3))
        return jnp.where(inside, value, 0.0)

    for p in range(2):
        xpart[p, :, pl.ds(0, TOP)] = jnp.zeros((2, TOP, 128), F32)

    early[0].wait()
    early[1].wait()
    loads[0].wait()
    loads[1].wait()
    num = jnp.zeros((OWN, COLS), F32)
    den = jnp.zeros((OWN, COLS), F32)
    for p in range(2):
        value = rows_down(xpart, (p,), first, PART)
        m = m_col_in[:, pl.ds(0, COLS)]
        value = dot(jnp.concatenate(split(value), 0), m)
        value = value[:PART] + value[PART:]
        z = dot(m_row_sub[pl.ds(0, OWN), pl.ds(0, 2 * PART)], tall(value))
        d = joined(xpart, (p,), pl.ds(pl.multiple_of(TOP + offset_of(first), 16), OWN)) - z
        w = weight(d)
        num = num + w * d
        den = den + w
    part[0] = num
    part[1] = den

    far_part = remote(part, part_in.at[core], part_send.at[0], part_recv.at[core], first, q)

    @pl.when(chip == 0)
    def _():
        pl.semaphore_wait(far_sem, 1)

    far_part.start()
    swaps[2].start()
    swaps[3].start()

    @pl.when(me == GATE)
    def _():
        pl.semaphore_wait(group_sem, 1)

        @pl.when(has_left)
        def _():
            tell(barrier, GATE, left)

        @pl.when(has_right)
        def _():
            tell(barrier, GATE, right)

    lane = lax.broadcasted_iota(jnp.int32, (MID, 128), 1)
    fold_lane = lax.broadcasted_iota(jnp.int32, (MID // 3, 128), 1)
    half_lane = lax.broadcasted_iota(jnp.int32, (SUB // 2, 128), 1)
    sub_lane = lax.broadcasted_iota(jnp.int32, (SUB, 128), 1)
    low_lane = lax.broadcasted_iota(jnp.int32, (KEEP2, 128), 1)
    keep_lane = lax.broadcasted_iota(jnp.int32, (KEEP, 128), 1)

    def turn(v, by):
        by = by % 128
        return pltpu.roll(v, by, 1) if by else v

    ahead = (q % 8 == 0) & has_left
    behind = (q % (count // 2) == 0) & has_left

    def meet():
        @pl.when(me == GATE)
        def _():
            pl.semaphore_wait(barrier, (q + count - 1) // count + (2 * count - 2 - q) // count)
            for plane in (0, 2, 3):
                tell(beside_sem, plane, q)

    def rows_in(b, p):
        if p == 0:
            own[2 * b].wait()
            own[2 * b + 1].wait()
        if p == 2:
            swaps[2 * b].wait_recv()
            swaps[2 * b + 1].wait_recv()
        return rows_down(xwin, (b, p), blocks[b], MID)

    def columns_in(b, planes):
        halves = []
        for p in planes:
            halves += split(rows_in(b, p))
        value = dot(jnp.concatenate(halves, 0), m_col_in[...])
        for i, p in enumerate(planes):
            keep[b, p] = value[2 * MID * i : 2 * MID * i + MID] + value[2 * MID * i + MID : 2 * MID * (i + 1)]

    def put(p, value):
        whi, wlo = split(value[:, :COLS])
        wide[p, 0] = whi
        wide[p, 1] = wlo
        c1[p] = value[:, COLS : COLS + 128]
        low[:, pl.ds(128 * p, 128)] = value[:, COLS + 128 :]

    def sums_zero(b, s):
        num = jnp.zeros((SUB, COLS), F32)
        den = jnp.zeros((SUB, COLS), F32)
        for p in range(4):
            rows = pl.ds(32 * s, 48)
            both = jnp.concatenate([wide[p, 0, rows], wide[p, 1, rows]], 0)
            z = dot(m_row_sub[:, pl.ds(0, 96)], both)
            d = joined(xwin, (b, p), pl.ds(pl.multiple_of(TOP + offset_of(blocks[b]) + SUB * s, 16), SUB)) - z
            w = weight(d)
            num = num + w * d
            den = den + w
        return num, den

    def columns_up(c2):
        return dot(jnp.concatenate(split(c2), 1), twice(m_col_base))

    def sums_one(b):
        c2 = dot(m_row_low[b, :, pl.ds(0, 2 * MID)], tall(low[...]))
        parts = [c2[:, 128 * p : 128 * p + 128] for p in range(4)]
        u = columns_up(jnp.concatenate(parts, 0))
        u = jnp.concatenate([u[LOW * p : LOW * p + LOW] for p in range(4)], 1)
        base = dot(m_row_base[:, pl.ds(0, 2 * LOW)], tall(u))
        num = jnp.zeros((MID, COLS), F32)
        den = jnp.zeros((MID, COLS), F32)
        for p in range(4):
            d = jnp.concatenate([c1[p], low[:, pl.ds(128 * p, 128)]], 1) - base[:, COLS * p : COLS * p + COLS]
            w = weight(d)
            num = num + w * d
            den = den + w
        return num, den, parts[0] + parts[1] + parts[2] + parts[3]

    def put_one(b, num, den):
        level1[b, 0] = num[:KEEP, :128]
        level1[b, 1] = den[:KEEP, :128]

    def late_tile(num, den, total):
        tile = turn(den[64 : 64 + KEEP2, 128:], 6)
        tile = jnp.where(low_lane < EXT + 6, turn(den[:KEEP2, 128:], 4), tile)
        tile = jnp.where(low_lane < EXT + 4, turn(num[64 : 64 + KEEP2, 128:], 2), tile)
        tile = jnp.where(low_lane < EXT + 2, num[:KEEP2, 128:], tile)
        tile = jnp.where(low_lane < EXT, total[:KEEP2], tile)
        for i, v in enumerate((num, den)):
            for h in range(2):
                at = EDGE + 20 * i + 10 * h
                tile = jnp.where(low_lane >= at, turn(v[64 * h : 64 * h + KEEP2, :128], 4 + at), tile)
        return tile

    far_zero = [remote(level0.at[0, s], far0.at[s], far_send.at[s], far_recv.at[s], far, q) for s in range(SUBS)]
    rest = pl.ds(OWN, SUB - OWN)
    far_rest = remote(level0.at[0, 0, :, rest], far0.at[0, :, rest], far_send.at[0], far_recv.at[0], far, q)
    far_one = remote(level1.at[0], far1, far_send.at[SUBS], far_recv.at[SUBS], far, q)
    far_last = remote(late.at[0], far_late, far_send.at[SUBS + 1], far_recv.at[SUBS + 1], far, q)
    columns_in(0, (0, 1))
    put(0, keep[0, 0])
    put(1, keep[0, 1])
    columns_in(1, (0, 1))
    columns_in(0, (2, 3))
    put(2, keep[0, 2])
    put(3, keep[0, 3])

    def far_chunk(s):
        num, den = sums_zero(0, s)
        level0[0, s, 0] = num
        level0[0, s, 1] = den

    for s in range(1, SUBS - 1):
        far_chunk(s)
        pl.when(core == 1)(far_zero[s].start)
    far_chunk(0)
    pl.when(core == 1)(far_rest.start)
    pl.when(jnp.logical_not(ahead))(meet)
    columns_in(1, (2, 3))
    packs = [jnp.zeros((MID // 3, 128), F32), jnp.zeros((MID // 3, 128), F32)]
    for b in range(2):
        for p in range(4):
            tile = keep[b, p, :, pl.ds(COLS + 128, 128)]
            for h in range(3):
                at = 40 * h + 20 * b + 5 * p
                here = (fold_lane >= at) & (fold_lane < at + 5)
                rows = tile[MID // 3 * h : MID // 3 * (h + 1)]
                packs[0] = jnp.where(here, turn(rows, at - TO_LEFT), packs[0])
                packs[1] = jnp.where(here, turn(rows, at - TO_RIGHT), packs[1])
    pack[0] = packs[0]
    pack[1] = packs[1]

    to_left = remote(pack.at[0], halo.at[1], halo_send.at[0], halo_recv.at[1], me, left)
    to_right = remote(pack.at[1], halo.at[0], halo_send.at[1], halo_recv.at[0], me, right)

    def send_halo():
        @pl.when(me != GATE)
        def _():
            pl.semaphore_wait(beside_sem, 1)

        @pl.when(has_left)
        def _():
            to_left.start()

        @pl.when(has_right)
        def _():
            to_right.start()

    pl.when(jnp.logical_not(ahead))(send_halo)

    for s in range(SUBS - 1):
        pl.when(core == 0)(far_zero[s].start)
    far_chunk(SUBS - 1)
    for copy in loads[2:5]:
        copy.wait()
    num, den, _ = sums_one(0)
    put_one(0, num, den)
    far_one.start()

    pl.when(ahead)(meet)
    pl.when(ahead)(send_halo)

    pl.when(behind)(far_zero[SUBS - 1].start)
    for copy in loads[5:]:
        copy.wait()

    @pl.when(has_left)
    def _():
        to_right.wait_recv()

    @pl.when(has_right)
    def _():
        to_left.wait_recv()

    for b in range(2):
        edges = []
        for p in range(4):
            at = 20 * b + 5 * p
            from_left = jnp.concatenate([turn(halo[0], -at - 40 * h) for h in range(3)], 0)
            from_right = jnp.concatenate([turn(halo[1], 8 - at - 40 * h) for h in range(3)], 0)
            edge = jnp.where((lane >= 8) & (lane < 13), from_right, jnp.where(lane < 5, from_left, 0.0))
            edges.append(jnp.concatenate(split(edge), 1))
        added = dot(jnp.concatenate(edges, 0), twice(m_col_halo))
        for p in range(4):
            put(p, keep[b, p] + added[MID * p : MID * (p + 1)])

        num, den, total = sums_one(b)
        late[b, pl.ds(0, KEEP2)] = late_tile(num, den, total)
        if b == 1:
            put_one(b, num, den)

        patch = jnp.zeros((SUB // 2, 128), F32)
        for s in range(SUBS):
            num, den = sums_zero(b, s)
            if b == 1:
                level0[1, s, 0] = num
                level0[1, s, 1] = den
                continue
            for i, v in enumerate((num, den)):
                edges = jnp.where(sub_lane < 64, v[:, :128], v[:, 128:])
                for h in range(2):
                    at = 32 * s + 16 * h + 8 * i
                    moved = turn(edges[32 * h : 32 * h + 32], 4 + at)
                    patch = jnp.where((half_lane >= at) & (half_lane < at + 8), moved, patch)
        if b == 0:
            late[0, pl.ds(KEEP2, SUB // 2)] = patch
            far_last.start()
            pl.when(jnp.logical_not(behind))(far_zero[SUBS - 1].start)

    far_one.wait_recv()
    far_last.wait_recv()
    own_tile, far_tile = late[1, pl.ds(0, KEEP2)], far_late[pl.ds(0, KEEP2)]
    tile = own_tile + far_tile
    total = jnp.concatenate([jnp.where(low_lane < EXT, tile, 0.0), jnp.zeros((LOW - KEEP2, 128), F32)], 0)
    coarse = m_col_up[pl.ds(256, 128)]
    base = dot(jnp.concatenate(split(total), 1), jnp.concatenate([coarse, coarse], 0))
    at_edge = (keep_lane < 6) | (keep_lane >= 124)
    sums = []
    for i in range(2):
        at = EDGE + 20 * i
        edges = jnp.concatenate([turn(far_tile, -(4 + at))[:64], turn(far_tile, -(14 + at))], 0)
        sums.append(level1[1, i] + jnp.where(at_edge, edges, far1[i]))
    jbuf[pl.ds(0, KEEP), pl.ds(0, 128)] = sums[0] * inverse(sums[1])
    outer = (low_lane >= EXT) & (low_lane < EXT + 4)
    ratio = jnp.where(outer, tile, 0.0) * inverse(jnp.where(outer, turn(tile, -4), 1.0))
    ratio = jnp.concatenate([ratio[:64], turn(ratio, -2)], 0)
    ratio = jnp.where((keep_lane >= EXT) & (keep_lane < EXT + 2), ratio, 0.0)
    jbuf[pl.ds(0, KEEP), pl.ds(128, 128)] = ratio
    m = m_col_up[pl.ds(0, 256)]
    u = dot(jnp.concatenate(split(jbuf[...]), 1), jnp.concatenate([m, m], 0))
    upper[...] = dot(m_row_up[:, pl.ds(0, 2 * (MID + LOW))], jnp.concatenate([tall(u), tall(base)], 0))

    @pl.when(core == 1)
    def _():
        for i in range(2):
            remote(part, part_in.at[i], part_send.at[0], part_recv.at[i], first, q).wait_recv()
        far_rest.wait_recv()
        far0[0, :, pl.ds(0, OWN)] = part_in[0] + part_in[1]

    pl.when(core == 0)(far_zero[0].wait_recv)
    patch = far_late[pl.ds(KEEP2, SUB // 2)]
    for s in range(SUBS):
        if s:
            far_zero[s].wait_recv()
        sums = []
        for i in range(2):
            at = 32 * s + 8 * i
            edges = jnp.concatenate([turn(patch, -(4 + at)), turn(patch, -(20 + at))], 0)
            first = jnp.where(sub_lane < 4, edges, far0[s, i, :, pl.ds(0, 128)])
            second = jnp.where(sub_lane >= 124, edges, far0[s, i, :, pl.ds(128, 128)])
            sums.append(level0[1, s, i] + jnp.concatenate([first, second], 1))
        rows = pl.ds(SUB * s, SUB)
        out_ref[rows] = sums[0] * inverse(sums[1]) + upper[rows]

    @pl.when(has_left)
    def _():
        to_left.wait_send()

    @pl.when(has_right)
    def _():
        to_right.wait_send()

    pl.when(core == 0)(far_zero[0].wait_send)
    pl.when(core == 1)(far_rest.wait_send)
    for copy in swaps + far_zero[1:] + [far_one, far_last, far_part]:
        copy.wait_send()


def solution(mesh):
    count = mesh.shape["col"]
    consts = matrices()

    def body(x):
        dma = pltpu.SemaphoreType.DMA
        vmem = pltpu.VMEM
        return pl.pallas_call(
            functools.partial(kernel, count),
            out_shape=jax.ShapeDtypeStruct((BLOCK, COLS), F32),
            in_specs=[pl.BlockSpec(memory_space=pl.ANY)] * 2,
            out_specs=pl.BlockSpec(memory_space=pltpu.VMEM),
            scratch_shapes=[
                vmem((2, 4, 2, TOP + WIN + BOTTOM, 128), F32),
                vmem((2, 2, TOP + 128, 128), F32),
                vmem((2, LOW, 384), BF),
                vmem((BLOCK, 512), BF),
                vmem((SUB, 128), BF),
                vmem((MID, 256), BF),
                vmem((256, 512), BF),
                vmem((128, 512), BF),
                vmem((384, 256), BF),
                vmem((128, 256), BF),
                vmem((2, 4, MID, 512), F32),
                vmem((2, MID // 3, 128), F32),
                vmem((2, MID // 3, 128), F32),
                vmem((4, 2, MID, COLS), BF),
                vmem((4, MID, 128), F32),
                vmem((MID, 512), F32),
                vmem((2, OWN, COLS), F32),
                vmem((2, 2, OWN, COLS), F32),
                vmem((2, SUBS, 2, SUB, COLS), F32),
                vmem((2, 2, KEEP, 128), F32),
                vmem((2, LATE, 128), F32),
                vmem((SUBS, 2, SUB, COLS), F32),
                vmem((2, KEEP, 128), F32),
                vmem((LATE, 128), F32),
                vmem((MID, COLS), F32),
                vmem((BLOCK, COLS), F32),
                dma((9,)),
                dma((3, 2)),
                dma((1,)),
                dma((2,)),
                dma((2, 2)),
                dma((2, 2)),
                dma((2,)),
                dma((2,)),
                dma((SUBS + 2,)),
                dma((SUBS + 2,)),
                pltpu.SemaphoreType.REGULAR,
                pltpu.SemaphoreType.REGULAR,
                pltpu.SemaphoreType.REGULAR,
                pltpu.SemaphoreType.REGULAR,
            ],
            compiler_params=pltpu.CompilerParams(
                collective_id=0, has_side_effects=True, vmem_limit_bytes=VMEM_BYTES
            ),
        )(x, consts)

    return jax.shard_map(body, mesh=mesh, in_specs=(P("plane", None, "col"),), out_specs=P("plane", "col"), check_vma=False)
```

```python
import functools

import jax
import jax.numpy as jnp
import ml_dtypes
import numpy as np
from jax import lax
from jax.experimental import pallas as pl
from jax.experimental.pallas import tpu as pltpu
from jax.sharding import PartitionSpec as P

TAPS = np.array([1.0, 4.0, 6.0, 4.0, 1.0]) / 16.0
MESH = pl.DeviceIdType.MESH
BF = jnp.bfloat16
F32 = jnp.float32

ROWS = 1024
BLOCK = 256
COLS = 256
WIN = 288
MID = 144
LOW = 80
KEEP = 136
KEEP2 = 72
SUB = 64
SUBS = BLOCK // SUB
EXT = 67
WIDE = 512
ROW_PART = LOW + BLOCK
COL_PART = 2 * 256 + 128
REST = 4 * ROW_PART + 3 * COL_PART
LATE = KEEP2 + SUB // 2
EDGE = 76
VMEM_BYTES = 52 * 1024 * 1024
TO_RIGHT = 72
TO_LEFT = 80
PART = 48
OWN = 32
TOP = 16
BOTTOM = 32
P_SIZE = 8
GATE = 1
EXPO = float(-4.0 * np.log2(np.e))


def reduce_matrix(n):
    m = np.zeros((n // 2, n))
    for i in range(n // 2):
        for t in range(5):
            j = 2 * i - 2 + t
            if 0 <= j < n:
                m[i, j] = TAPS[t]
    return m


def expand_matrix(n):
    m = np.zeros((2 * n, n))
    for j in range(2 * n):
        for i in range(max(0, j // 2 - 2), min(n, j // 2 + 3)):
            t = j - 2 * i + 2
            if 0 <= t <= 4:
                m[j, i] = 2.0 * TAPS[t]
    return m


def window(m, row, rows, col, cols):
    out = np.zeros((rows, cols))
    r0, r1 = max(row, 0), min(row + rows, m.shape[0])
    c0, c1 = max(col, 0), min(col + cols, m.shape[1])
    out[r0 - row : r1 - row, c0 - col : c1 - col] = m[r0:r1, c0:c1]
    return out


def exact(m):
    cast = m.astype(ml_dtypes.bfloat16)
    assert (cast.astype(np.float64) == m).all()
    return cast


@functools.lru_cache(None)
def matrices():
    r1 = reduce_matrix(ROWS // 2)
    e0 = expand_matrix(ROWS // 2)
    row_low, row_up = [], []
    for p in range(4):
        m = window(r1, 64 * p - 2, LOW, 128 * p - 4, MID)
        row_low.append(np.concatenate([m, m], 1))
        m = window(e0, BLOCK * p, BLOCK, 128 * p - 4, MID)
        row_up.append(np.concatenate([m, m], 1))
    m = window(e0, SUB, SUB, 28, 48)
    row_sub = np.concatenate([m, m], 1)
    m = window(expand_matrix(ROWS // 4), 124, MID, 62, LOW)
    row_base = np.concatenate([m, m], 1)
    row_both = [up[:, :MID] @ m for up in row_up]
    row_up = [np.concatenate([up, np.concatenate([v, v], 1)], 1) for up, v in zip(row_up, row_both)]
    n = 3 * COLS
    c0, c1 = reduce_matrix(n), reduce_matrix(n // 2)
    x0 = expand_matrix(n // 2)
    col_in, col_up = [], []
    for b in range(3):
        full = np.concatenate(
            [
                (x0 @ c0)[COLS * b : COLS * (b + 1)],
                c0[128 * b : 128 * (b + 1)],
                window(c1 @ c0, 64 * b - 1, 67, 0, n),
                window(c0, 128 * b - 1, 1, 0, n),
                window(c0, 128 * (b + 1), 1, 0, n),
                np.zeros((3, n)),
                window(c0, 128 * (b + 1) - 1, 2, 0, n),
                window(c1 @ c0, 64 * (b + 1) - 1, 2, 0, n),
                np.zeros((4, n)),
                window(c0, 128 * b - 1, 2, 0, n),
                window(c1 @ c0, 64 * b - 1, 3, 0, n),
                np.zeros((43, n)),
            ],
            0,
        ).T
        col_in.append(full[COLS * b : COLS * (b + 1)])
        up = x0[COLS * b : COLS * (b + 1)].T
        both = np.zeros((256, COLS))
        both[:128] = up[128 * b : 128 * (b + 1)]
        both[128 + EXT] = window(up, 128 * b - 1, 1, 0, COLS)[0]
        both[128 + EXT + 1] = window(up, 128 * (b + 1), 1, 0, COLS)[0]
        col_up.append(both)
    col_halo = np.zeros((128, 512))
    for lane, i in ((0, -1), (1, 0), (8, 127), (9, 128)):
        col_halo[lane, :COLS] = x0[COLS : 2 * COLS, 128 + i]
        if 0 <= i < 128:
            col_halo[lane, COLS + i] = 1.0
        else:
            col_halo[lane, COLS + 128 + EXT + (i > 0)] = 1.0
    col_halo[1, COLS + 128 + 2] = TAPS[0]
    for lane, i in ((2, -1), (3, 0), (10, 63), (11, 64), (12, 65)):
        col_halo[lane, COLS + 128 + 1 + i] = 1.0
    col_base = np.zeros((128, 256))
    base = expand_matrix(n // 4)
    col_base[:67, :128] = window(base, 128, 128, 63, 67).T
    col_base[:67, 128 + EXT] = window(base, 127, 1, 63, 67)[0]
    col_base[:67, 128 + EXT + 1] = window(base, 256, 1, 63, 67)[0]
    col_up = [np.concatenate([up, col_base @ up / P_SIZE], 0) for up in col_up]
    parts = []
    for p in range(4):
        parts += [row_low[p], row_up[p]]
    for b in range(3):
        parts += [col_in[b], col_up[b]]
    parts += [col_base, row_base, row_sub, col_halo]
    return np.concatenate([exact(np.pad(m, ((0, 0), (0, WIDE - m.shape[1])))) for m in parts], 0)


def split(v):
    hi = v.astype(BF)
    lo = (v - hi.astype(F32)).astype(BF)
    return hi, lo


def dot(a, b):
    return jnp.dot(a, b, preferred_element_type=F32)


def tall(v):
    return jnp.concatenate(split(v), 0)


def inverse(v):
    r = pl.reciprocal(v, approx=True)
    return r * (2.0 - v * r)


def weight(d):
    return jnp.exp2(EXPO * inverse(1.0 + d * d))


def kernel(
    count,
    x_ref, const_ref,
    out_ref,
    xwin, xpart, m_row_low, m_row_up, m_row_sub, m_row_base, m_col_in, m_col_halo, m_col_up, m_col_base,
    keep, pack, halo, wide, c1, low, part, part_in,
    level0, level1, late, far0, far1, far_late, jbuf, upper,
    m_sem, x_sem, part_send, part_recv, swap_send, swap_recv, halo_send, halo_recv, far_send, far_recv, group_sem, sibling_sem, far_sem, beside_sem,
):
    me = lax.axis_index("plane")
    q = lax.axis_index("col")
    chip, core = me // 2, me % 2
    far = 2 * (1 - chip) + core
    sibling = 2 * chip + 1 - core
    far_sibling = 2 * (1 - chip) + 1 - core
    side = (q + count - 2) // (count - 1) + q // (count - 1)
    left, right = (q + count - 1) % count, (q + 1) % count
    has_left, has_right = q > 0, q < count - 1
    blocks = (far, me)
    first = 2 * (1 - chip) + 1

    barrier = pltpu.get_barrier_semaphore()

    def tell(sem, plane, col):
        pl.semaphore_signal(sem, inc=1, device_id=(plane, col), device_id_type=MESH)

    @pl.when(me == GATE)
    def _():
        for plane in (0, 2, 3):
            tell(barrier, plane, q)

    @pl.when((me == 0) | (me == 3))
    def _():
        tell(barrier, 2, q)

    def start_of(p):
        return pl.multiple_of(BLOCK * p - 16 + 16 * ((3 - p) // 3) - 16 * (p // 3), 16)

    def offset_of(p):
        return pl.multiple_of(16 - 16 * ((3 - p) // 3) + 16 * (p // 3), 16)

    def half(ref, h):
        return ref.at[:, :, pl.ds(128 * h, 128)]

    own = []
    for b in range(2):
        for h in range(2):
            own.append(
                pltpu.make_async_copy(
                    half(x_ref.at[:, pl.ds(start_of(blocks[b]), WIN)], h),
                    xwin.at[b, pl.ds(0, 2), h, pl.ds(TOP, WIN)],
                    x_sem.at[b, h],
                )
            )

    def const(at, rows, cols):
        return const_ref.at[pl.ds(pl.multiple_of(at, 16), rows), pl.ds(0, cols)]

    col_at = 4 * ROW_PART + COL_PART * side
    loads = [
        (const(col_at, 256, 512), m_col_in),
        (const(REST + 128 + MID, SUB, 128), m_row_sub),
        (const(ROW_PART * far, LOW, 384), m_row_low.at[0]),
        (const(REST, 128, 256), m_col_base),
        (const(REST + 128, MID, 256), m_row_base),
        (const(REST + 128 + MID + SUB, 128, 512), m_col_halo),
        (const(ROW_PART * me, LOW, 384), m_row_low.at[1]),
        (const(col_at + 256, 256 + 128, 256), m_col_up),
        (const(ROW_PART * me + LOW, BLOCK, 512), m_row_up),
    ]
    loads = [pltpu.make_async_copy(s, d, m_sem.at[i]) for i, (s, d) in enumerate(loads)]
    early = [
        pltpu.make_async_copy(
            half(x_ref.at[:, pl.ds(start_of(first), 128)], h), xpart.at[:, h, pl.ds(TOP, 128)], x_sem.at[2, h]
        )
        for h in range(2)
    ]
    early[0].start()
    early[1].start()
    loads[0].start()
    loads[1].start()
    own[0].start()
    own[1].start()

    def twice(ref):
        m = ref[...]
        return jnp.concatenate([m, m], 0)

    @pl.when((me == 0) | (me == 3))
    def _():
        pl.semaphore_wait(barrier, 1)

    @pl.when(me == 2)
    def _():
        pl.semaphore_wait(barrier, 3)
        tell(sibling_sem, 3, q)
        tell(far_sem, 0, q)
        tell(group_sem, GATE, q)

    @pl.when(me == 0)
    def _():
        tell(sibling_sem, GATE, q)

    @pl.when(me == 3)
    def _():
        tell(far_sem, GATE, q)

    def remote(src, dst, send, recv, plane, col):
        return pltpu.make_async_remote_copy(
            src_ref=src, dst_ref=dst, send_sem=send, recv_sem=recv, device_id=(plane, col), device_id_type=MESH
        )

    swaps = []
    for b, p in enumerate((far_sibling, sibling)):
        for h in range(2):
            swaps.append(
                remote(
                    half(x_ref.at[:, pl.ds(start_of(p), WIN)], h),
                    xwin.at[b, pl.ds(2, 2), h, pl.ds(TOP, WIN)],
                    swap_send.at[b, h],
                    swap_recv.at[b, h],
                    sibling,
                    q,
                )
            )

    @pl.when(core == 1)
    def _():
        pl.semaphore_wait(sibling_sem, 1)

    swaps[0].start()
    swaps[1].start()

    for b in range(2):
        for p in range(4):
            xwin[b, p, :, pl.ds(0, TOP)] = jnp.zeros((2, TOP, 128), F32)
            xwin[b, p, :, pl.ds(TOP + WIN, BOTTOM)] = jnp.zeros((2, BOTTOM, 128), F32)
    own[2].start()
    own[3].start()
    for copy in loads[2:]:
        copy.start()
    jbuf[pl.ds(KEEP, MID - KEEP)] = jnp.zeros((MID - KEEP, COLS), F32)

    @pl.when(q == 0)
    def _():
        halo[0] = jnp.zeros((MID // 3, 128), F32)

    @pl.when(q == count - 1)
    def _():
        halo[1] = jnp.zeros((MID // 3, 128), F32)

    def joined(ref, at, rows):
        return jnp.concatenate([ref[at + (0, rows)], ref[at + (1, rows)]], 1)

    def rows_down(ref, at, block, rows):
        base = offset_of(block) + TOP - 10
        taps = [joined(ref, at, pl.ds(base + t, rows, stride=2)) for t in range(5)]
        value = (taps[0] + taps[4]) * TAPS[0] + (taps[1] + taps[3]) * TAPS[1] + taps[2] * TAPS[2]
        row = lax.broadcasted_iota(jnp.int32, (rows, COLS), 0)
        inside = (row >= 4 * ((3 - block) // 3)) & (row < MID - 12 * (block // 3))
        return jnp.where(inside, value, 0.0)

    for p in range(2):
        xpart[p, :, pl.ds(0, TOP)] = jnp.zeros((2, TOP, 128), F32)

    early[0].wait()
    early[1].wait()
    loads[0].wait()
    loads[1].wait()
    num = jnp.zeros((OWN, COLS), F32)
    den = jnp.zeros((OWN, COLS), F32)
    for p in range(2):
        value = rows_down(xpart, (p,), first, PART)
        m = m_col_in[:, pl.ds(0, COLS)]
        value = dot(jnp.concatenate(split(value), 0), m)
        value = value[:PART] + value[PART:]
        z = dot(m_row_sub[pl.ds(0, OWN), pl.ds(0, 2 * PART)], tall(value))
        d = joined(xpart, (p,), pl.ds(pl.multiple_of(TOP + offset_of(first), 16), OWN)) - z
        w = weight(d)
        num = num + w * d
        den = den + w
    part[0] = num
    part[1] = den

    far_part = remote(part, part_in.at[core], part_send.at[0], part_recv.at[core], first, q)

    @pl.when(chip == 0)
    def _():
        pl.semaphore_wait(far_sem, 1)

    far_part.start()
    swaps[2].start()
    swaps[3].start()

    @pl.when(me == GATE)
    def _():
        pl.semaphore_wait(group_sem, 1)

        @pl.when(has_left)
        def _():
            tell(barrier, GATE, left)

        @pl.when(has_right)
        def _():
            tell(barrier, GATE, right)

    lane = lax.broadcasted_iota(jnp.int32, (MID, 128), 1)
    fold_lane = lax.broadcasted_iota(jnp.int32, (MID // 3, 128), 1)
    half_lane = lax.broadcasted_iota(jnp.int32, (SUB // 2, 128), 1)
    sub_lane = lax.broadcasted_iota(jnp.int32, (SUB, 128), 1)
    low_lane = lax.broadcasted_iota(jnp.int32, (KEEP2, 128), 1)
    keep_lane = lax.broadcasted_iota(jnp.int32, (KEEP, 128), 1)

    def turn(v, by):
        by = by % 128
        return pltpu.roll(v, by, 1) if by else v

    ahead = (q % 8 == 0) & has_left
    behind = (q % (count // 2) == 0) & has_left

    def meet():
        @pl.when(me == GATE)
        def _():
            pl.semaphore_wait(barrier, (q + count - 1) // count + (2 * count - 2 - q) // count)
            for plane in (0, 2, 3):
                tell(beside_sem, plane, q)

    def rows_in(b, p):
        if p == 0:
            own[2 * b].wait()
            own[2 * b + 1].wait()
        if p == 2:
            swaps[2 * b].wait_recv()
            swaps[2 * b + 1].wait_recv()
        return rows_down(xwin, (b, p), blocks[b], MID)

    def columns_in(b, planes):
        halves = []
        for p in planes:
            halves += split(rows_in(b, p))
        value = dot(jnp.concatenate(halves, 0), m_col_in[...])
        for i, p in enumerate(planes):
            keep[b, p] = value[2 * MID * i : 2 * MID * i + MID] + value[2 * MID * i + MID : 2 * MID * (i + 1)]

    def put(p, value):
        whi, wlo = split(value[:, :COLS])
        wide[p, 0] = whi
        wide[p, 1] = wlo
        c1[p] = value[:, COLS : COLS + 128]
        low[:, pl.ds(128 * p, 128)] = value[:, COLS + 128 :]

    def sums_zero(b, s):
        num = jnp.zeros((SUB, COLS), F32)
        den = jnp.zeros((SUB, COLS), F32)
        for p in range(4):
            rows = pl.ds(32 * s, 48)
            both = jnp.concatenate([wide[p, 0, rows], wide[p, 1, rows]], 0)
            z = dot(m_row_sub[:, pl.ds(0, 96)], both)
            d = joined(xwin, (b, p), pl.ds(pl.multiple_of(TOP + offset_of(blocks[b]) + SUB * s, 16), SUB)) - z
            w = weight(d)
            num = num + w * d
            den = den + w
        return num, den

    def columns_up(c2):
        return dot(jnp.concatenate(split(c2), 1), twice(m_col_base))

    def sums_one(b):
        c2 = dot(m_row_low[b, :, pl.ds(0, 2 * MID)], tall(low[...]))
        parts = [c2[:, 128 * p : 128 * p + 128] for p in range(4)]
        u = columns_up(jnp.concatenate(parts, 0))
        u = jnp.concatenate([u[LOW * p : LOW * p + LOW] for p in range(4)], 1)
        base = dot(m_row_base[:, pl.ds(0, 2 * LOW)], tall(u))
        num = jnp.zeros((MID, COLS), F32)
        den = jnp.zeros((MID, COLS), F32)
        for p in range(4):
            d = jnp.concatenate([c1[p], low[:, pl.ds(128 * p, 128)]], 1) - base[:, COLS * p : COLS * p + COLS]
            w = weight(d)
            num = num + w * d
            den = den + w
        return num, den, parts[0] + parts[1] + parts[2] + parts[3]

    def put_one(b, num, den):
        level1[b, 0] = num[:KEEP, :128]
        level1[b, 1] = den[:KEEP, :128]

    def late_tile(num, den, total):
        tile = turn(den[64 : 64 + KEEP2, 128:], 6)
        tile = jnp.where(low_lane < EXT + 6, turn(den[:KEEP2, 128:], 4), tile)
        tile = jnp.where(low_lane < EXT + 4, turn(num[64 : 64 + KEEP2, 128:], 2), tile)
        tile = jnp.where(low_lane < EXT + 2, num[:KEEP2, 128:], tile)
        tile = jnp.where(low_lane < EXT, total[:KEEP2], tile)
        for i, v in enumerate((num, den)):
            for h in range(2):
                at = EDGE + 20 * i + 10 * h
                tile = jnp.where(low_lane >= at, turn(v[64 * h : 64 * h + KEEP2, :128], 4 + at), tile)
        return tile

    far_zero = [remote(level0.at[0, s], far0.at[s], far_send.at[s], far_recv.at[s], far, q) for s in range(SUBS)]
    rest = pl.ds(OWN, SUB - OWN)
    far_rest = remote(level0.at[0, 0, :, rest], far0.at[0, :, rest], far_send.at[0], far_recv.at[0], far, q)
    far_one = remote(level1.at[0], far1, far_send.at[SUBS], far_recv.at[SUBS], far, q)
    far_last = remote(late.at[0], far_late, far_send.at[SUBS + 1], far_recv.at[SUBS + 1], far, q)
    columns_in(0, (0, 1))
    put(0, keep[0, 0])
    put(1, keep[0, 1])
    columns_in(0, (2, 3))
    put(2, keep[0, 2])
    put(3, keep[0, 3])

    def far_chunk(s):
        num, den = sums_zero(0, s)
        level0[0, s, 0] = num
        level0[0, s, 1] = den

    for s in range(1, SUBS - 1):
        far_chunk(s)
        pl.when(core == 1)(far_zero[s].start)
    far_chunk(0)
    pl.when(core == 1)(far_rest.start)
    pl.when(jnp.logical_not(ahead))(meet)
    columns_in(1, (0, 1))
    columns_in(1, (2, 3))
    packs = [jnp.zeros((MID // 3, 128), F32), jnp.zeros((MID // 3, 128), F32)]
    for b in range(2):
        for p in range(4):
            tile = keep[b, p, :, pl.ds(COLS + 128, 128)]
            for h in range(3):
                at = 40 * h + 20 * b + 5 * p
                here = (fold_lane >= at) & (fold_lane < at + 5)
                rows = tile[MID // 3 * h : MID // 3 * (h + 1)]
                packs[0] = jnp.where(here, turn(rows, at - TO_LEFT), packs[0])
                packs[1] = jnp.where(here, turn(rows, at - TO_RIGHT), packs[1])
    pack[0] = packs[0]
    pack[1] = packs[1]

    to_left = remote(pack.at[0], halo.at[1], halo_send.at[0], halo_recv.at[1], me, left)
    to_right = remote(pack.at[1], halo.at[0], halo_send.at[1], halo_recv.at[0], me, right)

    def send_halo():
        @pl.when(me != GATE)
        def _():
            pl.semaphore_wait(beside_sem, 1)

        @pl.when(has_left)
        def _():
            to_left.start()

        @pl.when(has_right)
        def _():
            to_right.start()

    pl.when(jnp.logical_not(ahead))(send_halo)

    far_chunk(SUBS - 1)
    for copy in loads[2:5]:
        copy.wait()
    num, den, _ = sums_one(0)
    put_one(0, num, den)
    far_one.start()
    for s in range(SUBS - 1):
        pl.when(core == 0)(far_zero[s].start)

    pl.when(ahead)(meet)
    pl.when(ahead)(send_halo)

    pl.when(behind)(far_zero[SUBS - 1].start)
    for copy in loads[5:]:
        copy.wait()

    @pl.when(has_left)
    def _():
        to_right.wait_recv()

    @pl.when(has_right)
    def _():
        to_left.wait_recv()

    for b in range(2):
        edges = []
        for p in range(4):
            at = 20 * b + 5 * p
            from_left = jnp.concatenate([turn(halo[0], -at - 40 * h) for h in range(3)], 0)
            from_right = jnp.concatenate([turn(halo[1], 8 - at - 40 * h) for h in range(3)], 0)
            edge = jnp.where((lane >= 8) & (lane < 13), from_right, jnp.where(lane < 5, from_left, 0.0))
            edges.append(jnp.concatenate(split(edge), 1))
        added = dot(jnp.concatenate(edges, 0), twice(m_col_halo))
        for p in range(4):
            put(p, keep[b, p] + added[MID * p : MID * (p + 1)])

        num, den, total = sums_one(b)
        late[b, pl.ds(0, KEEP2)] = late_tile(num, den, total)
        if b == 1:
            put_one(b, num, den)

        patch = jnp.zeros((SUB // 2, 128), F32)
        for s in range(SUBS):
            num, den = sums_zero(b, s)
            if b == 1:
                level0[1, s, 0] = num
                level0[1, s, 1] = den
                continue
            for i, v in enumerate((num, den)):
                edges = jnp.where(sub_lane < 64, v[:, :128], v[:, 128:])
                for h in range(2):
                    at = 32 * s + 16 * h + 8 * i
                    moved = turn(edges[32 * h : 32 * h + 32], 4 + at)
                    patch = jnp.where((half_lane >= at) & (half_lane < at + 8), moved, patch)
        if b == 0:
            late[0, pl.ds(KEEP2, SUB // 2)] = patch
            far_last.start()
            pl.when(jnp.logical_not(behind))(far_zero[SUBS - 1].start)

    far_one.wait_recv()
    far_last.wait_recv()
    own_tile, far_tile = late[1, pl.ds(0, KEEP2)], far_late[pl.ds(0, KEEP2)]
    tile = own_tile + far_tile
    total = jnp.concatenate([jnp.where(low_lane < EXT, tile, 0.0), jnp.zeros((LOW - KEEP2, 128), F32)], 0)
    coarse = m_col_up[pl.ds(256, 128)]
    base = dot(jnp.concatenate(split(total), 1), jnp.concatenate([coarse, coarse], 0))
    at_edge = (keep_lane < 6) | (keep_lane >= 124)
    sums = []
    for i in range(2):
        at = EDGE + 20 * i
        edges = jnp.concatenate([turn(far_tile, -(4 + at))[:64], turn(far_tile, -(14 + at))], 0)
        sums.append(level1[1, i] + jnp.where(at_edge, edges, far1[i]))
    jbuf[pl.ds(0, KEEP), pl.ds(0, 128)] = sums[0] * inverse(sums[1])
    outer = (low_lane >= EXT) & (low_lane < EXT + 4)
    ratio = jnp.where(outer, tile, 0.0) * inverse(jnp.where(outer, turn(tile, -4), 1.0))
    ratio = jnp.concatenate([ratio[:64], turn(ratio, -2)], 0)
    ratio = jnp.where((keep_lane >= EXT) & (keep_lane < EXT + 2), ratio, 0.0)
    jbuf[pl.ds(0, KEEP), pl.ds(128, 128)] = ratio
    m = m_col_up[pl.ds(0, 256)]
    u = dot(jnp.concatenate(split(jbuf[...]), 1), jnp.concatenate([m, m], 0))
    upper[...] = dot(m_row_up[:, pl.ds(0, 2 * (MID + LOW))], jnp.concatenate([tall(u), tall(base)], 0))

    @pl.when(core == 1)
    def _():
        for i in range(2):
            remote(part, part_in.at[i], part_send.at[0], part_recv.at[i], first, q).wait_recv()
        far_rest.wait_recv()
        far0[0, :, pl.ds(0, OWN)] = part_in[0] + part_in[1]

    pl.when(core == 0)(far_zero[0].wait_recv)
    patch = far_late[pl.ds(KEEP2, SUB // 2)]
    for s in range(SUBS):
        if s:
            far_zero[s].wait_recv()
        sums = []
        for i in range(2):
            at = 32 * s + 8 * i
            edges = jnp.concatenate([turn(patch, -(4 + at)), turn(patch, -(20 + at))], 0)
            first = jnp.where(sub_lane < 4, edges, far0[s, i, :, pl.ds(0, 128)])
            second = jnp.where(sub_lane >= 124, edges, far0[s, i, :, pl.ds(128, 128)])
            sums.append(level0[1, s, i] + jnp.concatenate([first, second], 1))
        rows = pl.ds(SUB * s, SUB)
        out_ref[rows] = sums[0] * inverse(sums[1]) + upper[rows]

    @pl.when(has_left)
    def _():
        to_left.wait_send()

    @pl.when(has_right)
    def _():
        to_right.wait_send()

    pl.when(core == 0)(far_zero[0].wait_send)
    pl.when(core == 1)(far_rest.wait_send)
    for copy in swaps + far_zero[1:] + [far_one, far_last, far_part]:
        copy.wait_send()


def solution(mesh):
    count = mesh.shape["col"]
    consts = matrices()

    def body(x):
        dma = pltpu.SemaphoreType.DMA
        vmem = pltpu.VMEM
        return pl.pallas_call(
            functools.partial(kernel, count),
            out_shape=jax.ShapeDtypeStruct((BLOCK, COLS), F32),
            in_specs=[pl.BlockSpec(memory_space=pl.ANY)] * 2,
            out_specs=pl.BlockSpec(memory_space=pltpu.VMEM),
            scratch_shapes=[
                vmem((2, 4, 2, TOP + WIN + BOTTOM, 128), F32),
                vmem((2, 2, TOP + 128, 128), F32),
                vmem((2, LOW, 384), BF),
                vmem((BLOCK, 512), BF),
                vmem((SUB, 128), BF),
                vmem((MID, 256), BF),
                vmem((256, 512), BF),
                vmem((128, 512), BF),
                vmem((384, 256), BF),
                vmem((128, 256), BF),
                vmem((2, 4, MID, 512), F32),
                vmem((2, MID // 3, 128), F32),
                vmem((2, MID // 3, 128), F32),
                vmem((4, 2, MID, COLS), BF),
                vmem((4, MID, 128), F32),
                vmem((MID, 512), F32),
                vmem((2, OWN, COLS), F32),
                vmem((2, 2, OWN, COLS), F32),
                vmem((2, SUBS, 2, SUB, COLS), F32),
                vmem((2, 2, KEEP, 128), F32),
                vmem((2, LATE, 128), F32),
                vmem((SUBS, 2, SUB, COLS), F32),
                vmem((2, KEEP, 128), F32),
                vmem((LATE, 128), F32),
                vmem((MID, COLS), F32),
                vmem((BLOCK, COLS), F32),
                dma((9,)),
                dma((3, 2)),
                dma((1,)),
                dma((2,)),
                dma((2, 2)),
                dma((2, 2)),
                dma((2,)),
                dma((2,)),
                dma((SUBS + 2,)),
                dma((SUBS + 2,)),
                pltpu.SemaphoreType.REGULAR,
                pltpu.SemaphoreType.REGULAR,
                pltpu.SemaphoreType.REGULAR,
                pltpu.SemaphoreType.REGULAR,
            ],
            compiler_params=pltpu.CompilerParams(
                collective_id=0, has_side_effects=True, vmem_limit_bytes=VMEM_BYTES
            ),
        )(x, consts)

    return jax.shard_map(body, mesh=mesh, in_specs=(P("plane", None, "col"),), out_specs=P("plane", "col"), check_vma=False)
```

```python
import functools

import jax
import jax.numpy as jnp
import ml_dtypes
import numpy as np
from jax import lax
from jax.experimental import pallas as pl
from jax.experimental.pallas import tpu as pltpu
from jax.sharding import PartitionSpec as P

TAPS = np.array([1.0, 4.0, 6.0, 4.0, 1.0]) / 16.0
MESH = pl.DeviceIdType.MESH
BF = jnp.bfloat16
F32 = jnp.float32

ROWS = 1024
BLOCK = 256
COLS = 256
WIN = 288
MID = 144
LOW = 80
KEEP = 136
KEEP2 = 72
SUB = 64
SUBS = BLOCK // SUB
EXT = 67
WIDE = 512
ROW_PART = LOW + BLOCK
COL_PART = 2 * 256 + 128
REST = 4 * ROW_PART + 3 * COL_PART
LATE = KEEP2 + SUB // 2
EDGE = 76
VMEM_BYTES = 52 * 1024 * 1024
TO_RIGHT = 72
TO_LEFT = 80
PART = 48
OWN = 32
TOP = 16
BOTTOM = 32
P_SIZE = 8
GATE = 1
EXPO = float(-4.0 * np.log2(np.e))


def reduce_matrix(n):
    m = np.zeros((n // 2, n))
    for i in range(n // 2):
        for t in range(5):
            j = 2 * i - 2 + t
            if 0 <= j < n:
                m[i, j] = TAPS[t]
    return m


def expand_matrix(n):
    m = np.zeros((2 * n, n))
    for j in range(2 * n):
        for i in range(max(0, j // 2 - 2), min(n, j // 2 + 3)):
            t = j - 2 * i + 2
            if 0 <= t <= 4:
                m[j, i] = 2.0 * TAPS[t]
    return m


def window(m, row, rows, col, cols):
    out = np.zeros((rows, cols))
    r0, r1 = max(row, 0), min(row + rows, m.shape[0])
    c0, c1 = max(col, 0), min(col + cols, m.shape[1])
    out[r0 - row : r1 - row, c0 - col : c1 - col] = m[r0:r1, c0:c1]
    return out


def exact(m):
    cast = m.astype(ml_dtypes.bfloat16)
    assert (cast.astype(np.float64) == m).all()
    return cast


@functools.lru_cache(None)
def matrices():
    r1 = reduce_matrix(ROWS // 2)
    e0 = expand_matrix(ROWS // 2)
    row_low, row_up = [], []
    for p in range(4):
        m = window(r1, 64 * p - 2, LOW, 128 * p - 4, MID)
        row_low.append(np.concatenate([m, m], 1))
        m = window(e0, BLOCK * p, BLOCK, 128 * p - 4, MID)
        row_up.append(np.concatenate([m, m], 1))
    m = window(e0, SUB, SUB, 28, 48)
    row_sub = np.concatenate([m, m], 1)
    m = window(expand_matrix(ROWS // 4), 124, MID, 62, LOW)
    row_base = np.concatenate([m, m], 1)
    row_both = [up[:, :MID] @ m for up in row_up]
    row_up = [np.concatenate([up, np.concatenate([v, v], 1)], 1) for up, v in zip(row_up, row_both)]
    n = 3 * COLS
    c0, c1 = reduce_matrix(n), reduce_matrix(n // 2)
    x0 = expand_matrix(n // 2)
    col_in, col_up = [], []
    for b in range(3):
        full = np.concatenate(
            [
                (x0 @ c0)[COLS * b : COLS * (b + 1)],
                c0[128 * b : 128 * (b + 1)],
                window(c1 @ c0, 64 * b - 1, 67, 0, n),
                window(c0, 128 * b - 1, 1, 0, n),
                window(c0, 128 * (b + 1), 1, 0, n),
                np.zeros((3, n)),
                window(c0, 128 * (b + 1) - 1, 2, 0, n),
                window(c1 @ c0, 64 * (b + 1) - 1, 2, 0, n),
                np.zeros((4, n)),
                window(c0, 128 * b - 1, 2, 0, n),
                window(c1 @ c0, 64 * b - 1, 3, 0, n),
                np.zeros((43, n)),
            ],
            0,
        ).T
        col_in.append(full[COLS * b : COLS * (b + 1)])
        up = x0[COLS * b : COLS * (b + 1)].T
        both = np.zeros((256, COLS))
        both[:128] = up[128 * b : 128 * (b + 1)]
        both[128 + EXT] = window(up, 128 * b - 1, 1, 0, COLS)[0]
        both[128 + EXT + 1] = window(up, 128 * (b + 1), 1, 0, COLS)[0]
        col_up.append(both)
    col_halo = np.zeros((128, 512))
    for lane, i in ((0, -1), (1, 0), (8, 127), (9, 128)):
        col_halo[lane, :COLS] = x0[COLS : 2 * COLS, 128 + i]
        if 0 <= i < 128:
            col_halo[lane, COLS + i] = 1.0
        else:
            col_halo[lane, COLS + 128 + EXT + (i > 0)] = 1.0
    col_halo[1, COLS + 128 + 2] = TAPS[0]
    for lane, i in ((2, -1), (3, 0), (10, 63), (11, 64), (12, 65)):
        col_halo[lane, COLS + 128 + 1 + i] = 1.0
    col_base = np.zeros((128, 256))
    base = expand_matrix(n // 4)
    col_base[:67, :128] = window(base, 128, 128, 63, 67).T
    col_base[:67, 128 + EXT] = window(base, 127, 1, 63, 67)[0]
    col_base[:67, 128 + EXT + 1] = window(base, 256, 1, 63, 67)[0]
    col_up = [np.concatenate([up, col_base @ up / P_SIZE], 0) for up in col_up]
    parts = []
    for p in range(4):
        parts += [row_low[p], row_up[p]]
    for b in range(3):
        parts += [col_in[b], col_up[b]]
    parts += [col_base, row_base, row_sub, col_halo]
    return np.concatenate([exact(np.pad(m, ((0, 0), (0, WIDE - m.shape[1])))) for m in parts], 0)


def split(v):
    hi = v.astype(BF)
    lo = (v - hi.astype(F32)).astype(BF)
    return hi, lo


def dot(a, b):
    return jnp.dot(a, b, preferred_element_type=F32)


def tall(v):
    return jnp.concatenate(split(v), 0)


def inverse(v):
    r = pl.reciprocal(v, approx=True)
    return r * (2.0 - v * r)


def weight(d):
    return jnp.exp2(EXPO * inverse(1.0 + d * d))


def kernel(
    count,
    x_ref, const_ref,
    out_ref,
    xwin, xpart, m_row_low, m_row_up, m_row_sub, m_row_base, m_col_in, m_col_halo, m_col_up, m_col_base,
    keep, pack, halo, wide, c1, low, part, part_in,
    level0, level1, late, far0, far1, far_late, jbuf, upper,
    m_sem, x_sem, part_send, part_recv, swap_send, swap_recv, halo_send, halo_recv, far_send, far_recv, group_sem, sibling_sem, far_sem, beside_sem,
):
    me = lax.axis_index("plane")
    q = lax.axis_index("col")
    chip, core = me // 2, me % 2
    far = 2 * (1 - chip) + core
    sibling = 2 * chip + 1 - core
    far_sibling = 2 * (1 - chip) + 1 - core
    side = (q + count - 2) // (count - 1) + q // (count - 1)
    left, right = (q + count - 1) % count, (q + 1) % count
    has_left, has_right = q > 0, q < count - 1
    blocks = (far, me)
    first = 2 * (1 - chip) + 1

    barrier = pltpu.get_barrier_semaphore()

    def tell(sem, plane, col):
        pl.semaphore_signal(sem, inc=1, device_id=(plane, col), device_id_type=MESH)

    @pl.when(me == GATE)
    def _():
        for plane in (0, 2, 3):
            tell(barrier, plane, q)

    @pl.when((me == 0) | (me == 3))
    def _():
        tell(barrier, 2, q)

    def start_of(p):
        return pl.multiple_of(BLOCK * p - 16 + 16 * ((3 - p) // 3) - 16 * (p // 3), 16)

    def offset_of(p):
        return pl.multiple_of(16 - 16 * ((3 - p) // 3) + 16 * (p // 3), 16)

    def half(ref, h):
        return ref.at[:, :, pl.ds(128 * h, 128)]

    own = []
    for b in range(2):
        for h in range(2):
            own.append(
                pltpu.make_async_copy(
                    half(x_ref.at[:, pl.ds(start_of(blocks[b]), WIN)], h),
                    xwin.at[b, pl.ds(0, 2), h, pl.ds(TOP, WIN)],
                    x_sem.at[b, h],
                )
            )

    def const(at, rows, cols):
        return const_ref.at[pl.ds(pl.multiple_of(at, 16), rows), pl.ds(0, cols)]

    col_at = 4 * ROW_PART + COL_PART * side
    loads = [
        (const(col_at, 256, 512), m_col_in),
        (const(REST + 128 + MID, SUB, 128), m_row_sub),
        (const(ROW_PART * far, LOW, 384), m_row_low.at[0]),
        (const(REST, 128, 256), m_col_base),
        (const(REST + 128, MID, 256), m_row_base),
        (const(REST + 128 + MID + SUB, 128, 512), m_col_halo),
        (const(ROW_PART * me, LOW, 384), m_row_low.at[1]),
        (const(col_at + 256, 256 + 128, 256), m_col_up),
        (const(ROW_PART * me + LOW, BLOCK, 512), m_row_up),
    ]
    loads = [pltpu.make_async_copy(s, d, m_sem.at[i]) for i, (s, d) in enumerate(loads)]
    early = [
        pltpu.make_async_copy(
            half(x_ref.at[:, pl.ds(start_of(first), 128)], h), xpart.at[:, h, pl.ds(TOP, 128)], x_sem.at[2, h]
        )
        for h in range(2)
    ]
    early[0].start()
    early[1].start()
    loads[0].start()
    loads[1].start()
    own[0].start()
    own[1].start()

    def twice(ref):
        m = ref[...]
        return jnp.concatenate([m, m], 0)

    @pl.when((me == 0) | (me == 3))
    def _():
        pl.semaphore_wait(barrier, 1)

    @pl.when(me == 2)
    def _():
        pl.semaphore_wait(barrier, 3)
        tell(sibling_sem, 3, q)
        tell(far_sem, 0, q)
        tell(group_sem, GATE, q)

    @pl.when(me == 0)
    def _():
        tell(sibling_sem, GATE, q)

    @pl.when(me == 3)
    def _():
        tell(far_sem, GATE, q)

    def remote(src, dst, send, recv, plane, col):
        return pltpu.make_async_remote_copy(
            src_ref=src, dst_ref=dst, send_sem=send, recv_sem=recv, device_id=(plane, col), device_id_type=MESH
        )

    swaps = []
    for b, p in enumerate((far_sibling, sibling)):
        for h in range(2):
            swaps.append(
                remote(
                    half(x_ref.at[:, pl.ds(start_of(p), WIN)], h),
                    xwin.at[b, pl.ds(2, 2), h, pl.ds(TOP, WIN)],
                    swap_send.at[b, h],
                    swap_recv.at[b, h],
                    sibling,
                    q,
                )
            )

    @pl.when(core == 1)
    def _():
        pl.semaphore_wait(sibling_sem, 1)

    swaps[0].start()
    swaps[1].start()

    for b in range(2):
        for p in range(4):
            xwin[b, p, :, pl.ds(0, TOP)] = jnp.zeros((2, TOP, 128), F32)
            xwin[b, p, :, pl.ds(TOP + WIN, BOTTOM)] = jnp.zeros((2, BOTTOM, 128), F32)
    own[2].start()
    own[3].start()
    for copy in loads[2:]:
        copy.start()
    jbuf[pl.ds(KEEP, MID - KEEP)] = jnp.zeros((MID - KEEP, COLS), F32)

    @pl.when(q == 0)
    def _():
        halo[0] = jnp.zeros((MID // 3, 128), F32)

    @pl.when(q == count - 1)
    def _():
        halo[1] = jnp.zeros((MID // 3, 128), F32)

    def joined(ref, at, rows):
        return jnp.concatenate([ref[at + (0, rows)], ref[at + (1, rows)]], 1)

    def rows_down(ref, at, block, rows):
        base = offset_of(block) + TOP - 10
        taps = [joined(ref, at, pl.ds(base + t, rows, stride=2)) for t in range(5)]
        value = (taps[0] + taps[4]) * TAPS[0] + (taps[1] + taps[3]) * TAPS[1] + taps[2] * TAPS[2]
        row = lax.broadcasted_iota(jnp.int32, (rows, COLS), 0)
        inside = (row >= 4 * ((3 - block) // 3)) & (row < MID - 12 * (block // 3))
        return jnp.where(inside, value, 0.0)

    for p in range(2):
        xpart[p, :, pl.ds(0, TOP)] = jnp.zeros((2, TOP, 128), F32)

    early[0].wait()
    early[1].wait()
    loads[0].wait()
    loads[1].wait()
    num = jnp.zeros((OWN, COLS), F32)
    den = jnp.zeros((OWN, COLS), F32)
    for p in range(2):
        value = rows_down(xpart, (p,), first, PART)
        m = m_col_in[:, pl.ds(0, COLS)]
        value = dot(jnp.concatenate(split(value), 0), m)
        value = value[:PART] + value[PART:]
        z = dot(m_row_sub[pl.ds(0, OWN), pl.ds(0, 2 * PART)], tall(value))
        d = joined(xpart, (p,), pl.ds(pl.multiple_of(TOP + offset_of(first), 16), OWN)) - z
        w = weight(d)
        num = num + w * d
        den = den + w
    part[0] = num
    part[1] = den

    far_part = remote(part, part_in.at[core], part_send.at[0], part_recv.at[core], first, q)

    @pl.when(chip == 0)
    def _():
        pl.semaphore_wait(far_sem, 1)

    far_part.start()
    swaps[2].start()
    swaps[3].start()

    @pl.when(me == GATE)
    def _():
        pl.semaphore_wait(group_sem, 1)

        @pl.when(has_left)
        def _():
            tell(barrier, GATE, left)

        @pl.when(has_right)
        def _():
            tell(barrier, GATE, right)

    lane = lax.broadcasted_iota(jnp.int32, (MID, 128), 1)
    fold_lane = lax.broadcasted_iota(jnp.int32, (MID // 3, 128), 1)
    half_lane = lax.broadcasted_iota(jnp.int32, (SUB // 2, 128), 1)
    sub_lane = lax.broadcasted_iota(jnp.int32, (SUB, 128), 1)
    low_lane = lax.broadcasted_iota(jnp.int32, (KEEP2, 128), 1)
    keep_lane = lax.broadcasted_iota(jnp.int32, (KEEP, 128), 1)

    def turn(v, by):
        by = by % 128
        return pltpu.roll(v, by, 1) if by else v

    ahead = (q % 8 == 0) & has_left
    behind = (q % (count // 2) == 0) & has_left

    def meet():
        @pl.when(me == GATE)
        def _():
            pl.semaphore_wait(barrier, (q + count - 1) // count + (2 * count - 2 - q) // count)
            for plane in (0, 2, 3):
                tell(beside_sem, plane, q)

    def rows_in(b, p):
        if p == 0:
            own[2 * b].wait()
            own[2 * b + 1].wait()
        if p == 2:
            swaps[2 * b].wait_recv()
            swaps[2 * b + 1].wait_recv()
        return rows_down(xwin, (b, p), blocks[b], MID)

    def columns_in(b, planes):
        halves = []
        for p in planes:
            halves += split(rows_in(b, p))
        value = dot(jnp.concatenate(halves, 0), m_col_in[...])
        for i, p in enumerate(planes):
            keep[b, p] = value[2 * MID * i : 2 * MID * i + MID] + value[2 * MID * i + MID : 2 * MID * (i + 1)]

    def put(p, value):
        whi, wlo = split(value[:, :COLS])
        wide[p, 0] = whi
        wide[p, 1] = wlo
        c1[p] = value[:, COLS : COLS + 128]
        low[:, pl.ds(128 * p, 128)] = value[:, COLS + 128 :]

    def sums_zero(b, s):
        num = jnp.zeros((SUB, COLS), F32)
        den = jnp.zeros((SUB, COLS), F32)
        for p in range(4):
            rows = pl.ds(32 * s, 48)
            both = jnp.concatenate([wide[p, 0, rows], wide[p, 1, rows]], 0)
            z = dot(m_row_sub[:, pl.ds(0, 96)], both)
            d = joined(xwin, (b, p), pl.ds(pl.multiple_of(TOP + offset_of(blocks[b]) + SUB * s, 16), SUB)) - z
            w = weight(d)
            num = num + w * d
            den = den + w
        return num, den

    def columns_up(c2):
        return dot(jnp.concatenate(split(c2), 1), twice(m_col_base))

    def sums_one(b):
        c2 = dot(m_row_low[b, :, pl.ds(0, 2 * MID)], tall(low[...]))
        parts = [c2[:, 128 * p : 128 * p + 128] for p in range(4)]
        u = columns_up(jnp.concatenate(parts, 0))
        u = jnp.concatenate([u[LOW * p : LOW * p + LOW] for p in range(4)], 1)
        base = dot(m_row_base[:, pl.ds(0, 2 * LOW)], tall(u))
        num = jnp.zeros((MID, COLS), F32)
        den = jnp.zeros((MID, COLS), F32)
        for p in range(4):
            d = jnp.concatenate([c1[p], low[:, pl.ds(128 * p, 128)]], 1) - base[:, COLS * p : COLS * p + COLS]
            w = weight(d)
            num = num + w * d
            den = den + w
        return num, den, parts[0] + parts[1] + parts[2] + parts[3]

    def put_one(b, num, den):
        level1[b, 0] = num[:KEEP, :128]
        level1[b, 1] = den[:KEEP, :128]

    def late_tile(num, den, total):
        tile = turn(den[64 : 64 + KEEP2, 128:], 6)
        tile = jnp.where(low_lane < EXT + 6, turn(den[:KEEP2, 128:], 4), tile)
        tile = jnp.where(low_lane < EXT + 4, turn(num[64 : 64 + KEEP2, 128:], 2), tile)
        tile = jnp.where(low_lane < EXT + 2, num[:KEEP2, 128:], tile)
        tile = jnp.where(low_lane < EXT, total[:KEEP2], tile)
        for i, v in enumerate((num, den)):
            for h in range(2):
                at = EDGE + 20 * i + 10 * h
                tile = jnp.where(low_lane >= at, turn(v[64 * h : 64 * h + KEEP2, :128], 4 + at), tile)
        return tile

    far_zero = [remote(level0.at[0, s], far0.at[s], far_send.at[s], far_recv.at[s], far, q) for s in range(SUBS - 1)]
    far_ends = []
    for i in range(2):
        rows = pl.ds(SUB // 2 * i, SUB // 2)
        src, dst, at = level0.at[0, SUBS - 1, :, rows], far0.at[SUBS - 1, :, rows], SUBS + 2 * i
        far_ends.append(remote(src, dst, far_send.at[at], far_recv.at[at], far, q))
    rest = pl.ds(OWN, SUB - OWN)
    far_rest = remote(level0.at[0, 0, :, rest], far0.at[0, :, rest], far_send.at[0], far_recv.at[0], far, q)
    far_one = remote(level1.at[0], far1, far_send.at[SUBS - 1], far_recv.at[SUBS - 1], far, q)
    far_last = remote(late.at[0], far_late, far_send.at[SUBS + 1], far_recv.at[SUBS + 1], far, q)
    columns_in(0, (0, 1))
    put(0, keep[0, 0])
    put(1, keep[0, 1])
    columns_in(1, (0, 1))
    columns_in(0, (2, 3))
    put(2, keep[0, 2])
    put(3, keep[0, 3])

    def far_chunk(s):
        num, den = sums_zero(0, s)
        level0[0, s, 0] = num
        level0[0, s, 1] = den

    for s in range(1, SUBS - 1):
        far_chunk(s)
        pl.when(core == 1)(far_zero[s].start)
    far_chunk(0)
    pl.when(core == 1)(far_rest.start)
    pl.when(jnp.logical_not(ahead))(meet)
    columns_in(1, (2, 3))
    packs = [jnp.zeros((MID // 3, 128), F32), jnp.zeros((MID // 3, 128), F32)]
    for b in range(2):
        for p in range(4):
            tile = keep[b, p, :, pl.ds(COLS + 128, 128)]
            for h in range(3):
                at = 40 * h + 20 * b + 5 * p
                here = (fold_lane >= at) & (fold_lane < at + 5)
                rows = tile[MID // 3 * h : MID // 3 * (h + 1)]
                packs[0] = jnp.where(here, turn(rows, at - TO_LEFT), packs[0])
                packs[1] = jnp.where(here, turn(rows, at - TO_RIGHT), packs[1])
    pack[0] = packs[0]
    pack[1] = packs[1]

    to_left = remote(pack.at[0], halo.at[1], halo_send.at[0], halo_recv.at[1], me, left)
    to_right = remote(pack.at[1], halo.at[0], halo_send.at[1], halo_recv.at[0], me, right)

    def send_halo():
        @pl.when(me != GATE)
        def _():
            pl.semaphore_wait(beside_sem, 1)

        @pl.when(has_left)
        def _():
            to_left.start()

        @pl.when(has_right)
        def _():
            to_right.start()

    pl.when(jnp.logical_not(ahead))(send_halo)

    far_chunk(SUBS - 1)
    pl.when(behind)(far_ends[0].start)
    for copy in loads[2:5]:
        copy.wait()
    num, den, _ = sums_one(0)
    put_one(0, num, den)
    far_one.start()
    for s in range(SUBS - 1):
        pl.when(core == 0)(far_zero[s].start)

    pl.when(ahead)(meet)
    pl.when(ahead)(send_halo)

    for copy in loads[5:]:
        copy.wait()

    @pl.when(has_left)
    def _():
        to_right.wait_recv()

    @pl.when(has_right)
    def _():
        to_left.wait_recv()

    for b in range(2):
        edges = []
        for p in range(4):
            at = 20 * b + 5 * p
            from_left = jnp.concatenate([turn(halo[0], -at - 40 * h) for h in range(3)], 0)
            from_right = jnp.concatenate([turn(halo[1], 8 - at - 40 * h) for h in range(3)], 0)
            edge = jnp.where((lane >= 8) & (lane < 13), from_right, jnp.where(lane < 5, from_left, 0.0))
            edges.append(jnp.concatenate(split(edge), 1))
        added = dot(jnp.concatenate(edges, 0), twice(m_col_halo))
        for p in range(4):
            put(p, keep[b, p] + added[MID * p : MID * (p + 1)])

        num, den, total = sums_one(b)
        late[b, pl.ds(0, KEEP2)] = late_tile(num, den, total)
        if b == 1:
            put_one(b, num, den)

        patch = jnp.zeros((SUB // 2, 128), F32)
        for s in range(SUBS):
            num, den = sums_zero(b, s)
            if b == 1:
                level0[1, s, 0] = num
                level0[1, s, 1] = den
                continue
            for i, v in enumerate((num, den)):
                edges = jnp.where(sub_lane < 64, v[:, :128], v[:, 128:])
                for h in range(2):
                    at = 32 * s + 16 * h + 8 * i
                    moved = turn(edges[32 * h : 32 * h + 32], 4 + at)
                    patch = jnp.where((half_lane >= at) & (half_lane < at + 8), moved, patch)
        if b == 0:
            late[0, pl.ds(KEEP2, SUB // 2)] = patch
            far_last.start()
            pl.when(jnp.logical_not(behind))(far_ends[0].start)
            far_ends[1].start()

    far_one.wait_recv()
    far_last.wait_recv()
    own_tile, far_tile = late[1, pl.ds(0, KEEP2)], far_late[pl.ds(0, KEEP2)]
    tile = own_tile + far_tile
    total = jnp.concatenate([jnp.where(low_lane < EXT, tile, 0.0), jnp.zeros((LOW - KEEP2, 128), F32)], 0)
    coarse = m_col_up[pl.ds(256, 128)]
    base = dot(jnp.concatenate(split(total), 1), jnp.concatenate([coarse, coarse], 0))
    at_edge = (keep_lane < 6) | (keep_lane >= 124)
    sums = []
    for i in range(2):
        at = EDGE + 20 * i
        edges = jnp.concatenate([turn(far_tile, -(4 + at))[:64], turn(far_tile, -(14 + at))], 0)
        sums.append(level1[1, i] + jnp.where(at_edge, edges, far1[i]))
    jbuf[pl.ds(0, KEEP), pl.ds(0, 128)] = sums[0] * inverse(sums[1])
    outer = (low_lane >= EXT) & (low_lane < EXT + 4)
    ratio = jnp.where(outer, tile, 0.0) * inverse(jnp.where(outer, turn(tile, -4), 1.0))
    ratio = jnp.concatenate([ratio[:64], turn(ratio, -2)], 0)
    ratio = jnp.where((keep_lane >= EXT) & (keep_lane < EXT + 2), ratio, 0.0)
    jbuf[pl.ds(0, KEEP), pl.ds(128, 128)] = ratio
    m = m_col_up[pl.ds(0, 256)]
    u = dot(jnp.concatenate(split(jbuf[...]), 1), jnp.concatenate([m, m], 0))
    upper[...] = dot(m_row_up[:, pl.ds(0, 2 * (MID + LOW))], jnp.concatenate([tall(u), tall(base)], 0))

    @pl.when(core == 1)
    def _():
        for i in range(2):
            remote(part, part_in.at[i], part_send.at[0], part_recv.at[i], first, q).wait_recv()
        far_rest.wait_recv()
        far0[0, :, pl.ds(0, OWN)] = part_in[0] + part_in[1]

    pl.when(core == 0)(far_zero[0].wait_recv)
    patch = far_late[pl.ds(KEEP2, SUB // 2)]
    for s in range(SUBS):
        if s == SUBS - 1:
            far_ends[0].wait_recv()
            far_ends[1].wait_recv()
        elif s:
            far_zero[s].wait_recv()
        sums = []
        for i in range(2):
            at = 32 * s + 8 * i
            edges = jnp.concatenate([turn(patch, -(4 + at)), turn(patch, -(20 + at))], 0)
            first = jnp.where(sub_lane < 4, edges, far0[s, i, :, pl.ds(0, 128)])
            second = jnp.where(sub_lane >= 124, edges, far0[s, i, :, pl.ds(128, 128)])
            sums.append(level0[1, s, i] + jnp.concatenate([first, second], 1))
        rows = pl.ds(SUB * s, SUB)
        out_ref[rows] = sums[0] * inverse(sums[1]) + upper[rows]

    @pl.when(has_left)
    def _():
        to_left.wait_send()

    @pl.when(has_right)
    def _():
        to_right.wait_send()

    pl.when(core == 0)(far_zero[0].wait_send)
    pl.when(core == 1)(far_rest.wait_send)
    for copy in swaps + far_zero[1:] + far_ends + [far_one, far_last, far_part]:
        copy.wait_send()


def solution(mesh):
    count = mesh.shape["col"]
    consts = matrices()

    def body(x):
        dma = pltpu.SemaphoreType.DMA
        vmem = pltpu.VMEM
        return pl.pallas_call(
            functools.partial(kernel, count),
            out_shape=jax.ShapeDtypeStruct((BLOCK, COLS), F32),
            in_specs=[pl.BlockSpec(memory_space=pl.ANY)] * 2,
            out_specs=pl.BlockSpec(memory_space=pltpu.VMEM),
            scratch_shapes=[
                vmem((2, 4, 2, TOP + WIN + BOTTOM, 128), F32),
                vmem((2, 2, TOP + 128, 128), F32),
                vmem((2, LOW, 384), BF),
                vmem((BLOCK, 512), BF),
                vmem((SUB, 128), BF),
                vmem((MID, 256), BF),
                vmem((256, 512), BF),
                vmem((128, 512), BF),
                vmem((384, 256), BF),
                vmem((128, 256), BF),
                vmem((2, 4, MID, 512), F32),
                vmem((2, MID // 3, 128), F32),
                vmem((2, MID // 3, 128), F32),
                vmem((4, 2, MID, COLS), BF),
                vmem((4, MID, 128), F32),
                vmem((MID, 512), F32),
                vmem((2, OWN, COLS), F32),
                vmem((2, 2, OWN, COLS), F32),
                vmem((2, SUBS, 2, SUB, COLS), F32),
                vmem((2, 2, KEEP, 128), F32),
                vmem((2, LATE, 128), F32),
                vmem((SUBS, 2, SUB, COLS), F32),
                vmem((2, KEEP, 128), F32),
                vmem((LATE, 128), F32),
                vmem((MID, COLS), F32),
                vmem((BLOCK, COLS), F32),
                dma((9,)),
                dma((3, 2)),
                dma((1,)),
                dma((2,)),
                dma((2, 2)),
                dma((2, 2)),
                dma((2,)),
                dma((2,)),
                dma((SUBS + 3,)),
                dma((SUBS + 3,)),
                pltpu.SemaphoreType.REGULAR,
                pltpu.SemaphoreType.REGULAR,
                pltpu.SemaphoreType.REGULAR,
                pltpu.SemaphoreType.REGULAR,
            ],
            compiler_params=pltpu.CompilerParams(
                collective_id=0, has_side_effects=True, vmem_limit_bytes=VMEM_BYTES
            ),
        )(x, consts)

    return jax.shard_map(body, mesh=mesh, in_specs=(P("plane", None, "col"),), out_specs=P("plane", "col"), check_vma=False)
```
